32 devices in a mesh: groups: 2 (over x), inline: 16 (over z, y, core).
Axes of the slice: x: 2, y: 2, z: 4, core: 2. Of those that a mesh axis runs over, the one named last changes fastest.
Arguments:
- data: float32 [256, 8, 4096], P(('groups', 'inline')), parts along dimension 0, may hold values from -6 to 6
- trace_mask: int32 [256, 4096], P(('groups', 'inline')), parts along dimension 0, may hold values 0 or 1
- slope_inline: float32 [256, 8, 4096], P(('groups', 'inline')), parts along dimension 0, may hold values from -1 to 1
- slope_cross: float32 [256, 8, 4096], P(('groups', 'inline')), parts along dimension 0, may hold values from -1 to 1
- model: float32 [256, 8, 4096], P(('groups', 'inline')), parts along dimension 0, may hold values from -6 to 6
- direction: float32 [256, 8, 4096], P(('groups', 'inline')), parts along dimension 0, may hold values from -6 to 6
Outputs:
- model_out: float32 [256, 8, 4096], P(('groups', 'inline')), parts along dimension 0
- direction_out: float32 [256, 8, 4096], P(('groups', 'inline')), parts along dimension 0
The draws below stay inside these ranges and needn't reach their ends.
There are 2 independent parts, one for each index of `groups`. The reference program is written for one: setup_inputs(seed, part) draws one part's arguments, and reference() takes and returns one part's arrays. A program takes and returns all parts, laid end to end along the dimension named above; each array names one. Nothing has to cross between parts.
Inputs may be any that keep to these rules, and one draw needn't show every extreme that they name: `trace_mask`: 1 marks a recorded trace, 0 a missing one.
All inputs are finite; a program needn't handle non-finite values. No bound on the sum of `trace_mask` on one device may be relied on, other than what follows from the above.
Results may differ from the reference program's by a relative error of at most 0.0001.
Values sent between devices are 32-bit elements; how exact they have to be, the bound alone decides.
No kernel may reach another device: no remote copies, remote signals or barrier semaphores. Data moves between devices by JAX's collectives and lax.ppermute only.
A program may use at most 64 MiB of HBM per device.

```python
import jax
import jax.numpy as jnp
from jax import lax

XL = 4096
NT = 8
ITERS = 3
IL = 128


def touch_ends(result, key, least, high):
    place = [jax.random.randint(jax.random.fold_in(key, axis), (), 0, length) for axis, length in enumerate(result.shape)]
    main_axis = result.shape.index(max(result.shape))
    neighbour = place[:main_axis] + [(place[main_axis] + 1) % result.shape[main_axis]] + place[main_axis + 1:]
    return result.at[tuple(place)].set(least).at[tuple(neighbour)].set(high)


def levels(own_key, shape, cuts, smallest, largest):
    factor_of, own = 1.0, jax.random.fold_in(own_key, 6)
    for axis_at, blocks in cuts:
        draws = jnp.exp(jax.random.uniform(jax.random.fold_in(own, axis_at), (blocks,), jnp.float32, smallest / len(cuts), largest / len(cuts)))
        factor_of = factor_of * jnp.repeat(draws, shape[axis_at] // blocks).reshape([-1 if axis == axis_at else 1 for axis in range(len(shape))])
    return factor_of


def centred(own_key, shape, spread, most, shards=(), dtype=jnp.bfloat16):
    drawn = spread * jax.random.normal(own_key, shape, jnp.float32)
    if shards:
        drawn = drawn * levels(own_key, shape, shards, -0.22, 0.18)
    return jnp.clip(drawn, -most, most).astype(dtype)


def setup_inputs(seed: int = 0, part: int = 0) -> dict:
    key_of = jax.random.split(jax.random.key(seed), 7)
    part_splits = jax.random.split(jax.random.fold_in(key_of[6], part), 7)
    return {
        "data": centred(part_splits[0], (IL, NT, XL), 1.0, 6.0, ((0, 16),), jnp.float32),
        "trace_mask": touch_ends((jax.random.randint(part_splits[1], (IL, XL), 0, 3) < 2).astype(jnp.int32), jax.random.fold_in(part_splits[1], 1), 0, 1),
        "slope_inline": jnp.clip(jax.random.uniform(part_splits[2], (IL, NT, XL), jnp.float32, -1.0, 1.0) * levels(part_splits[2], (IL, NT, XL), ((0, 16),), -0.4, 0.0), -1.0, 1.0),
        "slope_cross": jnp.clip(jax.random.uniform(part_splits[3], (IL, NT, XL), jnp.float32, -1.0, 1.0) * levels(part_splits[3], (IL, NT, XL), ((0, 16),), -0.4, 0.0), -1.0, 1.0),
        "model": centred(part_splits[4], (IL, NT, XL), 1.0, 6.0, ((0, 16),), jnp.float32),
        "direction": centred(part_splits[5], (IL, NT, XL), 1.0, 6.0, ((0, 16),), jnp.float32),
    }


reg_weight = 1.0


def shift_ahead(values, along):
    length_along = values.shape[along]
    remaining = lax.slice_in_dim(values, 1, length_along, axis=along)
    return jnp.concatenate([remaining, jnp.zeros_like(lax.slice_in_dim(values, 0, 1, axis=along))], along)


def shift_behind(values, along):
    length_along = values.shape[along]
    remaining = lax.slice_in_dim(values, 0, length_along - 1, axis=along)
    return jnp.concatenate([jnp.zeros_like(lax.slice_in_dim(values, 0, 1, axis=along)), remaining], along)


def destruct(values, slopes, along):
    lower_coef = (1.0 - slopes) * 0.5
    upper_coef = (1.0 + slopes) * 0.5
    ahead_cells = shift_ahead(values, along)
    return lower_coef * (ahead_cells - shift_ahead(values, 1)) + upper_coef * (shift_ahead(ahead_cells, 1) - values)


def destruct_adjoint(residual, slopes, along):
    lower_part = ((1.0 - slopes) * 0.5) * residual
    upper_part = ((1.0 + slopes) * 0.5) * residual
    return shift_behind(lower_part, along) - shift_behind(lower_part, 1) + shift_behind(shift_behind(upper_part, along), 1) - upper_part


def inner_sum(left_terms, right_terms):
    total = jnp.sum(left_terms[0] * right_terms[0])
    total = total + jnp.sum(left_terms[1] * right_terms[1])
    return total + jnp.sum(left_terms[2] * right_terms[2])


def image_of(values, known_traces, slope_inline, slope_cross):
    return (known_traces * values, reg_weight * destruct(values, slope_inline, 0), reg_weight * destruct(values, slope_cross, 2))


def reference(data, trace_mask, slope_inline, slope_cross, model, direction):
    known_traces = trace_mask.astype(jnp.float32)[:, None, :]
    for iteration in range(ITERS):
        residual = (known_traces * (data - model), -reg_weight * destruct(model, slope_inline, 0), -reg_weight * destruct(model, slope_cross, 2))
        gradient = known_traces * residual[0] + reg_weight * (destruct_adjoint(residual[1], slope_inline, 0) + destruct_adjoint(residual[2], slope_cross, 2))
        grad_image = image_of(gradient, known_traces, slope_inline, slope_cross)
        dir_image = image_of(direction, known_traces, slope_inline, slope_cross)
        mixing = -inner_sum(grad_image, dir_image) / inner_sum(dir_image, dir_image)
        direction = gradient + mixing * direction
        conjugate = tuple(grad_term + mixing * dir_term for grad_term, dir_term in zip(grad_image, dir_image))
        step_size = inner_sum(residual, conjugate) / inner_sum(conjugate, conjugate)
        model = model + step_size * direction
    return model, direction
```

```python
import functools

import jax
import jax.numpy as jnp
from jax import lax
from jax.experimental import pallas as pl
from jax.experimental.pallas import tpu as pltpu
from jax.sharding import PartitionSpec as P

ITERS = 3
NT = 8
LANES = 128
CHUNK = 512
SHIFT = 18.0
M0, D0, SI0, SC0, G0, BG0, B2G0, BD0, B2D0 = range(9)
M1, D1, SI1, SC1, G1, BG1, BD1, SJ1 = range(8)
N_MOMENTS = 18
VMEM_LIMIT = 16 * 1024 * 1024

f32 = jnp.float32


def time_ahead(v):
    rolled = pltpu.roll(v, NT - 1, 0)
    return jnp.where(lax.broadcasted_iota(jnp.int32, v.shape, 0) == NT - 1, 0.0, rolled)


def time_behind(v):
    rolled = pltpu.roll(v, 1, 0)
    return jnp.where(lax.broadcasted_iota(jnp.int32, v.shape, 0) == 0, 0.0, rolled)


def sum_diff(v):
    ahead = time_ahead(v)
    return ahead + v, ahead - v


def head(pair, width):
    return pair[0][:, :width], pair[1][:, :width]


def inline_res(here, after, slope):
    return (after[0] - here[0]) + slope * (after[1] + here[1])


def parts(res, slope):
    scaled = slope * res
    return res - scaled, res + scaled


def to_next(ef):
    return ef[0] + time_behind(ef[1])


def to_self(ef):
    return -(ef[1] + time_behind(ef[0]))


def lane_ahead(v):
    width = v.shape[1]
    return pltpu.roll(v, width - 1, 1)[:, : width - LANES]


def lane_behind(before, v):
    joined = jnp.concatenate([before, v], axis=1)
    return pltpu.roll(joined, 1, 1)[:, LANES:]


def cross_res(sd, slope):
    width = sd[0].shape[1] - LANES
    here = head(sd, width)
    return (lane_ahead(sd[0]) - here[0]) + slope * (lane_ahead(sd[1]) + here[1])


def cross_terms(sd, slope, carry, slot):
    e, f = parts(cross_res(sd, slope), slope)
    e_behind = lane_behind(carry[slot, 0], e)
    f_behind = lane_behind(carry[slot, 1], f)
    carry[slot, 0] = e[:, -LANES:]
    carry[slot, 1] = f[:, -LANES:]
    return e_behind - f, f_behind - e


def stencil(load, slope_in, slope_cr, lo, hi, res_lo, res_hi, carry, slot, scale_lo=None):
    out = {}
    sd = {}

    def pair(i):
        if i not in sd:
            sd[i] = sum_diff(load(i))
        return sd[i]

    before = None
    for i in range(lo - 1, hi + 1):
        here = None
        if res_lo <= i <= res_hi:
            first = pair(i)
            second = pair(i + 1)
            width = first[0].shape[1] - LANES
            slope = slope_in(i)
            res = inline_res(head(first, width), head(second, width), slope)
            if i == -1 and scale_lo is not None:
                res = res * scale_lo
            here = parts(res, slope)
        if i >= lo:
            same, later = cross_terms(pair(i), slope_cr(i), carry, slot + i - lo)
            if before is not None:
                same = same + before[0]
                later = later + before[1]
            if here is not None:
                same = same - here[1]
                later = later - here[0]
            out[i] = same + time_behind(later)
        before = here
    return out


class Mended:
    def __init__(self, n, depth, whole, ends):
        self.n, self.depth, self.whole, self.ends = n, depth, whole, ends

    def at(self, i):
        if i < self.depth:
            return self.ends, i + 1
        if i >= self.n - self.depth:
            return self.ends, i - self.n + 2 * self.depth + 1
        return self.whole, i + 1

    def load(self, i, lanes):
        ref, row = self.at(i)
        return ref[row, :, lanes]

    def store(self, i, lanes, value):
        ref, row = self.at(i)
        ref[row, :, lanes] = value


def mended(n, whole, ends):
    return [Mended(n, depth, w, e) for depth, w, e in zip((1, 2, 3, 1, 2), whole, ends)]


def chunks(x):
    return x // CHUNK


def at_chunk(c):
    return pl.multiple_of(c * CHUNK, CHUNK)


def edge_kernel(
    n, x,
    data_hbm, mask_hbm, si_hbm, sc_hbm, model_hbm, dir_hbm, up_ref, down_ref,
    data_ref, mask_ref, si_ref, sc_ref, m_ref, d_ref, g_ref, bg_ref, bd_ref, carry, sems,
):
    lanes = pl.ds(0, x)
    copies = [pltpu.make_async_copy(mask_hbm, mask_ref, sems.at[0])]
    for ref, dst in ((model_hbm, m_ref), (si_hbm, si_ref), (sc_hbm, sc_ref), (data_hbm, data_ref), (dir_hbm, d_ref)):
        for rows in (pl.ds(0, 4), pl.ds(n - 3, 3)):
            to = dst.at[rows] if dst.shape[2] == x else dst.at[rows, :, lanes]
            copies.append(pltpu.make_async_copy(ref.at[rows], to, sems.at[len(copies)]))
    for copy in copies:
        copy.start()
    for ref in (m_ref, d_ref, g_ref, bg_ref, bd_ref):
        ref[:, :, pl.ds(x, LANES)] = jnp.zeros((n, NT, LANES), f32)
    carry[...] = jnp.zeros(carry.shape, f32)
    share = x // NT
    for copy in copies:
        copy.wait()
    for s in range(NT):
        up_ref[pl.ds(s, 1), pl.ds(9 * x, share)] = mask_ref[pl.ds(0, 1), pl.ds(s * share, share)].astype(f32)
        down_ref[pl.ds(s, 1), pl.ds(8 * x, share)] = mask_ref[pl.ds(n - 1, 1), pl.ds(s * share, share)].astype(f32)

    def known4(i, x0):
        return mask_ref[pl.ds(i, 1), pl.ds(x0, CHUNK)].astype(f32) * 4.0

    def level(x0, src, lo, hi, slot):
        return stencil(
            lambda i: src[i, :, pl.ds(x0, CHUNK + LANES)],
            lambda i: si_ref[i, :, pl.ds(x0, CHUNK)],
            lambda i: sc_ref[i, :, pl.ds(x0, CHUNK)],
            lo, hi, 0, n - 2, carry, slot,
        )

    def applied(x0, src, lo, hi, slot):
        out = level(x0, src, lo, hi, slot)
        return {i: (known4(i, x0) - SHIFT) * src[i, :, pl.ds(x0, CHUNK)] + out[i] for i in out}

    def send_up(slot, x0, value):
        up_ref[:, pl.ds(pl.multiple_of(x0 + slot * x, CHUNK), CHUNK)] = value

    def send_down(slot, x0, value):
        down_ref[:, pl.ds(pl.multiple_of(x0 + slot * x, CHUNK), CHUNK)] = value

    def first(c, _):
        x0 = at_chunk(c)
        here = pl.ds(x0, CHUNK)
        out = level(x0, m_ref, 0, 2, 0)
        out.update(level(x0, m_ref, n - 2, n - 1, 3))
        for i, value in out.items():
            out[i] = known4(i, x0) * (data_ref[i, :, here] - m_ref[i, :, here]) - value
            g_ref[i, :, here] = out[i]
        send_up(G0, x0, out[0])
        send_down(G1, x0, out[n - 1])
        out = applied(x0, d_ref, 0, 1, 5)
        for i in (0, 1):
            bd_ref[i, :, here] = out[i]
        send_up(BD0, x0, out[0])
        out = applied(x0, d_ref, n - 1, n - 1, 7)
        send_down(BD1, x0, out[n - 1])
        for slot, row in ((M0, m_ref), (D0, d_ref), (SI0, si_ref), (SC0, sc_ref)):
            send_up(slot, x0, row[0, :, here])
        for slot, row in ((M1, m_ref), (D1, d_ref), (SI1, si_ref), (SC1, sc_ref)):
            send_down(slot, x0, row[n - 1, :, here])
        send_down(SJ1, x0, si_ref[n - 2, :, here])
        return 0

    lax.fori_loop(0, chunks(x), first, 0)
    carry[...] = jnp.zeros(carry.shape, f32)

    def second(c, _):
        x0 = at_chunk(c)
        here = pl.ds(x0, CHUNK)
        out = applied(x0, g_ref, 0, 1, 0)
        for i in (0, 1):
            bg_ref[i, :, here] = out[i]
        send_up(BG0, x0, out[0])
        send_down(BG1, x0, applied(x0, g_ref, n - 1, n - 1, 2)[n - 1])
        send_up(B2D0, x0, applied(x0, bd_ref, 0, 0, 3)[0])
        return 0

    lax.fori_loop(0, chunks(x), second, 0)
    carry[...] = jnp.zeros(carry.shape, f32)

    def third(c, _):
        x0 = at_chunk(c)
        send_up(B2G0, x0, applied(x0, bg_ref, 0, 0, 0)[0])
        return 0

    lax.fori_loop(0, chunks(x), third, 0)


def local_kernel(
    n, x,
    data_hbm, mask_hbm, si_hbm, sc_hbm, model_hbm, dir_hbm,
    m_ref, d_ref, si_ref, sc_ref, mask_ref, g_ref, bg_ref, b2g_ref, bd_ref, b2d_ref, sums_ref,
    data_ref, carry, sems,
):
    body = (pl.ds(1, n), slice(None), pl.ds(0, x))
    copies = [
        pltpu.make_async_copy(model_hbm, m_ref.at[body], sems.at[0]),
        pltpu.make_async_copy(si_hbm, si_ref.at[pl.ds(1, n)], sems.at[1]),
        pltpu.make_async_copy(sc_hbm, sc_ref, sems.at[2]),
        pltpu.make_async_copy(data_hbm, data_ref, sems.at[3]),
        pltpu.make_async_copy(mask_hbm, mask_ref, sems.at[4]),
        pltpu.make_async_copy(dir_hbm, d_ref.at[body], sems.at[5]),
    ]
    for copy in copies:
        copy.start()
    pad = jnp.zeros((n + 2, NT, LANES), f32)
    for ref in (m_ref, d_ref, g_ref, bg_ref, b2g_ref, bd_ref, b2d_ref):
        ref[:, :, pl.ds(x, LANES)] = pad
    carry[...] = jnp.zeros(carry.shape, f32)
    sums_ref[...] = jnp.zeros(sums_ref.shape, f32)
    for copy in copies:
        copy.wait()

    def known4(i, x0):
        return mask_ref[pl.ds(i, 1), pl.ds(x0, CHUNK)].astype(f32) * 4.0

    def level(x0, src, lo, hi, slot):
        return stencil(
            lambda i: src[i + 1, :, pl.ds(x0, CHUNK + LANES)],
            lambda i: si_ref[i + 1, :, pl.ds(x0, CHUNK)],
            lambda i: sc_ref[i, :, pl.ds(x0, CHUNK)],
            lo, hi, 0, n - 2, carry, slot,
        )

    def apply(x0, src, dst, lo, hi, slot):
        here = pl.ds(x0, CHUNK)
        out = level(x0, src, lo, hi, slot)
        for i in range(lo, hi + 1):
            dst[i + 1, :, here] = (known4(i, x0) - SHIFT) * src[i + 1, :, here] + out[i]

    def first(c, _):
        x0 = at_chunk(c)
        here = pl.ds(x0, CHUNK)
        out = level(x0, m_ref, 0, n - 1, 0)
        for i in range(n):
            g_ref[i + 1, :, here] = known4(i, x0) * (data_ref[i, :, here] - m_ref[i + 1, :, here]) - out[i]
        apply(x0, d_ref, bd_ref, 0, n - 1, n)
        return 0

    lax.fori_loop(0, chunks(x), first, 0)
    carry[...] = jnp.zeros(carry.shape, f32)

    def second(c, _):
        x0 = at_chunk(c)
        apply(x0, g_ref, bg_ref, 2, n - 3, 0)
        apply(x0, bd_ref, b2d_ref, 2, n - 3, n)
        return 0

    lax.fori_loop(0, chunks(x), second, 0)
    carry[...] = jnp.zeros(carry.shape, f32)

    def third(c, _):
        apply(at_chunk(c), bg_ref, b2g_ref, 3, n - 4, 0)
        return 0

    lax.fori_loop(0, chunks(x), third, 0)

    def fourth(c, _):
        x0 = at_chunk(c)
        products(
            x0, range(3, n - 3), range(3, n - 4),
            [lambda i, lanes, ref=ref: ref[i + 1, :, lanes] for ref in (g_ref, bg_ref, b2g_ref, d_ref, bd_ref, b2d_ref)],
            known4, si_ref, sc_ref, sums_ref,
        )
        return 0

    lax.fori_loop(0, chunks(x), fourth, 0)


PAIRS = ((0, 0), (0, 1), (1, 1), (1, 2), (2, 2), None, (0, 3), (0, 4), (1, 4), (1, 5), (2, 5), None,
         (3, 3), (3, 4), (4, 4), (4, 5), (5, 5), None)


def products(x0, rows, inline_rows, loads, known4, si_ref, sc_ref, sums):
    here = pl.ds(x0, CHUNK)
    wide = pl.ds(x0, CHUNK + LANES)
    totals = [None] * N_MOMENTS

    def add(k, product):
        acc = product[:, :LANES]
        for j in range(1, CHUNK // LANES):
            acc = acc + product[:, j * LANES:(j + 1) * LANES]
        totals[k] = acc if totals[k] is None else totals[k] + acc

    def add_pairs(u, v):
        add(5, u * u)
        add(11, u * v)
        add(17, v * v)

    sums_of = {}

    def pair(which, i):
        if (which, i) not in sums_of:
            sums_of[which, i] = sum_diff(loads[which](i, wide))
        return sums_of[which, i]

    for i in sorted(set(rows) | set(inline_rows)):
        if i in inline_rows:
            slope = si_ref[i + 1, :, here]
            add_pairs(*(inline_res(head(pair(k, i), CHUNK), head(pair(k, i + 1), CHUNK), slope) for k in (2, 5)))
        if i in rows:
            cross = sc_ref[i, :, here]
            add_pairs(*(cross_res(pair(k, i), cross) for k in (2, 5)))
            values = [load(i, here) for load in loads]
            for k, which in enumerate(PAIRS):
                if which is not None:
                    add(k, values[which[0]] * values[which[1]])
            known = known4(i, x0)
            kept_g = known * values[2]
            add(5, kept_g * values[2])
            add(11, kept_g * values[5])
            add(17, known * values[5] * values[5])
    for k in range(N_MOMENTS):
        sums[k] = sums[k] + totals[k]


def join_kernel(
    n, x,
    m_ref, d_ref, si_ref, sc_ref, mask_ref, g_in, bg_in, b2g_in, bd_in, b2d_in, sums_in, up_ref, down_ref,
    g_out, bg_out, b2g_out, bd_out, b2d_out, moments_ref,
    eps_ref, eta_ref, epsb_ref, mask_up, mask_down, carry, sums,
):
    place = lax.axis_index("inline")
    not_first = (place > 0).astype(f32)
    not_last = (place < lax.axis_size("inline") - 1).astype(f32)
    share = x // NT
    pad = jnp.zeros((NT, LANES), f32)
    for i in range(3):
        eps_ref[i, :, pl.ds(x, LANES)] = pad
    eta_ref[:, pl.ds(x, LANES)] = pad
    for ref in (g_out, bg_out, b2g_out, bd_out, b2d_out):
        for i in range(ref.shape[0]):
            ref[i, :, pl.ds(x, LANES)] = pad
    g_rows, bg_rows, b2g_rows, bd_rows, b2d_rows = mended(
        n, (g_in, bg_in, b2g_in, bd_in, b2d_in), (g_out, bg_out, b2g_out, bd_out, b2d_out))
    epsb_ref[:, pl.ds(x, LANES)] = pad
    carry[...] = jnp.zeros(carry.shape, f32)
    sums[...] = sums_in[...]
    for s in range(NT):
        mask_up[:, pl.ds(s * share, share)] = up_ref[pl.ds(s, 1), pl.ds(9 * x, share)] * 4.0 - SHIFT
        mask_down[:, pl.ds(s * share, share)] = down_ref[pl.ds(s, 1), pl.ds(8 * x, share)] * 4.0 - SHIFT

    def from_up(slot, x0):
        return up_ref[:, pl.ds(pl.multiple_of(x0 + slot * x, CHUNK), CHUNK)]

    def from_down(slot, x0):
        return down_ref[:, pl.ds(pl.multiple_of(x0 + slot * x, CHUNK), CHUNK)]

    def known4(i, x0):
        return mask_ref[pl.ds(i, 1), pl.ds(x0, CHUNK)].astype(f32) * 4.0

    def zeroth(c, _):
        x0 = at_chunk(c)
        here = pl.ds(x0, CHUNK)
        slope = si_ref[n, :, here]

        ef = parts(inline_res(sum_diff(m_ref[n, :, here]), sum_diff(from_up(M0, x0)), slope), slope)
        eps = -to_next(ef)
        eps_ref[0, :, here] = eps
        g_rows.store(n, here, (from_up(G0, x0) + eps) * not_last)
        g_rows.store(n - 1, here, g_in[n, :, here] - to_self(ef))
        ef = parts(inline_res(sum_diff(d_ref[n, :, here]), sum_diff(from_up(D0, x0)), slope), slope)
        eta = to_next(ef)
        eta_ref[:, here] = eta
        bd_rows.store(n, here, (from_up(BD0, x0) + eta) * not_last)
        bd_rows.store(n - 1, here, bd_in[n, :, here] + to_self(ef))

        slope = from_down(SI1, x0)
        res = inline_res(sum_diff(from_down(M1, x0)), sum_diff(m_ref[1, :, here]), slope) * not_first
        ef = parts(res, slope)
        eps = -to_self(ef)
        epsb_ref[:, here] = eps
        g_rows.store(-1, here, from_down(G1, x0) + eps)
        g_rows.store(0, here, g_in[1, :, here] - to_next(ef))
        res = inline_res(sum_diff(from_down(D1, x0)), sum_diff(d_ref[1, :, here]), slope) * not_first
        ef = parts(res, slope)
        bd_rows.store(-1, here, from_down(BD1, x0) + to_self(ef))
        bd_rows.store(0, here, bd_in[1, :, here] + to_next(ef))
        return 0

    lax.fori_loop(0, chunks(x), zeroth, 0)

    def slope_in(x0):
        def get(i):
            if i == -1:
                return from_down(SI1, x0)
            return si_ref[i + 1, :, pl.ds(x0, CHUNK)]
        return get

    def edges(x0, src, dst, depth, slot):
        here = pl.ds(x0, CHUNK)
        for lo, hi in ((0, depth), (n - 1 - depth, n - 1)):
            out = stencil(
                lambda i: src.load(i, pl.ds(x0, CHUNK + LANES)),
                slope_in(x0),
                lambda i: sc_ref[i, :, here],
                lo, hi, -1, n - 1, carry, slot, not_first,
            )
            for i in range(lo, hi + 1):
                dst.store(i, here, (known4(i, x0) - SHIFT) * src.load(i, here) + out[i])
            slot += hi - lo + 1
        return slot

    def boundary(src, row, slope, here, scale=None):
        res = inline_res(sum_diff(src.load(row, here)), sum_diff(src.load(row + 1, here)), slope)
        if scale is not None:
            res = res * scale
        return parts(res, slope)

    def first(c, _):
        x0 = at_chunk(c)
        here = pl.ds(x0, CHUNK)
        wide = pl.ds(x0, CHUNK + LANES)
        slot = edges(x0, g_rows, bg_rows, 1, 0)
        slot = edges(x0, bd_rows, b2d_rows, 1, slot)
        slope = si_ref[n, :, here]
        slope_up = from_up(SI0, x0)
        cross_up = from_up(SC0, x0)
        sd = sum_diff(eps_ref[0, :, wide])
        near = head(sd, CHUNK)
        ef8 = parts(slope_up * near[1] - near[0], slope_up)
        same, later = cross_terms(sd, cross_up, carry, slot)
        own = mask_up[:, here] * eps_ref[0, :, here] + (same - ef8[1]) + time_behind(later - ef8[0])
        eps = own + to_next(boundary(g_rows, n - 1, slope, here))
        eps_ref[1, :, here] = eps
        eps_ref[2, :, here] = to_next(ef8)
        bg_rows.store(n, here, (from_up(BG0, x0) + eps) * not_last)
        sd = sum_diff(eta_ref[:, wide])
        near = head(sd, CHUNK)
        ef8 = parts(slope_up * near[1] - near[0], slope_up)
        same, later = cross_terms(sd, cross_up, carry, slot + 1)
        own = mask_up[:, here] * eta_ref[:, here] + (same - ef8[1]) + time_behind(later - ef8[0])
        b2d_rows.store(n, here, (from_up(B2D0, x0) + own + to_next(boundary(bd_rows, n - 1, slope, here))) * not_last)
        slope_low = from_down(SJ1, x0)
        sd = sum_diff(epsb_ref[:, wide])
        near = head(sd, CHUNK)
        ef2 = parts(near[0] + slope_low * near[1], slope_low)
        same, later = cross_terms(sd, from_down(SC1, x0), carry, slot + 2)
        own = mask_down[:, here] * epsb_ref[:, here] + (same + ef2[0]) + time_behind(later + ef2[1])
        bg_rows.store(-1, here, (
            from_down(BG1, x0) + own + to_self(boundary(g_rows, -1, from_down(SI1, x0), here, not_first))
        ))
        return 0

    lax.fori_loop(0, chunks(x), first, 0)
    carry[...] = jnp.zeros(carry.shape, f32)

    def second(c, _):
        x0 = at_chunk(c)
        here = pl.ds(x0, CHUNK)
        wide = pl.ds(x0, CHUNK + LANES)
        slot = edges(x0, bg_rows, b2g_rows, 2, 0)
        slope_up = from_up(SI0, x0)
        sd = sum_diff(eps_ref[1, :, wide])
        near = head(sd, CHUNK)
        ef8 = parts(inline_res(near, sum_diff(eps_ref[2, :, here]), slope_up), slope_up)
        same, later = cross_terms(sd, from_up(SC0, x0), carry, slot)
        own = mask_up[:, here] * eps_ref[1, :, here] + (same - ef8[1]) + time_behind(later - ef8[0])
        b2g_rows.store(n, here, (
            from_up(B2G0, x0) + own + to_next(boundary(bg_rows, n - 1, si_ref[n, :, here], here))
        ) * not_last)
        return 0

    lax.fori_loop(0, chunks(x), second, 0)

    done = range(3, n - 3)
    done_inline = range(3, n - 4)
    loads = [rows.load for rows in (g_rows, bg_rows, b2g_rows)]
    loads += [lambda i, lanes: d_ref[i + 1, :, lanes], bd_rows.load, b2d_rows.load]

    def third(c, _):
        products(
            at_chunk(c), [i for i in range(n) if i not in done], [i for i in range(n) if i not in done_inline],
            loads, known4, si_ref, sc_ref, sums,
        )
        return 0

    lax.fori_loop(0, chunks(x), third, 0)
    for k in range(N_MOMENTS):
        moments_ref[pl.ds(k, 1), :] = jnp.sum(sums[k], axis=0, keepdims=True)
    moments_ref[pl.ds(N_MOMENTS, 24 - N_MOMENTS), :] = jnp.zeros((24 - N_MOMENTS, LANES), f32)


def add_terms(terms):
    total = None
    for term in terms:
        total = term if total is None else total + term
    return total


def solve(moments):
    mu, nu, xi = moments[:6], moments[6:12], moments[12:]

    def entry(a, b, i, j):
        if a == 0 and b == 0:
            return mu[i + j]
        if a == 1 and b == 1:
            return xi[i + j]
        return nu[i + j]

    shifted = {}

    def entry_a(a, b, i, j):
        which = a + b
        if (which, i + j) not in shifted:
            if i + j == 4:
                value = entry(a, b, 2, 3)
            else:
                value = entry(a, b, i, j + 1) + SHIFT * entry(a, b, i, j)
            shifted[which, i + j] = value * 0.25
        return shifted[which, i + j]

    def form(get, u, v):
        rows = []
        for (a, i), left in u.items():
            inner = add_terms(right * get(a, b, i, j) for (b, j), right in v.items())
            rows.append(left * inner)
        return add_terms(rows)

    def axpy(scale, u, v):
        out = dict(v)
        for key, value in u.items():
            term = scale * value
            out[key] = out[key] + term if key in out else term
        return out

    one = jnp.ones_like(mu[0])
    gradient = {(0, 0): 0.25 * one}
    direction = {(1, 0): one}
    model = {}
    for iteration in range(ITERS):
        mixing = -form(entry_a, gradient, direction) / form(entry_a, direction, direction)
        direction = axpy(mixing, direction, gradient)
        step = form(entry, gradient, direction) / form(entry_a, direction, direction)
        model = axpy(step, direction, model)
        if iteration < ITERS - 1:
            image = {key: value * (0.25 * SHIFT) for key, value in direction.items()}
            image = axpy(0.25, {(a, i + 1): value for (a, i), value in direction.items()}, image)
            gradient = axpy(-step, image, gradient)
    return model, direction


def last_kernel(
    n, x, moments_ref, m_ref, d_ref, g_in, bg_in, b2g_in, bd_in, b2d_in, g_end, bg_end, b2g_end, bd_end, b2d_end,
    model_hbm, dir_hbm, mo_ref, do_ref, sems,
):
    moments = [
        jnp.broadcast_to(jnp.sum(moments_ref[pl.ds(k, 1), :], axis=1, keepdims=True), (NT, LANES))
        for k in range(N_MOMENTS)
    ]
    model, direction = solve(moments)
    rows = mended(n, (g_in, bg_in, b2g_in, bd_in, b2d_in), (g_end, bg_end, b2g_end, bd_end, b2d_end))
    keys = ((0, 0), (0, 1), (0, 2), (1, 1), (1, 2))
    copies = []
    for i in range(n):
        def step(c, _):
            x0 = pl.multiple_of(c * LANES, LANES)
            here = pl.ds(x0, LANES)
            values = {key: vector.load(i, here) for key, vector in zip(keys, rows)}
            values[1, 0] = d_ref[i + 1, :, here]
            mo_ref[i, :, here] = m_ref[i + 1, :, here] + add_terms(
                model[key] * value for key, value in values.items())
            do_ref[i, :, here] = add_terms(direction[key] * value for key, value in values.items())
            return 0

        lax.fori_loop(0, x // LANES, step, 0, unroll=4)
        for k, (src, dst) in enumerate(((mo_ref, model_hbm), (do_ref, dir_hbm))):
            copy = pltpu.make_async_copy(src.at[i], dst.at[i], sems.at[2 * i + k])
            copy.start()
            copies.append(copy)
    for copy in copies:
        copy.wait()


def in_vmem(values):
    return [pltpu.with_memory_space_constraint(v, pltpu.VMEM) for v in values]


def kept(shape, dtype=f32):
    return pltpu.VMEM(shape, dtype)


def on_device(*args):
    n, _, x = args[0].shape
    peers = lax.axis_size("inline")
    vmem = pl.BlockSpec(memory_space=pltpu.VMEM)
    hbm = pl.BlockSpec(memory_space=pl.ANY)
    params = pltpu.CompilerParams(vmem_limit_bytes=VMEM_LIMIT)
    wide = kept((n + 2, NT, x + LANES))
    share = x // NT

    args = [pltpu.with_memory_space_constraint(v, pltpu.HBM) for v in args]
    up, down = pl.pallas_call(
        functools.partial(edge_kernel, n, x),
        out_shape=[kept((NT, 9 * x + share)), kept((NT, 8 * x + share))],
        in_specs=[hbm] * 6,
        out_specs=[vmem] * 2,
        scratch_shapes=[
            pltpu.VMEM((n, NT, x), f32),
            pltpu.VMEM((n, x), jnp.int32),
            pltpu.VMEM((n, NT, x), f32),
            pltpu.VMEM((n, NT, x), f32),
        ] + [pltpu.VMEM((n, NT, x + LANES), f32)] * 5 + [
            pltpu.VMEM((8, 2, NT, LANES), f32),
            pltpu.SemaphoreType.DMA((11,)),
        ],
        compiler_params=params,
        name="edges",
    )(*args)
    up = lax.ppermute(up, "inline", [(i, i - 1) for i in range(1, peers)])
    down = lax.ppermute(down, "inline", [(i, i + 1) for i in range(peers - 1)])

    local = pl.pallas_call(
        functools.partial(local_kernel, n, x),
        out_shape=[
            wide, wide, kept((n + 2, NT, x)), kept((n, NT, x)), kept((n, x), jnp.int32),
            wide, wide, wide, wide, wide, kept((N_MOMENTS, NT, LANES)),
        ],
        in_specs=[hbm] * 6,
        out_specs=[vmem] * 11,
        scratch_shapes=[
            pltpu.VMEM((n, NT, x), f32),
            pltpu.VMEM((2 * n, 2, NT, LANES), f32),
            pltpu.SemaphoreType.DMA((6,)),
        ],
        compiler_params=params,
        name="local",
    )(*args)
    m, d, _, _, _, g, bg, b2g, bd, b2d, _ = local

    out = pl.pallas_call(
        functools.partial(join_kernel, n, x),
        out_shape=[kept((2 * depth + 2, NT, x + LANES)) for depth in (1, 2, 3, 1, 2)]
        + [jax.ShapeDtypeStruct((24, LANES), f32)],
        in_specs=[vmem] * 13,
        out_specs=[vmem] * 6,
        scratch_shapes=[
            pltpu.VMEM((3, NT, x + LANES), f32),
            pltpu.VMEM((NT, x + LANES), f32),
            pltpu.VMEM((NT, x + LANES), f32),
            pltpu.VMEM((1, x), f32),
            pltpu.VMEM((1, x), f32),
            pltpu.VMEM((12, 2, NT, LANES), f32),
            pltpu.VMEM((N_MOMENTS, NT, LANES), f32),
        ],
        compiler_params=params,
        name="join",
    )(*in_vmem(local), up, down)
    *ends_out, moments = out

    reach = 1
    while reach < peers:
        moments = moments + lax.ppermute(moments, "inline", [(i, i ^ reach) for i in range(peers)])
        reach *= 2

    return pl.pallas_call(
        functools.partial(last_kernel, n, x),
        out_shape=[jax.ShapeDtypeStruct((n, NT, x), f32)] * 2,
        in_specs=[vmem] * 13,
        out_specs=[hbm] * 2,
        scratch_shapes=[
            pltpu.VMEM((n, NT, x), f32),
            pltpu.VMEM((n, NT, x), f32),
            pltpu.SemaphoreType.DMA((2 * n,)),
        ],
        compiler_params=params,
        name="last",
    )(moments, *in_vmem([m, d, g, bg, b2g, bd, b2d, *ends_out]))


def solution(mesh):
    rows = P(("groups", "inline"), None, None)
    return jax.shard_map(
        on_device,
        mesh=mesh,
        in_specs=(rows, P(("groups", "inline"), None), rows, rows, rows, rows),
        out_specs=(rows, rows),
        check_vma=False,
    )
```

```python
import functools

import jax
import jax.numpy as jnp
from jax import lax
from jax.experimental import pallas as pl
from jax.experimental.pallas import tpu as pltpu
from jax.sharding import PartitionSpec as P

ITERS = 3
NT = 8
LANES = 128
CHUNK = 4096
SHIFT = 18.0
M0, D0, SI0, SC0, G0, BG0, B2G0, BD0, B2D0 = range(9)
M1, D1, SI1, SC1, G1, BG1, BD1, SJ1 = range(8)
N_MOMENTS = 18
VMEM_LIMIT = 16 * 1024 * 1024

f32 = jnp.float32


def time_ahead(v):
    rolled = pltpu.roll(v, NT - 1, 0)
    return jnp.where(lax.broadcasted_iota(jnp.int32, v.shape, 0) == NT - 1, 0.0, rolled)


def time_behind(v):
    rolled = pltpu.roll(v, 1, 0)
    return jnp.where(lax.broadcasted_iota(jnp.int32, v.shape, 0) == 0, 0.0, rolled)


def sum_diff(v):
    ahead = time_ahead(v)
    return ahead + v, ahead - v


def head(pair, width):
    return pair[0][:, :width], pair[1][:, :width]


def inline_res(here, after, slope):
    return (after[0] - here[0]) + slope * (after[1] + here[1])


def parts(res, slope):
    scaled = slope * res
    return res - scaled, res + scaled


def to_next(ef):
    return ef[0] + time_behind(ef[1])


def to_self(ef):
    return -(ef[1] + time_behind(ef[0]))


def lane_ahead(v):
    width = v.shape[1]
    return pltpu.roll(v, width - 1, 1)[:, : width - LANES]


def lane_behind(before, v):
    joined = jnp.concatenate([before, v], axis=1)
    return pltpu.roll(joined, 1, 1)[:, LANES:]


def cross_res(sd, slope):
    width = sd[0].shape[1] - LANES
    here = head(sd, width)
    return (lane_ahead(sd[0]) - here[0]) + slope * (lane_ahead(sd[1]) + here[1])


def cross_terms(sd, slope, carry, slot):
    e, f = parts(cross_res(sd, slope), slope)
    e_behind = lane_behind(carry[slot, 0], e)
    f_behind = lane_behind(carry[slot, 1], f)
    carry[slot, 0] = e[:, -LANES:]
    carry[slot, 1] = f[:, -LANES:]
    return e_behind - f, f_behind - e


def stencil(load, slope_in, slope_cr, lo, hi, res_lo, res_hi, carry, slot, scale_lo=None):
    out = {}
    sd = {}

    def pair(i):
        if i not in sd:
            sd[i] = sum_diff(load(i))
        return sd[i]

    before = None
    for i in range(lo - 1, hi + 1):
        here = None
        if res_lo <= i <= res_hi:
            first = pair(i)
            second = pair(i + 1)
            width = first[0].shape[1] - LANES
            slope = slope_in(i)
            res = inline_res(head(first, width), head(second, width), slope)
            if i == -1 and scale_lo is not None:
                res = res * scale_lo
            here = parts(res, slope)
        if i >= lo:
            same, later = cross_terms(pair(i), slope_cr(i), carry, slot + i - lo)
            if before is not None:
                same = same + before[0]
                later = later + before[1]
            if here is not None:
                same = same - here[1]
                later = later - here[0]
            out[i] = same + time_behind(later)
        before = here
    return out


class Mended:
    def __init__(self, n, depth, whole, ends):
        self.n, self.depth, self.whole, self.ends = n, depth, whole, ends

    def at(self, i):
        if i < self.depth:
            return self.ends, i + 1
        if i >= self.n - self.depth:
            return self.ends, i - self.n + 2 * self.depth + 1
        return self.whole, i + 1

    def load(self, i, lanes):
        ref, row = self.at(i)
        return ref[row, :, lanes]

    def store(self, i, lanes, value):
        ref, row = self.at(i)
        ref[row, :, lanes] = value


def mended(n, whole, ends):
    return [Mended(n, depth, w, e) for depth, w, e in zip((1, 2, 3, 1, 2), whole, ends)]


def chunks(x):
    return x // CHUNK


def at_chunk(c):
    return pl.multiple_of(c * CHUNK, CHUNK)


def edge_kernel(
    n, x,
    data_hbm, mask_hbm, si_hbm, sc_hbm, model_hbm, dir_hbm, up_ref, down_ref,
    data_ref, mask_ref, si_ref, sc_ref, m_ref, d_ref, g_ref, bg_ref, bd_ref, carry, sems,
):
    lanes = pl.ds(0, x)
    copies = [pltpu.make_async_copy(mask_hbm, mask_ref, sems.at[0])]
    for ref, dst in ((model_hbm, m_ref), (si_hbm, si_ref), (sc_hbm, sc_ref), (data_hbm, data_ref), (dir_hbm, d_ref)):
        for rows in (pl.ds(0, 4), pl.ds(n - 3, 3)):
            to = dst.at[rows] if dst.shape[2] == x else dst.at[rows, :, lanes]
            copies.append(pltpu.make_async_copy(ref.at[rows], to, sems.at[len(copies)]))
    for copy in copies:
        copy.start()
    for ref in (m_ref, d_ref, g_ref, bg_ref, bd_ref):
        ref[:, :, pl.ds(x, LANES)] = jnp.zeros((n, NT, LANES), f32)
    carry[...] = jnp.zeros(carry.shape, f32)
    share = x // NT
    for copy in copies:
        copy.wait()
    for s in range(NT):
        up_ref[pl.ds(s, 1), pl.ds(9 * x, share)] = mask_ref[pl.ds(0, 1), pl.ds(s * share, share)].astype(f32)
        down_ref[pl.ds(s, 1), pl.ds(8 * x, share)] = mask_ref[pl.ds(n - 1, 1), pl.ds(s * share, share)].astype(f32)

    def known4(i, x0):
        return mask_ref[pl.ds(i, 1), pl.ds(x0, CHUNK)].astype(f32) * 4.0

    def level(x0, src, lo, hi, slot):
        return stencil(
            lambda i: src[i, :, pl.ds(x0, CHUNK + LANES)],
            lambda i: si_ref[i, :, pl.ds(x0, CHUNK)],
            lambda i: sc_ref[i, :, pl.ds(x0, CHUNK)],
            lo, hi, 0, n - 2, carry, slot,
        )

    def applied(x0, src, lo, hi, slot):
        out = level(x0, src, lo, hi, slot)
        return {i: (known4(i, x0) - SHIFT) * src[i, :, pl.ds(x0, CHUNK)] + out[i] for i in out}

    def send_up(slot, x0, value):
        up_ref[:, pl.ds(pl.multiple_of(x0 + slot * x, CHUNK), CHUNK)] = value

    def send_down(slot, x0, value):
        down_ref[:, pl.ds(pl.multiple_of(x0 + slot * x, CHUNK), CHUNK)] = value

    def first(c, _):
        x0 = at_chunk(c)
        here = pl.ds(x0, CHUNK)
        out = level(x0, m_ref, 0, 2, 0)
        out.update(level(x0, m_ref, n - 2, n - 1, 3))
        for i, value in out.items():
            out[i] = known4(i, x0) * (data_ref[i, :, here] - m_ref[i, :, here]) - value
            g_ref[i, :, here] = out[i]
        send_up(G0, x0, out[0])
        send_down(G1, x0, out[n - 1])
        out = applied(x0, d_ref, 0, 1, 5)
        for i in (0, 1):
            bd_ref[i, :, here] = out[i]
        send_up(BD0, x0, out[0])
        out = applied(x0, d_ref, n - 1, n - 1, 7)
        send_down(BD1, x0, out[n - 1])
        for slot, row in ((M0, m_ref), (D0, d_ref), (SI0, si_ref), (SC0, sc_ref)):
            send_up(slot, x0, row[0, :, here])
        for slot, row in ((M1, m_ref), (D1, d_ref), (SI1, si_ref), (SC1, sc_ref)):
            send_down(slot, x0, row[n - 1, :, here])
        send_down(SJ1, x0, si_ref[n - 2, :, here])
        return 0

    lax.fori_loop(0, chunks(x), first, 0)
    carry[...] = jnp.zeros(carry.shape, f32)

    def second(c, _):
        x0 = at_chunk(c)
        here = pl.ds(x0, CHUNK)
        out = applied(x0, g_ref, 0, 1, 0)
        for i in (0, 1):
            bg_ref[i, :, here] = out[i]
        send_up(BG0, x0, out[0])
        send_down(BG1, x0, applied(x0, g_ref, n - 1, n - 1, 2)[n - 1])
        send_up(B2D0, x0, applied(x0, bd_ref, 0, 0, 3)[0])
        return 0

    lax.fori_loop(0, chunks(x), second, 0)
    carry[...] = jnp.zeros(carry.shape, f32)

    def third(c, _):
        x0 = at_chunk(c)
        send_up(B2G0, x0, applied(x0, bg_ref, 0, 0, 0)[0])
        return 0

    lax.fori_loop(0, chunks(x), third, 0)


def local_kernel(
    n, x,
    data_hbm, mask_hbm, si_hbm, sc_hbm, model_hbm, dir_hbm,
    m_ref, d_ref, si_ref, sc_ref, mask_ref, g_ref, bg_ref, b2g_ref, bd_ref, b2d_ref, sums_ref,
    data_ref, carry, sems,
):
    body = (pl.ds(1, n), slice(None), pl.ds(0, x))
    copies = [
        pltpu.make_async_copy(model_hbm, m_ref.at[body], sems.at[0]),
        pltpu.make_async_copy(si_hbm, si_ref.at[pl.ds(1, n)], sems.at[1]),
        pltpu.make_async_copy(sc_hbm, sc_ref, sems.at[2]),
        pltpu.make_async_copy(data_hbm, data_ref, sems.at[3]),
        pltpu.make_async_copy(mask_hbm, mask_ref, sems.at[4]),
        pltpu.make_async_copy(dir_hbm, d_ref.at[body], sems.at[5]),
    ]
    for copy in copies:
        copy.start()
    pad = jnp.zeros((n + 2, NT, LANES), f32)
    for ref in (m_ref, d_ref, g_ref, bg_ref, b2g_ref, bd_ref, b2d_ref):
        ref[:, :, pl.ds(x, LANES)] = pad
    carry[...] = jnp.zeros(carry.shape, f32)
    sums_ref[...] = jnp.zeros(sums_ref.shape, f32)
    for copy in copies:
        copy.wait()

    def known4(i, x0):
        return mask_ref[pl.ds(i, 1), pl.ds(x0, CHUNK)].astype(f32) * 4.0

    def level(x0, src, lo, hi, slot):
        return stencil(
            lambda i: src[i + 1, :, pl.ds(x0, CHUNK + LANES)],
            lambda i: si_ref[i + 1, :, pl.ds(x0, CHUNK)],
            lambda i: sc_ref[i, :, pl.ds(x0, CHUNK)],
            lo, hi, 0, n - 2, carry, slot,
        )

    def apply(x0, src, dst, lo, hi, slot):
        here = pl.ds(x0, CHUNK)
        out = level(x0, src, lo, hi, slot)
        for i in range(lo, hi + 1):
            dst[i + 1, :, here] = (known4(i, x0) - SHIFT) * src[i + 1, :, here] + out[i]

    def first(c, _):
        x0 = at_chunk(c)
        here = pl.ds(x0, CHUNK)
        out = level(x0, m_ref, 0, n - 1, 0)
        for i in range(n):
            g_ref[i + 1, :, here] = known4(i, x0) * (data_ref[i, :, here] - m_ref[i + 1, :, here]) - out[i]
        apply(x0, d_ref, bd_ref, 0, n - 1, n)
        return 0

    lax.fori_loop(0, chunks(x), first, 0)
    carry[...] = jnp.zeros(carry.shape, f32)

    def second(c, _):
        x0 = at_chunk(c)
        apply(x0, g_ref, bg_ref, 2, n - 3, 0)
        apply(x0, bd_ref, b2d_ref, 2, n - 3, n)
        return 0

    lax.fori_loop(0, chunks(x), second, 0)
    carry[...] = jnp.zeros(carry.shape, f32)

    def third(c, _):
        apply(at_chunk(c), bg_ref, b2g_ref, 3, n - 4, 0)
        return 0

    lax.fori_loop(0, chunks(x), third, 0)

    def fourth(c, _):
        x0 = at_chunk(c)
        products(
            x0, range(3, n - 3), range(3, n - 4),
            [lambda i, lanes, ref=ref: ref[i + 1, :, lanes] for ref in (g_ref, bg_ref, b2g_ref, d_ref, bd_ref, b2d_ref)],
            known4, si_ref, sc_ref, sums_ref,
        )
        return 0

    lax.fori_loop(0, chunks(x), fourth, 0)


PAIRS = ((0, 0), (0, 1), (1, 1), (1, 2), (2, 2), None, (0, 3), (0, 4), (1, 4), (1, 5), (2, 5), None,
         (3, 3), (3, 4), (4, 4), (4, 5), (5, 5), None)


def products(x0, rows, inline_rows, loads, known4, si_ref, sc_ref, sums):
    here = pl.ds(x0, CHUNK)
    wide = pl.ds(x0, CHUNK + LANES)
    totals = [None] * N_MOMENTS

    def add(k, product):
        acc = product[:, :LANES]
        for j in range(1, CHUNK // LANES):
            acc = acc + product[:, j * LANES:(j + 1) * LANES]
        totals[k] = acc if totals[k] is None else totals[k] + acc

    def add_pairs(u, v):
        add(5, u * u)
        add(11, u * v)
        add(17, v * v)

    sums_of = {}

    def pair(which, i):
        if (which, i) not in sums_of:
            sums_of[which, i] = sum_diff(loads[which](i, wide))
        return sums_of[which, i]

    for i in sorted(set(rows) | set(inline_rows)):
        if i in inline_rows:
            slope = si_ref[i + 1, :, here]
            add_pairs(*(inline_res(head(pair(k, i), CHUNK), head(pair(k, i + 1), CHUNK), slope) for k in (2, 5)))
        if i in rows:
            cross = sc_ref[i, :, here]
            add_pairs(*(cross_res(pair(k, i), cross) for k in (2, 5)))
            values = [load(i, here) for load in loads]
            for k, which in enumerate(PAIRS):
                if which is not None:
                    add(k, values[which[0]] * values[which[1]])
            known = known4(i, x0)
            kept_g = known * values[2]
            add(5, kept_g * values[2])
            add(11, kept_g * values[5])
            add(17, known * values[5] * values[5])
    for k in range(N_MOMENTS):
        sums[k] = sums[k] + totals[k]


def join_kernel(
    n, x,
    m_ref, d_ref, si_ref, sc_ref, mask_ref, g_in, bg_in, b2g_in, bd_in, b2d_in, sums_in, up_ref, down_ref,
    g_out, bg_out, b2g_out, bd_out, b2d_out, moments_ref,
    eps_ref, eta_ref, epsb_ref, mask_up, mask_down, carry, sums,
):
    place = lax.axis_index("inline")
    not_first = (place > 0).astype(f32)
    not_last = (place < lax.axis_size("inline") - 1).astype(f32)
    share = x // NT
    pad = jnp.zeros((NT, LANES), f32)
    for i in range(3):
        eps_ref[i, :, pl.ds(x, LANES)] = pad
    eta_ref[:, pl.ds(x, LANES)] = pad
    for ref in (g_out, bg_out, b2g_out, bd_out, b2d_out):
        for i in range(ref.shape[0]):
            ref[i, :, pl.ds(x, LANES)] = pad
    g_rows, bg_rows, b2g_rows, bd_rows, b2d_rows = mended(
        n, (g_in, bg_in, b2g_in, bd_in, b2d_in), (g_out, bg_out, b2g_out, bd_out, b2d_out))
    epsb_ref[:, pl.ds(x, LANES)] = pad
    carry[...] = jnp.zeros(carry.shape, f32)
    sums[...] = sums_in[...]
    for s in range(NT):
        mask_up[:, pl.ds(s * share, share)] = up_ref[pl.ds(s, 1), pl.ds(9 * x, share)] * 4.0 - SHIFT
        mask_down[:, pl.ds(s * share, share)] = down_ref[pl.ds(s, 1), pl.ds(8 * x, share)] * 4.0 - SHIFT

    def from_up(slot, x0):
        return up_ref[:, pl.ds(pl.multiple_of(x0 + slot * x, CHUNK), CHUNK)]

    def from_down(slot, x0):
        return down_ref[:, pl.ds(pl.multiple_of(x0 + slot * x, CHUNK), CHUNK)]

    def known4(i, x0):
        return mask_ref[pl.ds(i, 1), pl.ds(x0, CHUNK)].astype(f32) * 4.0

    def zeroth(c, _):
        x0 = at_chunk(c)
        here = pl.ds(x0, CHUNK)
        slope = si_ref[n, :, here]

        ef = parts(inline_res(sum_diff(m_ref[n, :, here]), sum_diff(from_up(M0, x0)), slope), slope)
        eps = -to_next(ef)
        eps_ref[0, :, here] = eps
        g_rows.store(n, here, (from_up(G0, x0) + eps) * not_last)
        g_rows.store(n - 1, here, g_in[n, :, here] - to_self(ef))
        ef = parts(inline_res(sum_diff(d_ref[n, :, here]), sum_diff(from_up(D0, x0)), slope), slope)
        eta = to_next(ef)
        eta_ref[:, here] = eta
        bd_rows.store(n, here, (from_up(BD0, x0) + eta) * not_last)
        bd_rows.store(n - 1, here, bd_in[n, :, here] + to_self(ef))

        slope = from_down(SI1, x0)
        res = inline_res(sum_diff(from_down(M1, x0)), sum_diff(m_ref[1, :, here]), slope) * not_first
        ef = parts(res, slope)
        eps = -to_self(ef)
        epsb_ref[:, here] = eps
        g_rows.store(-1, here, from_down(G1, x0) + eps)
        g_rows.store(0, here, g_in[1, :, here] - to_next(ef))
        res = inline_res(sum_diff(from_down(D1, x0)), sum_diff(d_ref[1, :, here]), slope) * not_first
        ef = parts(res, slope)
        bd_rows.store(-1, here, from_down(BD1, x0) + to_self(ef))
        bd_rows.store(0, here, bd_in[1, :, here] + to_next(ef))
        return 0

    lax.fori_loop(0, chunks(x), zeroth, 0)

    def slope_in(x0):
        def get(i):
            if i == -1:
                return from_down(SI1, x0)
            return si_ref[i + 1, :, pl.ds(x0, CHUNK)]
        return get

    def edges(x0, src, dst, depth, slot):
        here = pl.ds(x0, CHUNK)
        for lo, hi in ((0, depth), (n - 1 - depth, n - 1)):
            out = stencil(
                lambda i: src.load(i, pl.ds(x0, CHUNK + LANES)),
                slope_in(x0),
                lambda i: sc_ref[i, :, here],
                lo, hi, -1, n - 1, carry, slot, not_first,
            )
            for i in range(lo, hi + 1):
                dst.store(i, here, (known4(i, x0) - SHIFT) * src.load(i, here) + out[i])
            slot += hi - lo + 1
        return slot

    def boundary(src, row, slope, here, scale=None):
        res = inline_res(sum_diff(src.load(row, here)), sum_diff(src.load(row + 1, here)), slope)
        if scale is not None:
            res = res * scale
        return parts(res, slope)

    def first(c, _):
        x0 = at_chunk(c)
        here = pl.ds(x0, CHUNK)
        wide = pl.ds(x0, CHUNK + LANES)
        slot = edges(x0, g_rows, bg_rows, 1, 0)
        slot = edges(x0, bd_rows, b2d_rows, 1, slot)
        slope = si_ref[n, :, here]
        slope_up = from_up(SI0, x0)
        cross_up = from_up(SC0, x0)
        sd = sum_diff(eps_ref[0, :, wide])
        near = head(sd, CHUNK)
        ef8 = parts(slope_up * near[1] - near[0], slope_up)
        same, later = cross_terms(sd, cross_up, carry, slot)
        own = mask_up[:, here] * eps_ref[0, :, here] + (same - ef8[1]) + time_behind(later - ef8[0])
        eps = own + to_next(boundary(g_rows, n - 1, slope, here))
        eps_ref[1, :, here] = eps
        eps_ref[2, :, here] = to_next(ef8)
        bg_rows.store(n, here, (from_up(BG0, x0) + eps) * not_last)
        sd = sum_diff(eta_ref[:, wide])
        near = head(sd, CHUNK)
        ef8 = parts(slope_up * near[1] - near[0], slope_up)
        same, later = cross_terms(sd, cross_up, carry, slot + 1)
        own = mask_up[:, here] * eta_ref[:, here] + (same - ef8[1]) + time_behind(later - ef8[0])
        b2d_rows.store(n, here, (from_up(B2D0, x0) + own + to_next(boundary(bd_rows, n - 1, slope, here))) * not_last)
        slope_low = from_down(SJ1, x0)
        sd = sum_diff(epsb_ref[:, wide])
        near = head(sd, CHUNK)
        ef2 = parts(near[0] + slope_low * near[1], slope_low)
        same, later = cross_terms(sd, from_down(SC1, x0), carry, slot + 2)
        own = mask_down[:, here] * epsb_ref[:, here] + (same + ef2[0]) + time_behind(later + ef2[1])
        bg_rows.store(-1, here, (
            from_down(BG1, x0) + own + to_self(boundary(g_rows, -1, from_down(SI1, x0), here, not_first))
        ))
        return 0

    lax.fori_loop(0, chunks(x), first, 0)
    carry[...] = jnp.zeros(carry.shape, f32)

    def second(c, _):
        x0 = at_chunk(c)
        here = pl.ds(x0, CHUNK)
        wide = pl.ds(x0, CHUNK + LANES)
        slot = edges(x0, bg_rows, b2g_rows, 2, 0)
        slope_up = from_up(SI0, x0)
        sd = sum_diff(eps_ref[1, :, wide])
        near = head(sd, CHUNK)
        ef8 = parts(inline_res(near, sum_diff(eps_ref[2, :, here]), slope_up), slope_up)
        same, later = cross_terms(sd, from_up(SC0, x0), carry, slot)
        own = mask_up[:, here] * eps_ref[1, :, here] + (same - ef8[1]) + time_behind(later - ef8[0])
        b2g_rows.store(n, here, (
            from_up(B2G0, x0) + own + to_next(boundary(bg_rows, n - 1, si_ref[n, :, here], here))
        ) * not_last)
        return 0

    lax.fori_loop(0, chunks(x), second, 0)

    done = range(3, n - 3)
    done_inline = range(3, n - 4)
    loads = [rows.load for rows in (g_rows, bg_rows, b2g_rows)]
    loads += [lambda i, lanes: d_ref[i + 1, :, lanes], bd_rows.load, b2d_rows.load]

    def third(c, _):
        products(
            at_chunk(c), [i for i in range(n) if i not in done], [i for i in range(n) if i not in done_inline],
            loads, known4, si_ref, sc_ref, sums,
        )
        return 0

    lax.fori_loop(0, chunks(x), third, 0)
    for k in range(N_MOMENTS):
        moments_ref[pl.ds(k, 1), :] = jnp.sum(sums[k], axis=0, keepdims=True)
    moments_ref[pl.ds(N_MOMENTS, 24 - N_MOMENTS), :] = jnp.zeros((24 - N_MOMENTS, LANES), f32)


def add_terms(terms):
    total = None
    for term in terms:
        total = term if total is None else total + term
    return total


def solve(moments):
    mu, nu, xi = moments[:6], moments[6:12], moments[12:]

    def entry(a, b, i, j):
        if a == 0 and b == 0:
            return mu[i + j]
        if a == 1 and b == 1:
            return xi[i + j]
        return nu[i + j]

    shifted = {}

    def entry_a(a, b, i, j):
        which = a + b
        if (which, i + j) not in shifted:
            if i + j == 4:
                value = entry(a, b, 2, 3)
            else:
                value = entry(a, b, i, j + 1) + SHIFT * entry(a, b, i, j)
            shifted[which, i + j] = value * 0.25
        return shifted[which, i + j]

    def form(get, u, v):
        rows = []
        for (a, i), left in u.items():
            inner = add_terms(right * get(a, b, i, j) for (b, j), right in v.items())
            rows.append(left * inner)
        return add_terms(rows)

    def axpy(scale, u, v):
        out = dict(v)
        for key, value in u.items():
            term = scale * value
            out[key] = out[key] + term if key in out else term
        return out

    one = jnp.ones_like(mu[0])
    gradient = {(0, 0): 0.25 * one}
    direction = {(1, 0): one}
    model = {}
    for iteration in range(ITERS):
        mixing = -form(entry_a, gradient, direction) / form(entry_a, direction, direction)
        direction = axpy(mixing, direction, gradient)
        step = form(entry, gradient, direction) / form(entry_a, direction, direction)
        model = axpy(step, direction, model)
        if iteration < ITERS - 1:
            image = {key: value * (0.25 * SHIFT) for key, value in direction.items()}
            image = axpy(0.25, {(a, i + 1): value for (a, i), value in direction.items()}, image)
            gradient = axpy(-step, image, gradient)
    return model, direction


def last_kernel(
    n, x, moments_ref, m_ref, d_ref, g_in, bg_in, b2g_in, bd_in, b2d_in, g_end, bg_end, b2g_end, bd_end, b2d_end,
    model_hbm, dir_hbm, mo_ref, do_ref, sems,
):
    moments = [
        jnp.broadcast_to(jnp.sum(moments_ref[pl.ds(k, 1), :], axis=1, keepdims=True), (NT, LANES))
        for k in range(N_MOMENTS)
    ]
    model, direction = solve(moments)
    rows = mended(n, (g_in, bg_in, b2g_in, bd_in, b2d_in), (g_end, bg_end, b2g_end, bd_end, b2d_end))
    keys = ((0, 0), (0, 1), (0, 2), (1, 1), (1, 2))
    copies = []
    for i in range(n):
        def step(c, _):
            x0 = pl.multiple_of(c * LANES, LANES)
            here = pl.ds(x0, LANES)
            values = {key: vector.load(i, here) for key, vector in zip(keys, rows)}
            values[1, 0] = d_ref[i + 1, :, here]
            mo_ref[i, :, here] = m_ref[i + 1, :, here] + add_terms(
                model[key] * value for key, value in values.items())
            do_ref[i, :, here] = add_terms(direction[key] * value for key, value in values.items())
            return 0

        lax.fori_loop(0, x // LANES, step, 0, unroll=4)
        for k, (src, dst) in enumerate(((mo_ref, model_hbm), (do_ref, dir_hbm))):
            copy = pltpu.make_async_copy(src.at[i], dst.at[i], sems.at[2 * i + k])
            copy.start()
            copies.append(copy)
    for copy in copies:
        copy.wait()


def in_vmem(values):
    return [pltpu.with_memory_space_constraint(v, pltpu.VMEM) for v in values]


def kept(shape, dtype=f32):
    return pltpu.VMEM(shape, dtype)


def on_device(*args):
    n, _, x = args[0].shape
    peers = lax.axis_size("inline")
    vmem = pl.BlockSpec(memory_space=pltpu.VMEM)
    hbm = pl.BlockSpec(memory_space=pl.ANY)
    params = pltpu.CompilerParams(vmem_limit_bytes=VMEM_LIMIT)
    wide = kept((n + 2, NT, x + LANES))
    share = x // NT

    args = [pltpu.with_memory_space_constraint(v, pltpu.HBM) for v in args]
    up, down = pl.pallas_call(
        functools.partial(edge_kernel, n, x),
        out_shape=[kept((NT, 9 * x + share)), kept((NT, 8 * x + share))],
        in_specs=[hbm] * 6,
        out_specs=[vmem] * 2,
        scratch_shapes=[
            pltpu.VMEM((n, NT, x), f32),
            pltpu.VMEM((n, x), jnp.int32),
            pltpu.VMEM((n, NT, x), f32),
            pltpu.VMEM((n, NT, x), f32),
        ] + [pltpu.VMEM((n, NT, x + LANES), f32)] * 5 + [
            pltpu.VMEM((8, 2, NT, LANES), f32),
            pltpu.SemaphoreType.DMA((11,)),
        ],
        compiler_params=params,
        name="edges",
    )(*args)
    up = lax.ppermute(up, "inline", [(i, i - 1) for i in range(1, peers)])
    down = lax.ppermute(down, "inline", [(i, i + 1) for i in range(peers - 1)])

    local = pl.pallas_call(
        functools.partial(local_kernel, n, x),
        out_shape=[
            wide, wide, kept((n + 2, NT, x)), kept((n, NT, x)), kept((n, x), jnp.int32),
            wide, wide, wide, wide, wide, kept((N_MOMENTS, NT, LANES)),
        ],
        in_specs=[hbm] * 6,
        out_specs=[vmem] * 11,
        scratch_shapes=[
            pltpu.VMEM((n, NT, x), f32),
            pltpu.VMEM((2 * n, 2, NT, LANES), f32),
            pltpu.SemaphoreType.DMA((6,)),
        ],
        compiler_params=params,
        name="local",
    )(*args)
    m, d, _, _, _, g, bg, b2g, bd, b2d, _ = local

    out = pl.pallas_call(
        functools.partial(join_kernel, n, x),
        out_shape=[kept((2 * depth + 2, NT, x + LANES)) for depth in (1, 2, 3, 1, 2)]
        + [jax.ShapeDtypeStruct((24, LANES), f32)],
        in_specs=[vmem] * 13,
        out_specs=[vmem] * 6,
        scratch_shapes=[
            pltpu.VMEM((3, NT, x + LANES), f32),
            pltpu.VMEM((NT, x + LANES), f32),
            pltpu.VMEM((NT, x + LANES), f32),
            pltpu.VMEM((1, x), f32),
            pltpu.VMEM((1, x), f32),
            pltpu.VMEM((12, 2, NT, LANES), f32),
            pltpu.VMEM((N_MOMENTS, NT, LANES), f32),
        ],
        compiler_params=params,
        name="join",
    )(*in_vmem(local), up, down)
    *ends_out, moments = out

    reach = 1
    while reach < peers:
        moments = moments + lax.ppermute(moments, "inline", [(i, i ^ reach) for i in range(peers)])
        reach *= 2

    return pl.pallas_call(
        functools.partial(last_kernel, n, x),
        out_shape=[jax.ShapeDtypeStruct((n, NT, x), f32)] * 2,
        in_specs=[vmem] * 13,
        out_specs=[hbm] * 2,
        scratch_shapes=[
            pltpu.VMEM((n, NT, x), f32),
            pltpu.VMEM((n, NT, x), f32),
            pltpu.SemaphoreType.DMA((2 * n,)),
        ],
        compiler_params=params,
        name="last",
    )(moments, *in_vmem([m, d, g, bg, b2g, bd, b2d, *ends_out]))


def solution(mesh):
    rows = P(("groups", "inline"), None, None)
    return jax.shard_map(
        on_device,
        mesh=mesh,
        in_specs=(rows, P(("groups", "inline"), None), rows, rows, rows, rows),
        out_specs=(rows, rows),
        check_vma=False,
    )
```

```python
import functools

import jax
import jax.numpy as jnp
from jax import lax
from jax.experimental import pallas as pl
from jax.experimental.pallas import tpu as pltpu
from jax.sharding import PartitionSpec as P

ITERS = 3
NT = 8
LANES = 128
CHUNK = 4096
SHIFT = 18.0
M0, D0, SI0, SC0, G0, BD0, FIRST0 = range(7)
BG0, B2D0, B2G0, LATE0 = range(4)
M1, D1, SI1, SC1, SJ1, G1, BD1, FIRST1 = range(8)
BG1, LATE1 = range(2)
N_MOMENTS = 18
VMEM_LIMIT = 16 * 1024 * 1024

f32 = jnp.float32


def time_ahead(v):
    rolled = pltpu.roll(v, NT - 1, 0)
    return jnp.where(lax.broadcasted_iota(jnp.int32, v.shape, 0) == NT - 1, 0.0, rolled)


def time_behind(v):
    rolled = pltpu.roll(v, 1, 0)
    return jnp.where(lax.broadcasted_iota(jnp.int32, v.shape, 0) == 0, 0.0, rolled)


def sum_diff(v):
    ahead = time_ahead(v)
    return ahead + v, ahead - v


def head(pair, width):
    return pair[0][:, :width], pair[1][:, :width]


def inline_res(here, after, slope):
    return (after[0] - here[0]) + slope * (after[1] + here[1])


def parts(res, slope):
    scaled = slope * res
    return res - scaled, res + scaled


def to_next(ef):
    return ef[0] + time_behind(ef[1])


def to_self(ef):
    return -(ef[1] + time_behind(ef[0]))


def lane_ahead(v):
    width = v.shape[1]
    return pltpu.roll(v, width - 1, 1)[:, : width - LANES]


def lane_behind(before, v):
    joined = jnp.concatenate([before, v], axis=1)
    return pltpu.roll(joined, 1, 1)[:, LANES:]


def cross_res(sd, slope):
    width = sd[0].shape[1] - LANES
    here = head(sd, width)
    return (lane_ahead(sd[0]) - here[0]) + slope * (lane_ahead(sd[1]) + here[1])


def cross_terms(sd, slope, carry, slot):
    e, f = parts(cross_res(sd, slope), slope)
    e_behind = lane_behind(carry[slot, 0], e)
    f_behind = lane_behind(carry[slot, 1], f)
    carry[slot, 0] = e[:, -LANES:]
    carry[slot, 1] = f[:, -LANES:]
    return e_behind - f, f_behind - e


def stencil(load, slope_in, slope_cr, lo, hi, res_lo, res_hi, carry, slot, scale_lo=None):
    out = {}
    sd = {}

    def pair(i):
        if i not in sd:
            sd[i] = sum_diff(load(i))
        return sd[i]

    before = None
    for i in range(lo - 1, hi + 1):
        here = None
        if res_lo <= i <= res_hi:
            first = pair(i)
            second = pair(i + 1)
            width = first[0].shape[1] - LANES
            slope = slope_in(i)
            res = inline_res(head(first, width), head(second, width), slope)
            if i == -1 and scale_lo is not None:
                res = res * scale_lo
            here = parts(res, slope)
        if i >= lo:
            same, later = cross_terms(pair(i), slope_cr(i), carry, slot + i - lo)
            if before is not None:
                same = same + before[0]
                later = later + before[1]
            if here is not None:
                same = same - here[1]
                later = later - here[0]
            out[i] = same + time_behind(later)
        before = here
    return out


class Mended:
    def __init__(self, n, depth, whole, ends, before=None, after=None):
        self.n, self.depth, self.whole, self.ends, self.before, self.after = n, depth, whole, ends, before, after

    def at(self, i):
        if i < 0:
            return self.before
        if i >= self.n:
            return self.after
        if i < self.depth:
            return self.ends, i
        if i >= self.n - self.depth:
            return self.ends, i - self.n + 2 * self.depth
        return self.whole, i + 1

    def load(self, i, lanes):
        ref, row = self.at(i)
        return ref[row, :, lanes]

    def store(self, i, lanes, value):
        ref, row = self.at(i)
        ref[row, :, lanes] = value


def chunks(x):
    return x // CHUNK


def at_chunk(c):
    return pl.multiple_of(c * CHUNK, CHUNK)


class Own:
    def __init__(self, n, x0, si_ref, sc_ref, mask_ref, carry):
        self.n, self.x0, self.here = n, x0, pl.ds(x0, CHUNK)
        self.si_ref, self.sc_ref, self.mask_ref, self.carry = si_ref, sc_ref, mask_ref, carry

    def known4(self, i):
        return self.mask_ref[pl.ds(i, 1), self.here].astype(f32) * 4.0

    def level(self, src, lo, hi, slot):
        return stencil(
            lambda i: src[i + 1, :, pl.ds(self.x0, CHUNK + LANES)],
            lambda i: self.si_ref[i + 1, :, self.here],
            lambda i: self.sc_ref[i, :, self.here],
            lo, hi, 0, self.n - 2, self.carry, slot,
        )

    def applied(self, src, lo, hi, slot):
        out = self.level(src, lo, hi, slot)
        return {i: (self.known4(i) - SHIFT) * src[i + 1, :, self.here] + out[i] for i in out}

    def gradient(self, data_ref, m_ref, lo, hi, slot):
        out = self.level(m_ref, lo, hi, slot)
        return {i: self.known4(i) * (data_ref[i, :, self.here] - m_ref[i + 1, :, self.here]) - out[i] for i in out}


def put(ref, slot, x, x0, value):
    ref[:, pl.ds(pl.multiple_of(x0 + slot * x, CHUNK), CHUNK)] = value


def first_kernel(
    n, x,
    data_hbm, mask_hbm, si_hbm, sc_hbm, model_hbm, dir_hbm,
    data_ref, mask_ref, si_ref, sc_ref, m_ref, d_ref, up_ref, down_ref,
    carry, sems,
):
    body = (pl.ds(1, n), slice(None), pl.ds(0, x))
    copies = [
        pltpu.make_async_copy(source, target, sems.at[k])
        for k, (source, target) in enumerate((
            (model_hbm, m_ref.at[body]), (dir_hbm, d_ref.at[body]), (si_hbm, si_ref.at[pl.ds(1, n)]), (sc_hbm, sc_ref),
            (mask_hbm, mask_ref), (data_hbm, data_ref),
        ))
    ]
    for copy in copies:
        copy.start()
    clear_pads(x, (m_ref, d_ref))
    carry[...] = jnp.zeros(carry.shape, f32)
    for copy in copies:
        copy.wait()
    share = x // NT
    for s in range(NT):
        up_ref[pl.ds(s, 1), pl.ds(FIRST0 * x, share)] = mask_ref[pl.ds(0, 1), pl.ds(s * share, share)].astype(f32)
        down_ref[pl.ds(s, 1), pl.ds(FIRST1 * x, share)] = mask_ref[pl.ds(n - 1, 1), pl.ds(s * share, share)].astype(f32)

    def rows(c, _):
        x0 = at_chunk(c)
        here = pl.ds(x0, CHUNK)
        own = Own(n, x0, si_ref, sc_ref, mask_ref, carry)
        put(up_ref, G0, x, x0, own.gradient(data_ref, m_ref, 0, 0, 0)[0])
        put(up_ref, BD0, x, x0, own.applied(d_ref, 0, 0, 1)[0])
        put(down_ref, G1, x, x0, own.gradient(data_ref, m_ref, n - 1, n - 1, 2)[n - 1])
        put(down_ref, BD1, x, x0, own.applied(d_ref, n - 1, n - 1, 3)[n - 1])
        put(up_ref, M0, x, x0, m_ref[1, :, here])
        put(up_ref, D0, x, x0, d_ref[1, :, here])
        put(up_ref, SI0, x, x0, si_ref[1, :, here])
        put(up_ref, SC0, x, x0, sc_ref[0, :, here])
        put(down_ref, M1, x, x0, m_ref[n, :, here])
        put(down_ref, D1, x, x0, d_ref[n, :, here])
        put(down_ref, SI1, x, x0, si_ref[n, :, here])
        put(down_ref, SC1, x, x0, sc_ref[n - 1, :, here])
        put(down_ref, SJ1, x, x0, si_ref[n - 1, :, here])
        return 0

    lax.fori_loop(0, chunks(x), rows, 0)


def edge_kernel(
    n, x, data_ref, mask_ref, si_ref, sc_ref, m_ref, d_ref, up_first, down_first, up_ref, down_ref,
    g_ref, bg_ref, bd_ref, carry,
):
    clear_pads(x, (g_ref, bg_ref, bd_ref))
    carry[...] = jnp.zeros(carry.shape, f32)

    def first(c, _):
        x0 = at_chunk(c)
        here = pl.ds(x0, CHUNK)
        own = Own(n, x0, si_ref, sc_ref, mask_ref, carry)
        for i, value in {**own.gradient(data_ref, m_ref, 1, 2, 0), **own.gradient(data_ref, m_ref, n - 2, n - 2, 2)}.items():
            g_ref[i + 1, :, here] = value
        g_ref[1, :, here] = row_of(up_first, G0, x, x0)
        g_ref[n, :, here] = row_of(down_first, G1, x, x0)
        bd_ref[1, :, here] = row_of(up_first, BD0, x, x0)
        bd_ref[2, :, here] = own.applied(d_ref, 1, 1, 3)[1]
        return 0

    lax.fori_loop(0, chunks(x), first, 0)
    carry[...] = jnp.zeros(carry.shape, f32)

    def second(c, _):
        x0 = at_chunk(c)
        here = pl.ds(x0, CHUNK)
        own = Own(n, x0, si_ref, sc_ref, mask_ref, carry)
        out = own.applied(g_ref, 0, 1, 0)
        for i in (0, 1):
            bg_ref[i + 1, :, here] = out[i]
        put(up_ref, BG0, x, x0, out[0])
        put(down_ref, BG1, x, x0, own.applied(g_ref, n - 1, n - 1, 2)[n - 1])
        put(up_ref, B2D0, x, x0, own.applied(bd_ref, 0, 0, 3)[0])
        return 0

    lax.fori_loop(0, chunks(x), second, 0)
    carry[...] = jnp.zeros(carry.shape, f32)

    def third(c, _):
        x0 = at_chunk(c)
        put(up_ref, B2G0, x, x0, Own(n, x0, si_ref, sc_ref, mask_ref, carry).applied(bg_ref, 0, 0, 0)[0])
        return 0

    lax.fori_loop(0, chunks(x), third, 0)


def local_kernel(
    n, x, data_ref, mask_ref, si_ref, sc_ref, m_ref, d_ref,
    g_ref, bg_ref, b2g_ref, bd_ref, b2d_ref, sums_ref, carry,
):
    clear_pads(x, (g_ref, bg_ref, b2g_ref, bd_ref, b2d_ref))
    carry[...] = jnp.zeros(carry.shape, f32)
    sums_ref[...] = jnp.zeros(sums_ref.shape, f32)

    def first(c, _):
        x0 = at_chunk(c)
        own = Own(n, x0, si_ref, sc_ref, mask_ref, carry)
        for i, value in own.gradient(data_ref, m_ref, 0, n - 1, 0).items():
            g_ref[i + 1, :, own.here] = value
        for i, value in own.applied(d_ref, 0, n - 1, n).items():
            bd_ref[i + 1, :, own.here] = value
        return 0

    lax.fori_loop(0, chunks(x), first, 0)
    carry[...] = jnp.zeros(carry.shape, f32)

    def second(c, _):
        x0 = at_chunk(c)
        own = Own(n, x0, si_ref, sc_ref, mask_ref, carry)
        for i, value in own.applied(g_ref, 2, n - 3, 0).items():
            bg_ref[i + 1, :, own.here] = value
        for i, value in own.applied(bd_ref, 2, n - 3, n).items():
            b2d_ref[i + 1, :, own.here] = value
        return 0

    lax.fori_loop(0, chunks(x), second, 0)
    carry[...] = jnp.zeros(carry.shape, f32)

    def third(c, _):
        x0 = at_chunk(c)
        own = Own(n, x0, si_ref, sc_ref, mask_ref, carry)
        for i, value in own.applied(bg_ref, 3, n - 4, 0).items():
            b2g_ref[i + 1, :, own.here] = value
        return 0

    lax.fori_loop(0, chunks(x), third, 0)

    def fourth(c, _):
        x0 = at_chunk(c)
        here = pl.ds(x0, CHUNK)
        own = Own(n, x0, si_ref, sc_ref, mask_ref, carry)
        refs = (g_ref, bg_ref, b2g_ref, d_ref, bd_ref, b2d_ref)
        totals = Totals()
        pairs = [Pairs(lambda i, lanes, ref=ref: ref[i + 1, :, lanes], x0) for ref in (b2g_ref, b2d_ref)]
        for i in range(3, n - 3):
            values = [ref[i + 1, :, here] for ref in refs]
            for k, which in enumerate(PAIRS):
                if which is not None:
                    totals.add(k, values[which[0]], values[which[1]])
            known = own.known4(i)
            members = [(values[2], values[5], known * values[2], known * values[5])]
            members.append(tuple(pair.cross(i, sc_ref[i, :, here]) for pair in pairs) * 2)
            if i < n - 4:
                members.append(tuple(pair.inline(i, si_ref[i + 1, :, here]) for pair in pairs) * 2)
            for u, v, also_u, also_v in members:
                totals.add(5, u, also_u)
                totals.add(11, v, also_u)
                totals.add(17, v, also_v)
        totals.put(sums_ref)
        return 0

    lax.fori_loop(0, chunks(x), fourth, 0)


PAIRS = ((0, 0), (0, 1), (1, 1), (1, 2), (2, 2), None, (0, 3), (0, 4), (1, 4), (1, 5), (2, 5), None,
         (3, 3), (3, 4), (4, 4), (4, 5), (5, 5), None)


class Totals:
    def __init__(self):
        self.of = {}

    def add(self, k, left, right):
        product = left * right
        acc = product[:, :LANES]
        for j in range(1, CHUNK // LANES):
            acc = acc + product[:, j * LANES:(j + 1) * LANES]
        self.of[k] = self.of[k] + acc if k in self.of else acc

    def put(self, sums):
        for k, value in self.of.items():
            sums[k] = sums[k] + value


class Pairs:
    def __init__(self, load, x0):
        self.load, self.lanes, self.of = load, pl.ds(x0, CHUNK + LANES), {}

    def at(self, i):
        if i not in self.of:
            self.of[i] = sum_diff(self.load(i, self.lanes))
        return self.of[i]

    def inline(self, i, slope):
        return inline_res(head(self.at(i), CHUNK), head(self.at(i + 1), CHUNK), slope)

    def cross(self, i, slope):
        return cross_res(self.at(i), slope)


def place_flags():
    place = lax.axis_index("inline")
    return (place > 0).astype(f32), (place < lax.axis_size("inline") - 1).astype(f32)


def row_of(ref, slot, x, x0):
    return ref[:, pl.ds(pl.multiple_of(x0 + slot * x, CHUNK), CHUNK)]


def boundary(rows, i, slope, here, scale=None):
    res = inline_res(sum_diff(rows.load(i, here)), sum_diff(rows.load(i + 1, here)), slope)
    if scale is not None:
        res = res * scale
    return parts(res, slope)


def clear_pads(x, refs):
    for ref in refs:
        for i in range(ref.shape[0]):
            ref[i, :, pl.ds(x, LANES)] = jnp.zeros((NT, LANES), f32)


def end_rows(n, x0, src, dst, depth, slope_before, si_ref, sc_ref, known4, scale, carry, slot):
    here = pl.ds(x0, CHUNK)
    for lo, hi in ((0, depth), (n - 1 - depth, n - 1)):
        out = stencil(
            lambda i: src.load(i, pl.ds(x0, CHUNK + LANES)),
            lambda i: slope_before if i == -1 else si_ref[i + 1, :, here],
            lambda i: sc_ref[i, :, here],
            lo, hi, -1, n - 1, carry, slot, scale,
        )
        for i in range(lo, hi + 1):
            dst.store(i, here, (known4(i, x0) - SHIFT) * src.load(i, here) + out[i])
        slot += hi - lo + 1
    return slot


def beyond(rows_ref, row, wide, width, diagonal, cross, slope_inner, carry, slot, after, further=None):
    here = pl.ds(wide.start, width)
    sd = sum_diff(rows_ref[row, :, wide])
    near = head(sd, width)
    same, later = cross_terms(sd, cross, carry, slot)
    if after:
        if further is None:
            inner = parts(slope_inner * near[1] - near[0], slope_inner)
        else:
            inner = parts(inline_res(near, sum_diff(further), slope_inner), slope_inner)
        same, later = same - inner[1], later - inner[0]
    else:
        inner = parts(near[0] + slope_inner * near[1], slope_inner)
        same, later = same + inner[0], later + inner[1]
    return diagonal * rows_ref[row, :, here] + same + time_behind(later), inner


def join_kernel(
    n, x,
    m_ref, d_ref, si_ref, sc_ref, mask_ref, g_in, bg_in, bd_in, b2d_in, sums_in, up_ref, down_ref,
    g_out, bg_out, bd_out, b2d_out, sums, eps_out, res_out, mask_up,
    eps_ref, ghosts, mask_down, carry,
):
    not_first, not_last = place_flags()
    share = x // NT
    clear_pads(x, (eps_ref, eps_out, ghosts, g_out, bg_out, bd_out, b2d_out))
    carry[...] = jnp.zeros(carry.shape, f32)
    sums[...] = sums_in[...]
    for s in range(NT):
        mask_up[:, pl.ds(s * share, share)] = up_ref[pl.ds(s, 1), pl.ds(FIRST0 * x, share)] * 4.0 - SHIFT
        mask_down[:, pl.ds(s * share, share)] = down_ref[pl.ds(s, 1), pl.ds(FIRST1 * x, share)] * 4.0 - SHIFT
    g_rows = Mended(n, 1, g_in, g_out, (ghosts, 0), (ghosts, 1))
    bd_rows = Mended(n, 1, bd_in, bd_out, (ghosts, 2), (ghosts, 3))
    bg_rows = Mended(n, 2, bg_in, bg_out)
    b2d_rows = Mended(n, 2, b2d_in, b2d_out)

    def known4(i, x0):
        return mask_ref[pl.ds(i, 1), pl.ds(x0, CHUNK)].astype(f32) * 4.0

    def zeroth(c, _):
        x0 = at_chunk(c)
        here = pl.ds(x0, CHUNK)
        slope = si_ref[n, :, here]
        ef = parts(inline_res(sum_diff(m_ref[n, :, here]), sum_diff(row_of(up_ref, M0, x, x0)), slope), slope)
        eps = -to_next(ef)
        eps_ref[0, :, here] = eps
        g_rows.store(n, here, (row_of(up_ref, G0, x, x0) + eps) * not_last)
        g_rows.store(n - 1, here, g_in[n, :, here] - to_self(ef))
        ef = parts(inline_res(sum_diff(d_ref[n, :, here]), sum_diff(row_of(up_ref, D0, x, x0)), slope), slope)
        eps = to_next(ef)
        eps_ref[1, :, here] = eps
        bd_rows.store(n, here, (row_of(up_ref, BD0, x, x0) + eps) * not_last)
        bd_rows.store(n - 1, here, bd_in[n, :, here] + to_self(ef))

        slope = row_of(down_ref, SI1, x, x0)
        res = inline_res(sum_diff(row_of(down_ref, M1, x, x0)), sum_diff(m_ref[1, :, here]), slope) * not_first
        ef = parts(res, slope)
        eps = -to_self(ef)
        eps_ref[2, :, here] = eps
        g_rows.store(-1, here, row_of(down_ref, G1, x, x0) + eps)
        g_rows.store(0, here, g_in[1, :, here] - to_next(ef))
        res = inline_res(sum_diff(row_of(down_ref, D1, x, x0)), sum_diff(d_ref[1, :, here]), slope) * not_first
        ef = parts(res, slope)
        bd_rows.store(-1, here, row_of(down_ref, BD1, x, x0) + to_self(ef))
        bd_rows.store(0, here, bd_in[1, :, here] + to_next(ef))
        return 0

    lax.fori_loop(0, chunks(x), zeroth, 0)

    def first(c, _):
        x0 = at_chunk(c)
        here = pl.ds(x0, CHUNK)
        wide = pl.ds(x0, CHUNK + LANES)
        before = row_of(down_ref, SI1, x, x0)
        slot = end_rows(n, x0, g_rows, bg_rows, 1, before, si_ref, sc_ref, known4, not_first, carry, 0)
        slot = end_rows(n, x0, bd_rows, b2d_rows, 1, before, si_ref, sc_ref, known4, not_first, carry, slot)
        slope = si_ref[n, :, here]
        slope_up = row_of(up_ref, SI0, x, x0)
        cross_up = row_of(up_ref, SC0, x, x0)
        diagonal = mask_up[:, here]
        own, inner = beyond(eps_ref, 0, wide, CHUNK, diagonal, cross_up, slope_up, carry, slot, True)
        eps_out[0, :, here] = own + to_next(boundary(g_rows, n - 1, slope, here))
        eps_out[1, :, here] = to_next(inner)
        own, _ = beyond(eps_ref, 1, wide, CHUNK, diagonal, cross_up, slope_up, carry, slot + 1, True)
        eps_out[2, :, here] = own + to_next(boundary(bd_rows, n - 1, slope, here))
        own, _ = beyond(
            eps_ref, 2, wide, CHUNK, mask_down[:, here], row_of(down_ref, SC1, x, x0), row_of(down_ref, SJ1, x, x0),
            carry, slot + 2, False)
        eps_out[3, :, here] = own + to_self(boundary(g_rows, -1, before, here, not_first))
        return 0

    lax.fori_loop(0, chunks(x), first, 0)

    def second(c, _):
        x0 = at_chunk(c)
        here = pl.ds(x0, CHUNK)
        totals = Totals()
        pair = Pairs(b2d_rows.load, x0)
        for i in range(n):
            if not 3 <= i < n - 3:
                values = [g_rows.load(i, here), bg_rows.load(i, here), None, d_ref[i + 1, :, here],
                          bd_rows.load(i, here), b2d_rows.load(i, here)]
                for k, which in enumerate(PAIRS):
                    if which is not None and 2 not in which:
                        totals.add(k, values[which[0]], values[which[1]])
                totals.add(17, values[5], known4(i, x0) * values[5])
                res = pair.cross(i, sc_ref[i, :, here])
                res_out[n + i, :, here] = res
                totals.add(17, res, res)
            if not 3 <= i < n - 4 and i < n - 1:
                res = pair.inline(i, si_ref[i + 1, :, here])
                res_out[i, :, here] = res
                totals.add(17, res, res)
        totals.put(sums)
        return 0

    lax.fori_loop(0, chunks(x), second, 0)


def close_kernel(
    n, x,
    si_ref, sc_ref, mask_ref, bg_in, b2g_in, b2d_in, bg_end, b2d_end, sums_in, eps_ref, res_ref, mask_up, up_first, down_first,
    up_ref, down_ref,
    b2g_out, moments_ref,
    ghosts, carry, sums,
):
    not_first, not_last = place_flags()
    clear_pads(x, (ghosts, b2g_out))
    carry[...] = jnp.zeros(carry.shape, f32)
    sums[...] = sums_in[...]
    bg_rows = Mended(n, 2, bg_in, bg_end, (ghosts, 0), (ghosts, 1))
    b2g_rows = Mended(n, 3, b2g_in, b2g_out, None, (ghosts, 2))
    b2d_rows = Mended(n, 2, b2d_in, b2d_end)

    def known4(i, x0):
        return mask_ref[pl.ds(i, 1), pl.ds(x0, CHUNK)].astype(f32) * 4.0

    def first(c, _):
        x0 = at_chunk(c)
        here = pl.ds(x0, CHUNK)
        bg_rows.store(-1, here, row_of(down_ref, BG1, x, x0) + eps_ref[3, :, here])
        bg_rows.store(n, here, (row_of(up_ref, BG0, x, x0) + eps_ref[0, :, here]) * not_last)
        return 0

    lax.fori_loop(0, chunks(x), first, 0)

    def second(c, _):
        x0 = at_chunk(c)
        here = pl.ds(x0, CHUNK)
        wide = pl.ds(x0, CHUNK + LANES)
        slot = end_rows(n, x0, bg_rows, b2g_rows, 2, row_of(down_first, SI1, x, x0), si_ref, sc_ref, known4, not_first, carry, 0)
        own, _ = beyond(
            eps_ref, 0, wide, CHUNK, mask_up[:, here], row_of(up_first, SC0, x, x0), row_of(up_first, SI0, x, x0),
            carry, slot, True, eps_ref[1, :, here])
        edge = to_next(boundary(bg_rows, n - 1, si_ref[n, :, here], here))
        b2g_rows.store(n, here, (row_of(up_ref, B2G0, x, x0) + own + edge) * not_last)
        return 0

    lax.fori_loop(0, chunks(x), second, 0)

    def third(c, _):
        x0 = at_chunk(c)
        here = pl.ds(x0, CHUNK)
        totals = Totals()
        pair = Pairs(b2g_rows.load, x0)
        for i in range(n):
            if not 3 <= i < n - 3:
                bg, b2g, b2d = (rows.load(i, here) for rows in (bg_rows, b2g_rows, b2d_rows))
                totals.add(3, bg, b2g)
                totals.add(4, b2g, b2g)
                totals.add(10, b2g, b2d)
                weighed = known4(i, x0) * b2g
                totals.add(5, b2g, weighed)
                totals.add(11, b2d, weighed)
                res = pair.cross(i, sc_ref[i, :, here])
                totals.add(5, res, res)
                totals.add(11, res, res_ref[n + i, :, here])
            if not 3 <= i < n - 4:
                slope = si_ref[i + 1, :, here]
                res = pair.inline(i, slope)
                if i < n - 1:
                    other = res_ref[i, :, here]
                else:
                    after = (row_of(up_ref, B2D0, x, x0) + eps_ref[2, :, here]) * not_last
                    other = inline_res(sum_diff(b2d_rows.load(i, here)), sum_diff(after), slope)
                    totals.add(17, other, other)
                totals.add(5, res, res)
                totals.add(11, res, other)
        totals.put(sums)
        return 0

    lax.fori_loop(0, chunks(x), third, 0)
    for k in range(N_MOMENTS):
        moments_ref[pl.ds(k, 1), :] = jnp.sum(sums[k], axis=0, keepdims=True)
    moments_ref[pl.ds(N_MOMENTS, 24 - N_MOMENTS), :] = jnp.zeros((24 - N_MOMENTS, LANES), f32)


def add_terms(terms):
    total = None
    for term in terms:
        total = term if total is None else total + term
    return total


def solve(moments):
    mu, nu, xi = moments[:6], moments[6:12], moments[12:]

    def entry(a, b, i, j):
        if a == 0 and b == 0:
            return mu[i + j]
        if a == 1 and b == 1:
            return xi[i + j]
        return nu[i + j]

    shifted = {}

    def entry_a(a, b, i, j):
        which = a + b
        if (which, i + j) not in shifted:
            if i + j == 4:
                value = entry(a, b, 2, 3)
            else:
                value = entry(a, b, i, j + 1) + SHIFT * entry(a, b, i, j)
            shifted[which, i + j] = value * 0.25
        return shifted[which, i + j]

    def form(get, u, v):
        rows = []
        for (a, i), left in u.items():
            inner = add_terms(right * get(a, b, i, j) for (b, j), right in v.items())
            rows.append(left * inner)
        return add_terms(rows)

    def axpy(scale, u, v):
        out = dict(v)
        for key, value in u.items():
            term = scale * value
            out[key] = out[key] + term if key in out else term
        return out

    one = jnp.ones_like(mu[0])
    gradient = {(0, 0): 0.25 * one}
    direction = {(1, 0): one}
    model = {}
    for iteration in range(ITERS):
        mixing = -form(entry_a, gradient, direction) / form(entry_a, direction, direction)
        direction = axpy(mixing, direction, gradient)
        step = form(entry, gradient, direction) / form(entry_a, direction, direction)
        model = axpy(step, direction, model)
        if iteration < ITERS - 1:
            image = {key: value * (0.25 * SHIFT) for key, value in direction.items()}
            image = axpy(0.25, {(a, i + 1): value for (a, i), value in direction.items()}, image)
            gradient = axpy(-step, image, gradient)
    return model, direction


def last_kernel(
    n, x, moments_ref, m_ref, d_ref, g_in, bg_in, b2g_in, bd_in, b2d_in, g_end, bg_end, b2g_end, bd_end, b2d_end,
    model_hbm, dir_hbm, mo_ref, do_ref, sems,
):
    moments = [
        jnp.broadcast_to(jnp.sum(moments_ref[pl.ds(k, 1), :], axis=1, keepdims=True), (NT, LANES))
        for k in range(N_MOMENTS)
    ]
    model, direction = solve(moments)
    rows = [
        Mended(n, depth, whole, ends)
        for depth, whole, ends in ((1, g_in, g_end), (2, bg_in, bg_end), (3, b2g_in, b2g_end), (1, bd_in, bd_end), (2, b2d_in, b2d_end))
    ]
    keys = ((0, 0), (0, 1), (0, 2), (1, 1), (1, 2))
    copies = []
    for i in range(n):
        def step(c, _):
            x0 = pl.multiple_of(c * LANES, LANES)
            here = pl.ds(x0, LANES)
            values = {key: vector.load(i, here) for key, vector in zip(keys, rows)}
            values[1, 0] = d_ref[i + 1, :, here]
            mo_ref[i, :, here] = m_ref[i + 1, :, here] + add_terms(
                model[key] * value for key, value in values.items())
            do_ref[i, :, here] = add_terms(direction[key] * value for key, value in values.items())
            return 0

        lax.fori_loop(0, x // LANES, step, 0, unroll=4)
        for k, (src, dst) in enumerate(((mo_ref, model_hbm), (do_ref, dir_hbm))):
            copy = pltpu.make_async_copy(src.at[i], dst.at[i], sems.at[2 * i + k])
            copy.start()
            copies.append(copy)
    for copy in copies:
        copy.wait()


def in_vmem(values):
    return [pltpu.with_memory_space_constraint(v, pltpu.VMEM) for v in values]


def kept(shape, dtype=f32):
    return pltpu.VMEM(shape, dtype)


def on_device(*args):
    n, _, x = args[0].shape
    peers = lax.axis_size("inline")
    vmem = pl.BlockSpec(memory_space=pltpu.VMEM)
    hbm = pl.BlockSpec(memory_space=pl.ANY)
    params = pltpu.CompilerParams(vmem_limit_bytes=VMEM_LIMIT)
    wide = kept((n + 2, NT, x + LANES))
    share = x // NT

    args = [pltpu.with_memory_space_constraint(v, pltpu.HBM) for v in args]
    def exchange(up, down):
        return (
            lax.ppermute(up, "inline", [(i, i - 1) for i in range(1, peers)]),
            lax.ppermute(down, "inline", [(i, i + 1) for i in range(peers - 1)]),
        )

    *loaded, up, down = pl.pallas_call(
        functools.partial(first_kernel, n, x),
        out_shape=[
            kept((n, NT, x)), kept((n, x), jnp.int32), kept((n + 2, NT, x)), kept((n, NT, x)), wide, wide,
            kept((NT, FIRST0 * x + share)), kept((NT, FIRST1 * x + share)),
        ],
        in_specs=[hbm] * 6,
        out_specs=[vmem] * 8,
        scratch_shapes=[pltpu.VMEM((4, 2, NT, LANES), f32), pltpu.SemaphoreType.DMA((6,))],
        compiler_params=params,
        name="first",
    )(*args)
    loaded = in_vmem(loaded)
    _, mask, si, sc, m, d = loaded
    first = exchange(up, down)

    late = exchange(*pl.pallas_call(
        functools.partial(edge_kernel, n, x),
        out_shape=[kept((NT, LATE0 * x)), kept((NT, LATE1 * x))],
        in_specs=[vmem] * 8,
        out_specs=[vmem] * 2,
        scratch_shapes=[pltpu.VMEM((n + 2, NT, x + LANES), f32)] * 3 + [pltpu.VMEM((4, 2, NT, LANES), f32)],
        compiler_params=params,
        name="edges",
    )(*loaded, up, down))

    g, bg, b2g, bd, b2d, sums = in_vmem(pl.pallas_call(
        functools.partial(local_kernel, n, x),
        out_shape=[wide, wide, wide, wide, wide, kept((N_MOMENTS, NT, LANES))],
        in_specs=[vmem] * 6,
        out_specs=[vmem] * 6,
        scratch_shapes=[pltpu.VMEM((2 * n, 2, NT, LANES), f32)],
        compiler_params=params,
        name="local",
    )(*loaded))

    def ends(rows):
        return kept((rows, NT, x + LANES))

    out = pl.pallas_call(
        functools.partial(join_kernel, n, x),
        out_shape=[
            ends(2), ends(4), ends(2), ends(4), kept((N_MOMENTS, NT, LANES)), ends(4), kept((2 * n, NT, x)), kept((1, x)),
        ],
        in_specs=[vmem] * 12,
        out_specs=[vmem] * 8,
        scratch_shapes=[
            pltpu.VMEM((3, NT, x + LANES), f32),
            pltpu.VMEM((4, NT, x + LANES), f32),
            pltpu.VMEM((1, x), f32),
            pltpu.VMEM((11, 2, NT, LANES), f32),
        ],
        compiler_params=params,
        name="join",
    )(m, d, si, sc, mask, g, bg, bd, b2d, sums, *first)
    g_end, bg_end, bd_end, b2d_end, sums, eps, res, mask_up = in_vmem(out)

    b2g_end, moments = pl.pallas_call(
        functools.partial(close_kernel, n, x),
        out_shape=[ends(6), jax.ShapeDtypeStruct((24, LANES), f32)],
        in_specs=[vmem] * 16,
        out_specs=[vmem] * 2,
        scratch_shapes=[
            pltpu.VMEM((3, NT, x + LANES), f32),
            pltpu.VMEM((7, 2, NT, LANES), f32),
            pltpu.VMEM((N_MOMENTS, NT, LANES), f32),
        ],
        compiler_params=params,
        name="close",
    )(si, sc, mask, bg, b2g, b2d, bg_end, b2d_end, sums, eps, res, mask_up, *first, *late)

    reach = 1
    while reach < peers:
        moments = moments + lax.ppermute(moments, "inline", [(i, i ^ reach) for i in range(peers)])
        reach *= 2

    return pl.pallas_call(
        functools.partial(last_kernel, n, x),
        out_shape=[jax.ShapeDtypeStruct((n, NT, x), f32)] * 2,
        in_specs=[vmem] * 13,
        out_specs=[hbm] * 2,
        scratch_shapes=[
            pltpu.VMEM((n, NT, x), f32),
            pltpu.VMEM((n, NT, x), f32),
            pltpu.SemaphoreType.DMA((2 * n,)),
        ],
        compiler_params=params,
        name="last",
    )(
        moments, m, d, g, bg, b2g, bd, b2d, g_end, bg_end, *in_vmem([b2g_end]), bd_end, b2d_end)


def solution(mesh):
    rows = P(("groups", "inline"), None, None)
    return jax.shard_map(
        on_device,
        mesh=mesh,
        in_specs=(rows, P(("groups", "inline"), None), rows, rows, rows, rows),
        out_specs=(rows, rows),
        check_vma=False,
    )
```

```python
import functools

import jax
import jax.numpy as jnp
from jax import lax
from jax.experimental import pallas as pl
from jax.experimental.pallas import tpu as pltpu
from jax.sharding import PartitionSpec as P

ITERS = 3
NT = 8
LANES = 128
CHUNK = 4096
SHIFT = 18.0
M0, D0, SI0, FIRST0 = range(4)
SC0, G0, BD0, BG0, B2D0, B2G0, LATE0 = range(7)
WM1, WD1, SI1, G1, BD1, BG1, DOWN1 = range(7)
N_MOMENTS = 18
VMEM_LIMIT = 16 * 1024 * 1024

f32 = jnp.float32


def time_ahead(v):
    rolled = pltpu.roll(v, NT - 1, 0)
    return jnp.where(lax.broadcasted_iota(jnp.int32, v.shape, 0) == NT - 1, 0.0, rolled)


def time_behind(v):
    rolled = pltpu.roll(v, 1, 0)
    return jnp.where(lax.broadcasted_iota(jnp.int32, v.shape, 0) == 0, 0.0, rolled)


def sum_diff(v):
    ahead = time_ahead(v)
    return ahead + v, ahead - v


def head(pair, width):
    return pair[0][:, :width], pair[1][:, :width]


def inline_res(here, after, slope):
    return (after[0] - here[0]) + slope * (after[1] + here[1])


def parts(res, slope):
    scaled = slope * res
    return res - scaled, res + scaled


def to_next(ef):
    return ef[0] + time_behind(ef[1])


def to_self(ef):
    return -(ef[1] + time_behind(ef[0]))


def lane_ahead(v):
    width = v.shape[1]
    return pltpu.roll(v, width - 1, 1)[:, : width - LANES]


def lane_behind(before, v):
    joined = jnp.concatenate([before, v], axis=1)
    return pltpu.roll(joined, 1, 1)[:, LANES:]


def cross_res(sd, slope):
    width = sd[0].shape[1] - LANES
    here = head(sd, width)
    return (lane_ahead(sd[0]) - here[0]) + slope * (lane_ahead(sd[1]) + here[1])


def cross_terms(sd, slope, carry, slot):
    e, f = parts(cross_res(sd, slope), slope)
    e_behind = lane_behind(carry[slot, 0], e)
    f_behind = lane_behind(carry[slot, 1], f)
    carry[slot, 0] = e[:, -LANES:]
    carry[slot, 1] = f[:, -LANES:]
    return e_behind - f, f_behind - e


def stencil(load, slope_in, slope_cr, lo, hi, res_lo, res_hi, carry, slot, scale_lo=None):
    out = {}
    sd = {}

    def pair(i):
        if i not in sd:
            sd[i] = sum_diff(load(i))
        return sd[i]

    before = None
    for i in range(lo - 1, hi + 1):
        here = None
        if res_lo <= i <= res_hi:
            first = pair(i)
            second = pair(i + 1)
            width = first[0].shape[1] - LANES
            slope = slope_in(i)
            res = inline_res(head(first, width), head(second, width), slope)
            if i == -1 and scale_lo is not None:
                res = res * scale_lo
            here = parts(res, slope)
        if i >= lo:
            same, later = cross_terms(pair(i), slope_cr(i), carry, slot + i - lo)
            if before is not None:
                same = same + before[0]
                later = later + before[1]
            if here is not None:
                same = same - here[1]
                later = later - here[0]
            out[i] = same + time_behind(later)
        before = here
    return out


class Mended:
    def __init__(self, n, low, high, whole, ends, before=None, after=None):
        self.n, self.low, self.high, self.whole, self.ends, self.before, self.after = n, low, high, whole, ends, before, after

    def at(self, i):
        if i < 0:
            return self.before
        if i >= self.n:
            return self.after
        if i < self.low:
            return self.ends, i
        if i >= self.n - self.high:
            return self.ends, self.low + i - self.n + self.high
        return self.whole, i + 1

    def load(self, i, lanes):
        ref, row = self.at(i)
        return ref[row, :, lanes]

    def store(self, i, lanes, value):
        ref, row = self.at(i)
        ref[row, :, lanes] = value


def chunks(x):
    return x // CHUNK


def at_chunk(c):
    return pl.multiple_of(c * CHUNK, CHUNK)


class Own:
    def __init__(self, n, x0, si_ref, sc_ref, mask_ref, carry):
        self.n, self.x0, self.here = n, x0, pl.ds(x0, CHUNK)
        self.si_ref, self.sc_ref, self.mask_ref, self.carry = si_ref, sc_ref, mask_ref, carry

    def known4(self, i):
        return self.mask_ref[pl.ds(i, 1), self.here].astype(f32) * 4.0

    def level(self, src, lo, hi, slot):
        return stencil(
            lambda i: src[i + 1, :, pl.ds(self.x0, CHUNK + LANES)],
            lambda i: self.si_ref[i + 1, :, self.here],
            lambda i: self.sc_ref[i, :, self.here],
            lo, hi, 0, self.n - 2, self.carry, slot,
        )

    def applied(self, src, lo, hi, slot):
        out = self.level(src, lo, hi, slot)
        return {i: (self.known4(i) - SHIFT) * src[i + 1, :, self.here] + out[i] for i in out}

    def gradient(self, data_ref, m_ref, lo, hi, slot):
        out = self.level(m_ref, lo, hi, slot)
        return {i: self.known4(i) * (data_ref[i, :, self.here] - m_ref[i + 1, :, self.here]) - out[i] for i in out}


def put(ref, slot, x, x0, value):
    ref[:, pl.ds(pl.multiple_of(x0 + slot * x, CHUNK), CHUNK)] = value


def pack_kernel(n, x, si_hbm, model_hbm, dir_hbm, up_ref, sems):
    copies = [
        pltpu.make_async_copy(source.at[0], up_ref.at[:, pl.ds(slot * x, x)], sems.at[slot])
        for source, slot in ((model_hbm, M0), (dir_hbm, D0), (si_hbm, SI0))
    ]
    for copy in copies:
        copy.start()
    for copy in copies:
        copy.wait()


def first_kernel(
    n, x,
    data_hbm, mask_hbm, si_hbm, sc_hbm, model_hbm, dir_hbm,
    data_ref, mask_ref, si_ref, sc_ref, m_ref, d_ref, up_ref,
    g_ref, bg_ref, bd_ref, carry, sems,
):
    body = (pl.ds(1, n), slice(None), pl.ds(0, x))
    copies = [
        pltpu.make_async_copy(source, target, sems.at[k])
        for k, (source, target) in enumerate((
            (model_hbm, m_ref.at[body]), (dir_hbm, d_ref.at[body]), (si_hbm, si_ref.at[pl.ds(1, n)]), (sc_hbm, sc_ref),
            (mask_hbm, mask_ref), (data_hbm, data_ref),
        ))
    ]
    for copy in copies:
        copy.start()
    clear_pads(x, (m_ref, d_ref, g_ref, bg_ref, bd_ref))
    carry[...] = jnp.zeros(carry.shape, f32)
    for copy in copies:
        copy.wait()
    share = x // NT
    for s in range(NT):
        up_ref[pl.ds(s, 1), pl.ds(LATE0 * x, share)] = mask_ref[pl.ds(0, 1), pl.ds(s * share, share)].astype(f32)

    def first(c, _):
        x0 = at_chunk(c)
        own = Own(n, x0, si_ref, sc_ref, mask_ref, carry)
        put(up_ref, SC0, x, x0, sc_ref[0, :, own.here])
        out = own.gradient(data_ref, m_ref, 0, 2, 0)
        put(up_ref, G0, x, x0, out[0])
        for i, value in out.items():
            g_ref[i + 1, :, own.here] = value
        out = own.applied(d_ref, 0, 1, 3)
        put(up_ref, BD0, x, x0, out[0])
        for i, value in out.items():
            bd_ref[i + 1, :, own.here] = value
        return 0

    lax.fori_loop(0, chunks(x), first, 0)
    carry[...] = jnp.zeros(carry.shape, f32)

    def second(c, _):
        x0 = at_chunk(c)
        own = Own(n, x0, si_ref, sc_ref, mask_ref, carry)
        out = own.applied(g_ref, 0, 1, 0)
        put(up_ref, BG0, x, x0, out[0])
        for i, value in out.items():
            bg_ref[i + 1, :, own.here] = value
        put(up_ref, B2D0, x, x0, own.applied(bd_ref, 0, 0, 2)[0])
        return 0

    lax.fori_loop(0, chunks(x), second, 0)
    carry[...] = jnp.zeros(carry.shape, f32)

    def third(c, _):
        x0 = at_chunk(c)
        put(up_ref, B2G0, x, x0, Own(n, x0, si_ref, sc_ref, mask_ref, carry).applied(bg_ref, 0, 0, 0)[0])
        return 0

    lax.fori_loop(0, chunks(x), third, 0)


def down_kernel(
    n, x, data_ref, mask_ref, si_ref, sc_ref, m_ref, d_ref, up_first,
    down_ref, eps_ref,
    g_ref, carry,
):
    clear_pads(x, (g_ref, eps_ref))
    carry[...] = jnp.zeros(carry.shape, f32)

    def first(c, _):
        x0 = at_chunk(c)
        here = pl.ds(x0, CHUNK)
        own = Own(n, x0, si_ref, sc_ref, mask_ref, carry)
        slope = si_ref[n, :, here]
        out = own.gradient(data_ref, m_ref, n - 2, n - 1, 0)
        ef = parts(inline_res(sum_diff(m_ref[n, :, here]), sum_diff(row_of(up_first, M0, x, x0)), slope), slope)
        g_ref[n - 1, :, here] = out[n - 2]
        g_ref[n, :, here] = out[n - 1] - to_self(ef)
        put(down_ref, G1, x, x0, g_ref[n, :, here])
        eps_ref[0, :, here] = -to_next(ef)
        put(down_ref, WM1, x, x0, eps_ref[0, :, here])
        ef = parts(inline_res(sum_diff(d_ref[n, :, here]), sum_diff(row_of(up_first, D0, x, x0)), slope), slope)
        put(down_ref, BD1, x, x0, own.applied(d_ref, n - 1, n - 1, 2)[n - 1] + to_self(ef))
        eps_ref[1, :, here] = to_next(ef)
        put(down_ref, WD1, x, x0, eps_ref[1, :, here])
        put(down_ref, SI1, x, x0, slope)
        return 0

    lax.fori_loop(0, chunks(x), first, 0)
    carry[...] = jnp.zeros(carry.shape, f32)

    def second(c, _):
        x0 = at_chunk(c)
        own = Own(n, x0, si_ref, sc_ref, mask_ref, carry)
        put(down_ref, BG1, x, x0, own.applied(g_ref, n - 1, n - 1, 0)[n - 1])
        return 0

    lax.fori_loop(0, chunks(x), second, 0)


def local_kernel(
    n, x, data_ref, mask_ref, si_ref, sc_ref, m_ref, d_ref, down_ref,
    g_ref, bg_ref, b2g_ref, bd_ref, b2d_ref, sums_ref, carry,
):
    clear_pads(x, (g_ref, bg_ref, b2g_ref, bd_ref, b2d_ref))
    carry[...] = jnp.zeros(carry.shape, f32)
    sums_ref[...] = jnp.zeros(sums_ref.shape, f32)

    def first(c, _):
        x0 = at_chunk(c)
        here = pl.ds(x0, CHUNK)
        own = Own(n, x0, si_ref, sc_ref, mask_ref, carry)
        for i, value in own.gradient(data_ref, m_ref, 0, n - 2, 0).items():
            g_ref[i + 1, :, here] = value
        for i, value in own.applied(d_ref, 0, n - 2, n).items():
            bd_ref[i + 1, :, here] = value
        g_ref[n, :, here] = row_of(down_ref, G1, x, x0)
        bd_ref[n, :, here] = row_of(down_ref, BD1, x, x0)
        return 0

    lax.fori_loop(0, chunks(x), first, 0)
    carry[...] = jnp.zeros(carry.shape, f32)

    def second(c, _):
        x0 = at_chunk(c)
        own = Own(n, x0, si_ref, sc_ref, mask_ref, carry)
        for i, value in own.applied(g_ref, 2, n - 2, 0).items():
            bg_ref[i + 1, :, own.here] = value
        for i, value in own.applied(bd_ref, 2, n - 2, n).items():
            b2d_ref[i + 1, :, own.here] = value
        return 0

    lax.fori_loop(0, chunks(x), second, 0)
    carry[...] = jnp.zeros(carry.shape, f32)

    def third(c, _):
        x0 = at_chunk(c)
        own = Own(n, x0, si_ref, sc_ref, mask_ref, carry)
        for i, value in own.applied(bg_ref, 3, n - 3, 0).items():
            b2g_ref[i + 1, :, own.here] = value
        return 0

    lax.fori_loop(0, chunks(x), third, 0)

    def fourth(c, _):
        x0 = at_chunk(c)
        loads = [lambda i, lanes, ref=ref: ref[i + 1, :, lanes] for ref in (g_ref, bg_ref, b2g_ref, d_ref, bd_ref, b2d_ref)]
        products(n, x0, loads, mask_ref, si_ref, sc_ref, sums_ref, lambda done: done)
        return 0

    lax.fori_loop(0, chunks(x), fourth, 0)


PAIRS = ((0, 0), (0, 1), (1, 1), (1, 2), (2, 2), None, (0, 3), (0, 4), (1, 4), (1, 5), (2, 5), None,
         (3, 3), (3, 4), (4, 4), (4, 5), (5, 5), None)


class Totals:
    def __init__(self):
        self.of = {}

    def add(self, k, left, right):
        product = left * right
        acc = product[:, :LANES]
        for j in range(1, CHUNK // LANES):
            acc = acc + product[:, j * LANES:(j + 1) * LANES]
        self.of[k] = self.of[k] + acc if k in self.of else acc

    def put(self, sums):
        for k, value in self.of.items():
            sums[k] = sums[k] + value


class Pairs:
    def __init__(self, load, x0):
        self.load, self.lanes, self.of = load, pl.ds(x0, CHUNK + LANES), {}

    def at(self, i):
        if i not in self.of:
            self.of[i] = sum_diff(self.load(i, self.lanes))
        return self.of[i]

    def inline(self, i, slope):
        return inline_res(head(self.at(i), CHUNK), head(self.at(i + 1), CHUNK), slope)

    def cross(self, i, slope):
        return cross_res(self.at(i), slope)


LOW = (1, 2, 3, 0, 1, 2)
HIGH = (0, 1, 2, 0, 0, 1)


def products(n, x0, loads, mask_ref, si_ref, sc_ref, sums, take):
    here = pl.ds(x0, CHUNK)
    totals = Totals()
    pair_g, pair_d = Pairs(loads[2], x0), Pairs(loads[5], x0)

    def turn(i, *vectors):
        return take(all(LOW[v] <= i < n - HIGH[v] for v in vectors))

    for i in range(n):
        values = {}

        def row(v):
            if v not in values:
                values[v] = loads[v](i, here)
            return values[v]

        for k, which in enumerate(PAIRS):
            if which is not None and turn(i, *which):
                totals.add(k, row(which[0]), row(which[1]))
        res = {}
        for k, left, right in ((5, 2, 2), (11, 2, 5), (17, 5, 5)):
            if turn(i, left, right):
                known = mask_ref[pl.ds(i, 1), here].astype(f32) * 4.0
                totals.add(k, known * row(left), row(right))
                for v, pair in ((left, pair_g if left == 2 else pair_d), (right, pair_d if right == 5 else pair_g)):
                    if ("cross", v) not in res:
                        res["cross", v] = pair.cross(i, sc_ref[i, :, here])
                totals.add(k, res["cross", left], res["cross", right])
            if take(all(LOW[v] <= i < n - 1 - HIGH[v] for v in (left, right))):
                for v, pair in ((left, pair_g if left == 2 else pair_d), (right, pair_d if right == 5 else pair_g)):
                    if ("inline", v) not in res:
                        res["inline", v] = pair.inline(i, si_ref[i + 1, :, here])
                totals.add(k, res["inline", left], res["inline", right])
    totals.put(sums)


def place_flags():
    place = lax.axis_index("inline")
    return (place > 0).astype(f32), (place < lax.axis_size("inline") - 1).astype(f32)


def row_of(ref, slot, x, x0):
    return ref[:, pl.ds(pl.multiple_of(x0 + slot * x, CHUNK), CHUNK)]


def boundary(rows, i, slope, here, scale=None):
    res = inline_res(sum_diff(rows.load(i, here)), sum_diff(rows.load(i + 1, here)), slope)
    if scale is not None:
        res = res * scale
    return parts(res, slope)


def clear_pads(x, refs):
    for ref in refs:
        for i in range(ref.shape[0]):
            ref[i, :, pl.ds(x, LANES)] = jnp.zeros((NT, LANES), f32)


def end_rows(n, x0, src, dst, slope_before, si_ref, sc_ref, mask_ref, scale, carry, slot):
    here = pl.ds(x0, CHUNK)
    for lo, hi in ((0, dst.low - 1), (n - dst.high, n - 1)):
        out = stencil(
            lambda i: src.load(i, pl.ds(x0, CHUNK + LANES)),
            lambda i: slope_before if i == -1 else si_ref[i + 1, :, here],
            lambda i: sc_ref[i, :, here],
            lo, hi, -1, n - 1, carry, slot, scale,
        )
        for i in range(lo, hi + 1):
            known = mask_ref[pl.ds(i, 1), here].astype(f32) * 4.0
            dst.store(i, here, (known - SHIFT) * src.load(i, here) + out[i])
        slot += hi - lo + 1
    return slot


def beyond(rows_ref, row, wide, diagonal, cross, slope, carry, slot, further=None):
    here = pl.ds(wide.start, CHUNK)
    sd = sum_diff(rows_ref[row, :, wide])
    near = head(sd, CHUNK)
    same, later = cross_terms(sd, cross, carry, slot)
    if further is None:
        inner = parts(slope * near[1] - near[0], slope)
    else:
        inner = parts(inline_res(near, sum_diff(further), slope), slope)
    return diagonal * rows_ref[row, :, here] + (same - inner[1]) + time_behind(later - inner[0]), inner


def join_kernel(
    n, x,
    d_ref, si_ref, sc_ref, mask_ref, g_in, bg_in, b2g_in, bd_in, b2d_in, sums_in, eps_in,
    up_first, up_ref, down_ref,
    g_out, bg_out, b2g_out, bd_out, b2d_out, moments_ref,
    eps_ref, mask_up, ghosts, carry, sums,
):
    not_first, not_last = place_flags()
    clear_pads(x, (eps_ref, ghosts, g_out, bg_out, b2g_out, bd_out, b2d_out))
    carry[...] = jnp.zeros(carry.shape, f32)
    sums[...] = sums_in[...]
    share = x // NT
    for s in range(NT):
        mask_up[:, pl.ds(s * share, share)] = up_ref[pl.ds(s, 1), pl.ds(LATE0 * x, share)] * 4.0 - SHIFT
    g_rows, bg_rows, b2g_rows, d_rows, bd_rows, b2d_rows = (
        Mended(n, low, high, whole, ends, (ghosts, 2 * k), (ghosts, 2 * k + 1))
        for k, (low, high, whole, ends) in enumerate(zip(
            LOW, HIGH, (g_in, bg_in, b2g_in, d_ref, bd_in, b2d_in), (g_out, bg_out, b2g_out, None, bd_out, b2d_out)))
    )

    def zeroth(c, _):
        x0 = at_chunk(c)
        here = pl.ds(x0, CHUNK)
        g_rows.store(-1, here, row_of(down_ref, G1, x, x0))
        g_rows.store(0, here, g_in[1, :, here] + row_of(down_ref, WM1, x, x0))
        g_rows.store(n, here, (row_of(up_ref, G0, x, x0) + eps_in[0, :, here]) * not_last)
        bd_rows.store(-1, here, row_of(down_ref, BD1, x, x0))
        bd_rows.store(0, here, bd_in[1, :, here] + row_of(down_ref, WD1, x, x0))
        bd_rows.store(n, here, (row_of(up_ref, BD0, x, x0) + eps_in[1, :, here]) * not_last)
        return 0

    lax.fori_loop(0, chunks(x), zeroth, 0)

    def first(c, _):
        x0 = at_chunk(c)
        here = pl.ds(x0, CHUNK)
        before = row_of(down_ref, SI1, x, x0)
        slope = si_ref[n, :, here]
        slot = end_rows(n, x0, g_rows, bg_rows, before, si_ref, sc_ref, mask_ref, not_first, carry, 0)
        slot = end_rows(n, x0, bd_rows, b2d_rows, before, si_ref, sc_ref, mask_ref, not_first, carry, slot)
        wide = pl.ds(x0, CHUNK + LANES)
        slope_up, cross_up = row_of(up_first, SI0, x, x0), row_of(up_ref, SC0, x, x0)
        diagonal = mask_up[:, here]
        own, inner = beyond(eps_in, 0, wide, diagonal, cross_up, slope_up, carry, slot)
        eps = own + to_next(boundary(g_rows, n - 1, slope, here))
        eps_ref[0, :, here] = eps
        eps_ref[1, :, here] = to_next(inner)
        bg_rows.store(n, here, (row_of(up_ref, BG0, x, x0) + eps) * not_last)
        own, _ = beyond(eps_in, 1, wide, diagonal, cross_up, slope_up, carry, slot + 1)
        eps = own + to_next(boundary(bd_rows, n - 1, slope, here))
        b2d_rows.store(n, here, (row_of(up_ref, B2D0, x, x0) + eps) * not_last)
        bg_rows.store(-1, here, row_of(down_ref, BG1, x, x0) + to_self(boundary(g_rows, -1, before, here, not_first)))
        return 0

    lax.fori_loop(0, chunks(x), first, 0)
    carry[...] = jnp.zeros(carry.shape, f32)

    def second(c, _):
        x0 = at_chunk(c)
        here = pl.ds(x0, CHUNK)
        wide = pl.ds(x0, CHUNK + LANES)
        before = row_of(down_ref, SI1, x, x0)
        slot = end_rows(n, x0, bg_rows, b2g_rows, before, si_ref, sc_ref, mask_ref, not_first, carry, 0)
        own, _ = beyond(
            eps_ref, 0, wide, mask_up[:, here], row_of(up_ref, SC0, x, x0), row_of(up_first, SI0, x, x0),
            carry, slot, eps_ref[1, :, here])
        edge = to_next(boundary(bg_rows, n - 1, si_ref[n, :, here], here))
        b2g_rows.store(n, here, (row_of(up_ref, B2G0, x, x0) + own + edge) * not_last)
        return 0

    lax.fori_loop(0, chunks(x), second, 0)

    def third(c, _):
        loads = [rows.load for rows in (g_rows, bg_rows, b2g_rows, d_rows, bd_rows, b2d_rows)]
        products(n, at_chunk(c), loads, mask_ref, si_ref, sc_ref, sums, lambda done: not done)
        return 0

    lax.fori_loop(0, chunks(x), third, 0)
    for k in range(N_MOMENTS):
        moments_ref[pl.ds(k, 1), :] = jnp.sum(sums[k], axis=0, keepdims=True)
    moments_ref[pl.ds(N_MOMENTS, 24 - N_MOMENTS), :] = jnp.zeros((24 - N_MOMENTS, LANES), f32)


def add_terms(terms):
    total = None
    for term in terms:
        total = term if total is None else total + term
    return total


def solve(moments):
    mu, nu, xi = moments[:6], moments[6:12], moments[12:]

    def entry(a, b, i, j):
        if a == 0 and b == 0:
            return mu[i + j]
        if a == 1 and b == 1:
            return xi[i + j]
        return nu[i + j]

    shifted = {}

    def entry_a(a, b, i, j):
        which = a + b
        if (which, i + j) not in shifted:
            if i + j == 4:
                value = entry(a, b, 2, 3)
            else:
                value = entry(a, b, i, j + 1) + SHIFT * entry(a, b, i, j)
            shifted[which, i + j] = value * 0.25
        return shifted[which, i + j]

    def form(get, u, v):
        rows = []
        for (a, i), left in u.items():
            inner = add_terms(right * get(a, b, i, j) for (b, j), right in v.items())
            rows.append(left * inner)
        return add_terms(rows)

    def axpy(scale, u, v):
        out = dict(v)
        for key, value in u.items():
            term = scale * value
            out[key] = out[key] + term if key in out else term
        return out

    one = jnp.ones_like(mu[0])
    gradient = {(0, 0): 0.25 * one}
    direction = {(1, 0): one}
    model = {}
    for iteration in range(ITERS):
        mixing = -form(entry_a, gradient, direction) / form(entry_a, direction, direction)
        direction = axpy(mixing, direction, gradient)
        step = form(entry, gradient, direction) / form(entry_a, direction, direction)
        model = axpy(step, direction, model)
        if iteration < ITERS - 1:
            image = {key: value * (0.25 * SHIFT) for key, value in direction.items()}
            image = axpy(0.25, {(a, i + 1): value for (a, i), value in direction.items()}, image)
            gradient = axpy(-step, image, gradient)
    return model, direction


def last_kernel(
    n, x, moments_ref, m_ref, d_ref, g_in, bg_in, b2g_in, bd_in, b2d_in, g_end, bg_end, b2g_end, bd_end, b2d_end,
    model_hbm, dir_hbm, mo_ref, do_ref, sems,
):
    moments = [
        jnp.broadcast_to(jnp.sum(moments_ref[pl.ds(k, 1), :], axis=1, keepdims=True), (NT, LANES))
        for k in range(N_MOMENTS)
    ]
    model, direction = solve(moments)
    rows = [
        Mended(n, LOW[k], HIGH[k], whole, ends)
        for k, whole, ends in ((0, g_in, g_end), (1, bg_in, bg_end), (2, b2g_in, b2g_end), (4, bd_in, bd_end), (5, b2d_in, b2d_end))
    ]
    keys = ((0, 0), (0, 1), (0, 2), (1, 1), (1, 2))
    copies = []
    for i in range(n):
        def step(c, _):
            x0 = pl.multiple_of(c * LANES, LANES)
            here = pl.ds(x0, LANES)
            values = {key: vector.load(i, here) for key, vector in zip(keys, rows)}
            values[1, 0] = d_ref[i + 1, :, here]
            mo_ref[i, :, here] = m_ref[i + 1, :, here] + add_terms(
                model[key] * value for key, value in values.items())
            do_ref[i, :, here] = add_terms(direction[key] * value for key, value in values.items())
            return 0

        lax.fori_loop(0, x // LANES, step, 0, unroll=4)
        for k, (src, dst) in enumerate(((mo_ref, model_hbm), (do_ref, dir_hbm))):
            copy = pltpu.make_async_copy(src.at[i], dst.at[i], sems.at[2 * i + k])
            copy.start()
            copies.append(copy)
    for copy in copies:
        copy.wait()


def in_vmem(values):
    return [pltpu.with_memory_space_constraint(v, pltpu.VMEM) for v in values]


def kept(shape, dtype=f32):
    return pltpu.VMEM(shape, dtype)


def on_device(*args):
    n, _, x = args[0].shape
    peers = lax.axis_size("inline")
    assert peers & (peers - 1) == 0 and n >= 7 and x % CHUNK == 0
    vmem = pl.BlockSpec(memory_space=pltpu.VMEM)
    hbm = pl.BlockSpec(memory_space=pl.ANY)
    params = pltpu.CompilerParams(vmem_limit_bytes=VMEM_LIMIT)
    wide = kept((n + 2, NT, x + LANES))
    share = x // NT

    args = [pltpu.with_memory_space_constraint(v, pltpu.HBM) for v in args]

    def call(kernel, out_shape, in_specs, scratch_shapes, name):
        return pl.pallas_call(
            functools.partial(kernel, n, x),
            out_shape=out_shape,
            in_specs=in_specs,
            out_specs=[vmem] * len(out_shape),
            scratch_shapes=scratch_shapes,
            compiler_params=params,
            name=name,
        )

    def carry(slots):
        return pltpu.VMEM((slots, 2, NT, LANES), f32)

    def ends(rows):
        return kept((rows, NT, x + LANES))

    def to_before(value):
        return lax.ppermute(value, "inline", [(i, i - 1) for i in range(1, peers)])

    up_first, = call(
        pack_kernel, [kept((NT, FIRST0 * x))], [hbm] * 3, [pltpu.SemaphoreType.DMA((3,))], "pack",
    )(args[2], args[4], args[5])
    up_first = to_before(up_first)

    *loaded, up = call(
        first_kernel,
        [kept((n, NT, x)), kept((n, x), jnp.int32), kept((n + 2, NT, x)), kept((n, NT, x)), wide, wide,
         kept((NT, LATE0 * x + share))],
        [hbm] * 6,
        [pltpu.VMEM((4, NT, x + LANES), f32)] * 3 + [carry(5), pltpu.SemaphoreType.DMA((6,))], "first",
    )(*args)
    loaded = in_vmem(loaded)
    _, mask, si, sc, m, d = loaded
    up = to_before(up)

    down, eps = call(
        down_kernel, [kept((NT, DOWN1 * x)), ends(2)], [vmem] * 7,
        [pltpu.VMEM((n + 2, NT, x + LANES), f32), carry(3)], "down",
    )(*loaded, up_first)
    received = lax.ppermute(down, "inline", [(i, i + 1) for i in range(peers - 1)])

    made = call(
        local_kernel, [wide, wide, wide, wide, wide, kept((N_MOMENTS, NT, LANES))], [vmem] * 7,
        [carry(2 * n)], "local",
    )(*loaded, down)
    g, bg, b2g, bd, b2d, sums = in_vmem(made)

    out = call(
        join_kernel,
        [ends(LOW[k] + HIGH[k]) for k in (0, 1, 2, 4, 5)] + [jax.ShapeDtypeStruct((24, LANES), f32)], [vmem] * 14,
        [pltpu.VMEM((2, NT, x + LANES), f32), pltpu.VMEM((1, x), f32), pltpu.VMEM((12, NT, x + LANES), f32), carry(8),
         pltpu.VMEM((N_MOMENTS, NT, LANES), f32)], "join",
    )(d, si, sc, mask, g, bg, b2g, bd, b2d, sums, eps, up_first, up, received)
    moments = out[5]

    reach = 1
    while reach < peers:
        span = min(4, peers // reach)
        others = [lax.ppermute(moments, "inline", [(i, i ^ (k * reach)) for i in range(peers)]) for k in range(1, span)]
        moments = moments + add_terms(others)
        reach *= span

    return pl.pallas_call(
        functools.partial(last_kernel, n, x),
        out_shape=[jax.ShapeDtypeStruct((n, NT, x), f32)] * 2,
        in_specs=[vmem] * 13,
        out_specs=[hbm] * 2,
        scratch_shapes=[
            pltpu.VMEM((n, NT, x), f32),
            pltpu.VMEM((n, NT, x), f32),
            pltpu.SemaphoreType.DMA((2 * n,)),
        ],
        compiler_params=params,
        name="last",
    )(
        moments, m, d, g, bg, b2g, bd, b2d, *in_vmem(out[:5]))


def solution(mesh):
    rows = P(("groups", "inline"), None, None)
    return jax.shard_map(
        on_device,
        mesh=mesh,
        in_specs=(rows, P(("groups", "inline"), None), rows, rows, rows, rows),
        out_specs=(rows, rows),
        check_vma=False,
    )
```

```python
import functools

import jax
import jax.numpy as jnp
from jax import lax
from jax.experimental import pallas as pl
from jax.experimental.pallas import tpu as pltpu
from jax.sharding import PartitionSpec as P

ITERS = 3
NT = 8
LANES = 128
CHUNK = 4096
SHIFT = 18.0
M0, D0, SI0, SC0, FIRST0 = range(5)
G0, BD0, BG0, B2D0, B2G0, LATE0 = range(6)
WM1, WD1, G1, BD1, BG1, DOWN1 = range(6)
N_MOMENTS = 18
VMEM_LIMIT = 16 * 1024 * 1024

f32 = jnp.float32


def time_ahead(v):
    rolled = pltpu.roll(v, NT - 1, 0)
    return jnp.where(lax.broadcasted_iota(jnp.int32, v.shape, 0) == NT - 1, 0.0, rolled)


def time_behind(v):
    rolled = pltpu.roll(v, 1, 0)
    return jnp.where(lax.broadcasted_iota(jnp.int32, v.shape, 0) == 0, 0.0, rolled)


def sum_diff(v):
    ahead = time_ahead(v)
    return ahead + v, ahead - v


def head(pair, width):
    return pair[0][:, :width], pair[1][:, :width]


def inline_res(here, after, slope):
    return (after[0] - here[0]) + slope * (after[1] + here[1])


def parts(res, slope):
    scaled = slope * res
    return res - scaled, res + scaled


def to_next(ef):
    return ef[0] + time_behind(ef[1])


def to_self(ef):
    return -(ef[1] + time_behind(ef[0]))


def lane_ahead(v):
    width = v.shape[1]
    return pltpu.roll(v, width - 1, 1)[:, : width - LANES]


def lane_behind(before, v):
    joined = jnp.concatenate([before, v], axis=1)
    return pltpu.roll(joined, 1, 1)[:, LANES:]


def cross_res(sd, slope):
    width = sd[0].shape[1] - LANES
    here = head(sd, width)
    return (lane_ahead(sd[0]) - here[0]) + slope * (lane_ahead(sd[1]) + here[1])


def cross_terms(sd, slope, carry, slot):
    e, f = parts(cross_res(sd, slope), slope)
    e_behind = lane_behind(carry[slot, 0], e)
    f_behind = lane_behind(carry[slot, 1], f)
    carry[slot, 0] = e[:, -LANES:]
    carry[slot, 1] = f[:, -LANES:]
    return e_behind - f, f_behind - e


def stencil(load, slope_in, slope_cr, lo, hi, res_lo, res_hi, carry, slot, scale_lo=None):
    out = {}
    sd = {}

    def pair(i):
        if i not in sd:
            sd[i] = sum_diff(load(i))
        return sd[i]

    before = None
    for i in range(lo - 1, hi + 1):
        here = None
        if res_lo <= i <= res_hi:
            first = pair(i)
            second = pair(i + 1)
            width = first[0].shape[1] - LANES
            slope = slope_in(i)
            res = inline_res(head(first, width), head(second, width), slope)
            if i == -1 and scale_lo is not None:
                res = res * scale_lo
            here = parts(res, slope)
        if i >= lo:
            same, later = cross_terms(pair(i), slope_cr(i), carry, slot + i - lo)
            if before is not None:
                same = same + before[0]
                later = later + before[1]
            if here is not None:
                same = same - here[1]
                later = later - here[0]
            out[i] = same + time_behind(later)
        before = here
    return out


class Mended:
    def __init__(self, n, low, high, whole, ends, before=None, after=None):
        self.n, self.low, self.high, self.whole, self.ends, self.before, self.after = n, low, high, whole, ends, before, after

    def at(self, i):
        if i < 0:
            return self.before
        if i >= self.n:
            return self.after
        if i < self.low:
            return self.ends, i
        if i >= self.n - self.high:
            return self.ends, self.low + i - self.n + self.high
        return self.whole, i + 1

    def load(self, i, lanes):
        ref, row = self.at(i)
        return ref[row, :, lanes]

    def store(self, i, lanes, value):
        ref, row = self.at(i)
        ref[row, :, lanes] = value


def chunks(x):
    return x // CHUNK


def at_chunk(c):
    return pl.multiple_of(c * CHUNK, CHUNK)


class Own:
    def __init__(self, n, x0, si_ref, sc_ref, mask_ref, carry):
        self.n, self.x0, self.here = n, x0, pl.ds(x0, CHUNK)
        self.si_ref, self.sc_ref, self.mask_ref, self.carry = si_ref, sc_ref, mask_ref, carry

    def known4(self, i):
        return self.mask_ref[pl.ds(i, 1), self.here].astype(f32) * 4.0

    def level(self, src, lo, hi, slot):
        return stencil(
            lambda i: src[i + 1, :, pl.ds(self.x0, CHUNK + LANES)],
            lambda i: self.si_ref[i + 1, :, self.here],
            lambda i: self.sc_ref[i, :, self.here],
            lo, hi, 0, self.n - 2, self.carry, slot,
        )

    def applied(self, src, lo, hi, slot):
        out = self.level(src, lo, hi, slot)
        return {i: (self.known4(i) - SHIFT) * src[i + 1, :, self.here] + out[i] for i in out}

    def gradient(self, data_ref, m_ref, lo, hi, slot):
        out = self.level(m_ref, lo, hi, slot)
        return {i: self.known4(i) * (data_ref[i, :, self.here] - m_ref[i + 1, :, self.here]) - out[i] for i in out}


def put(ref, slot, x, x0, value):
    ref[:, pl.ds(pl.multiple_of(x0 + slot * x, CHUNK), CHUNK)] = value


def pack_kernel(n, x, si_hbm, sc_hbm, model_hbm, dir_hbm, up_ref, sems):
    copies = [
        pltpu.make_async_copy(source.at[0], up_ref.at[:, pl.ds(slot * x, x)], sems.at[slot])
        for source, slot in ((model_hbm, M0), (dir_hbm, D0), (si_hbm, SI0), (sc_hbm, SC0))
    ]
    for copy in copies:
        copy.start()
    for copy in copies:
        copy.wait()


def first_kernel(
    n, x,
    data_hbm, mask_hbm, si_hbm, sc_hbm, model_hbm, dir_hbm,
    data_ref, mask_ref, si_ref, sc_ref, m_ref, d_ref, up_ref, slope_ref,
    g_ref, bg_ref, bd_ref, carry, sems,
):
    lanes = pl.ds(0, x)
    copies = [pltpu.make_async_copy(mask_hbm, mask_ref, sems.at[0])]
    for top in (True, False):
        for source, target, skip in (
            (model_hbm, m_ref, 1), (si_hbm, si_ref, 1), (sc_hbm, sc_ref, 0), (data_hbm, data_ref, 0), (dir_hbm, d_ref, 1),
        ):
            start, size = (0, 4) if top else (4, n - 4)
            copies.append(pltpu.make_async_copy(
                source.at[pl.ds(start, size)], target.at[pl.ds(start + skip, size), :, lanes], sems.at[len(copies)]))
    for copy in copies:
        copy.start()
    clear_pads(x, (m_ref, d_ref, g_ref, bg_ref, bd_ref))
    carry[...] = jnp.zeros(carry.shape, f32)
    for copy in copies[:6]:
        copy.wait()
    share = x // NT
    for s in range(NT):
        up_ref[pl.ds(s, 1), pl.ds(LATE0 * x, share)] = mask_ref[pl.ds(0, 1), pl.ds(s * share, share)].astype(f32)

    def first(c, _):
        x0 = at_chunk(c)
        own = Own(n, x0, si_ref, sc_ref, mask_ref, carry)
        out = own.gradient(data_ref, m_ref, 0, 2, 0)
        put(up_ref, G0, x, x0, out[0])
        for i, value in out.items():
            g_ref[i + 1, :, own.here] = value
        out = own.applied(d_ref, 0, 1, 3)
        put(up_ref, BD0, x, x0, out[0])
        for i, value in out.items():
            bd_ref[i + 1, :, own.here] = value
        return 0

    lax.fori_loop(0, chunks(x), first, 0)
    carry[...] = jnp.zeros(carry.shape, f32)

    def second(c, _):
        x0 = at_chunk(c)
        own = Own(n, x0, si_ref, sc_ref, mask_ref, carry)
        out = own.applied(g_ref, 0, 1, 0)
        put(up_ref, BG0, x, x0, out[0])
        for i, value in out.items():
            bg_ref[i + 1, :, own.here] = value
        put(up_ref, B2D0, x, x0, own.applied(bd_ref, 0, 0, 2)[0])
        return 0

    lax.fori_loop(0, chunks(x), second, 0)
    carry[...] = jnp.zeros(carry.shape, f32)

    def third(c, _):
        x0 = at_chunk(c)
        put(up_ref, B2G0, x, x0, Own(n, x0, si_ref, sc_ref, mask_ref, carry).applied(bg_ref, 0, 0, 0)[0])
        return 0

    lax.fori_loop(0, chunks(x), third, 0)
    for copy in copies[6:]:
        copy.wait()
    slope_ref[...] = si_ref[n, :, lanes]


def down_kernel(
    n, x, data_ref, mask_ref, si_ref, sc_ref, m_ref, d_ref, up_first,
    down_ref, eps_ref,
    g_ref, carry,
):
    clear_pads(x, (g_ref, eps_ref))
    carry[...] = jnp.zeros(carry.shape, f32)

    def first(c, _):
        x0 = at_chunk(c)
        here = pl.ds(x0, CHUNK)
        own = Own(n, x0, si_ref, sc_ref, mask_ref, carry)
        slope = si_ref[n, :, here]
        out = own.gradient(data_ref, m_ref, n - 2, n - 1, 0)
        ef = parts(inline_res(sum_diff(m_ref[n, :, here]), sum_diff(row_of(up_first, M0, x, x0)), slope), slope)
        g_ref[n - 1, :, here] = out[n - 2]
        g_ref[n, :, here] = out[n - 1] - to_self(ef)
        put(down_ref, G1, x, x0, g_ref[n, :, here])
        eps_ref[0, :, here] = -to_next(ef)
        put(down_ref, WM1, x, x0, eps_ref[0, :, here])
        ef = parts(inline_res(sum_diff(d_ref[n, :, here]), sum_diff(row_of(up_first, D0, x, x0)), slope), slope)
        put(down_ref, BD1, x, x0, own.applied(d_ref, n - 1, n - 1, 2)[n - 1] + to_self(ef))
        eps_ref[1, :, here] = to_next(ef)
        put(down_ref, WD1, x, x0, eps_ref[1, :, here])
        return 0

    lax.fori_loop(0, chunks(x), first, 0)
    carry[...] = jnp.zeros(carry.shape, f32)

    def second(c, _):
        x0 = at_chunk(c)
        own = Own(n, x0, si_ref, sc_ref, mask_ref, carry)
        put(down_ref, BG1, x, x0, own.applied(g_ref, n - 1, n - 1, 0)[n - 1])
        return 0

    lax.fori_loop(0, chunks(x), second, 0)


def local_kernel(
    n, x, data_ref, mask_ref, si_ref, sc_ref, m_ref, d_ref, down_ref,
    g_ref, bg_ref, b2g_ref, bd_ref, b2d_ref, sums_ref, carry,
):
    clear_pads(x, (g_ref, bg_ref, b2g_ref, bd_ref, b2d_ref))
    carry[...] = jnp.zeros(carry.shape, f32)
    sums_ref[...] = jnp.zeros(sums_ref.shape, f32)

    def first(c, _):
        x0 = at_chunk(c)
        here = pl.ds(x0, CHUNK)
        own = Own(n, x0, si_ref, sc_ref, mask_ref, carry)
        for i, value in own.gradient(data_ref, m_ref, 0, n - 2, 0).items():
            g_ref[i + 1, :, here] = value
        for i, value in own.applied(d_ref, 0, n - 2, n).items():
            bd_ref[i + 1, :, here] = value
        g_ref[n, :, here] = row_of(down_ref, G1, x, x0)
        bd_ref[n, :, here] = row_of(down_ref, BD1, x, x0)
        return 0

    lax.fori_loop(0, chunks(x), first, 0)
    carry[...] = jnp.zeros(carry.shape, f32)

    def second(c, _):
        x0 = at_chunk(c)
        own = Own(n, x0, si_ref, sc_ref, mask_ref, carry)
        for i, value in own.applied(g_ref, 2, n - 2, 0).items():
            bg_ref[i + 1, :, own.here] = value
        for i, value in own.applied(bd_ref, 2, n - 2, n).items():
            b2d_ref[i + 1, :, own.here] = value
        return 0

    lax.fori_loop(0, chunks(x), second, 0)
    carry[...] = jnp.zeros(carry.shape, f32)

    def third(c, _):
        x0 = at_chunk(c)
        own = Own(n, x0, si_ref, sc_ref, mask_ref, carry)
        for i, value in own.applied(bg_ref, 3, n - 3, 0).items():
            b2g_ref[i + 1, :, own.here] = value
        return 0

    lax.fori_loop(0, chunks(x), third, 0)

    def fourth(c, _):
        x0 = at_chunk(c)
        loads = [lambda i, lanes, ref=ref: ref[i + 1, :, lanes] for ref in (g_ref, bg_ref, b2g_ref, d_ref, bd_ref, b2d_ref)]
        products(n, x0, loads, mask_ref, si_ref, sc_ref, sums_ref, lambda done: done)
        return 0

    lax.fori_loop(0, chunks(x), fourth, 0)


PAIRS = ((0, 0), (0, 1), (1, 1), (1, 2), (2, 2), None, (0, 3), (0, 4), (1, 4), (1, 5), (2, 5), None,
         (3, 3), (3, 4), (4, 4), (4, 5), (5, 5), None)


class Totals:
    def __init__(self):
        self.of = {}

    def add(self, k, left, right):
        product = left * right
        acc = product[:, :LANES]
        for j in range(1, CHUNK // LANES):
            acc = acc + product[:, j * LANES:(j + 1) * LANES]
        self.of[k] = self.of[k] + acc if k in self.of else acc

    def put(self, sums):
        for k, value in self.of.items():
            sums[k] = sums[k] + value


class Pairs:
    def __init__(self, load, x0):
        self.load, self.lanes, self.of = load, pl.ds(x0, CHUNK + LANES), {}

    def at(self, i):
        if i not in self.of:
            self.of[i] = sum_diff(self.load(i, self.lanes))
        return self.of[i]

    def inline(self, i, slope):
        return inline_res(head(self.at(i), CHUNK), head(self.at(i + 1), CHUNK), slope)

    def cross(self, i, slope):
        return cross_res(self.at(i), slope)


LOW = (1, 2, 3, 0, 1, 2)
HIGH = (0, 1, 2, 0, 0, 1)


def products(n, x0, loads, mask_ref, si_ref, sc_ref, sums, take):
    here = pl.ds(x0, CHUNK)
    totals = Totals()
    pair_g, pair_d = Pairs(loads[2], x0), Pairs(loads[5], x0)

    def turn(i, *vectors):
        return take(all(LOW[v] <= i < n - HIGH[v] for v in vectors))

    for i in range(n):
        values = {}

        def row(v):
            if v not in values:
                values[v] = loads[v](i, here)
            return values[v]

        for k, which in enumerate(PAIRS):
            if which is not None and turn(i, *which):
                totals.add(k, row(which[0]), row(which[1]))
        res = {}
        for k, left, right in ((5, 2, 2), (11, 2, 5), (17, 5, 5)):
            if turn(i, left, right):
                known = mask_ref[pl.ds(i, 1), here].astype(f32) * 4.0
                totals.add(k, known * row(left), row(right))
                for v, pair in ((left, pair_g if left == 2 else pair_d), (right, pair_d if right == 5 else pair_g)):
                    if ("cross", v) not in res:
                        res["cross", v] = pair.cross(i, sc_ref[i, :, here])
                totals.add(k, res["cross", left], res["cross", right])
            if take(all(LOW[v] <= i < n - 1 - HIGH[v] for v in (left, right))):
                for v, pair in ((left, pair_g if left == 2 else pair_d), (right, pair_d if right == 5 else pair_g)):
                    if ("inline", v) not in res:
                        res["inline", v] = pair.inline(i, si_ref[i + 1, :, here])
                totals.add(k, res["inline", left], res["inline", right])
    totals.put(sums)


def place_flags():
    place = lax.axis_index("inline")
    return (place > 0).astype(f32), (place < lax.axis_size("inline") - 1).astype(f32)


def row_of(ref, slot, x, x0):
    return ref[:, pl.ds(pl.multiple_of(x0 + slot * x, CHUNK), CHUNK)]


def boundary(rows, i, slope, here, scale=None):
    res = inline_res(sum_diff(rows.load(i, here)), sum_diff(rows.load(i + 1, here)), slope)
    if scale is not None:
        res = res * scale
    return parts(res, slope)


def clear_pads(x, refs):
    for ref in refs:
        for i in range(ref.shape[0]):
            ref[i, :, pl.ds(x, LANES)] = jnp.zeros((NT, LANES), f32)


def end_rows(n, x0, src, dst, slope_before, si_ref, sc_ref, mask_ref, scale, carry, slot):
    here = pl.ds(x0, CHUNK)
    for lo, hi in ((0, dst.low - 1), (n - dst.high, n - 1)):
        out = stencil(
            lambda i: src.load(i, pl.ds(x0, CHUNK + LANES)),
            lambda i: slope_before if i == -1 else si_ref[i + 1, :, here],
            lambda i: sc_ref[i, :, here],
            lo, hi, -1, n - 1, carry, slot, scale,
        )
        for i in range(lo, hi + 1):
            known = mask_ref[pl.ds(i, 1), here].astype(f32) * 4.0
            dst.store(i, here, (known - SHIFT) * src.load(i, here) + out[i])
        slot += hi - lo + 1
    return slot


def beyond(rows_ref, row, wide, diagonal, cross, slope, carry, slot, further=None):
    here = pl.ds(wide.start, CHUNK)
    sd = sum_diff(rows_ref[row, :, wide])
    near = head(sd, CHUNK)
    same, later = cross_terms(sd, cross, carry, slot)
    if further is None:
        inner = parts(slope * near[1] - near[0], slope)
    else:
        inner = parts(inline_res(near, sum_diff(further), slope), slope)
    return diagonal * rows_ref[row, :, here] + (same - inner[1]) + time_behind(later - inner[0]), inner


def join_kernel(
    n, x,
    d_ref, si_ref, sc_ref, mask_ref, g_in, bg_in, b2g_in, bd_in, b2d_in, sums_in, eps_in,
    up_first, up_ref, slope_ref, down_ref,
    g_out, bg_out, b2g_out, bd_out, b2d_out, moments_ref,
    eps_ref, mask_up, ghosts, carry, sums,
):
    not_first, not_last = place_flags()
    clear_pads(x, (eps_ref, ghosts, g_out, bg_out, b2g_out, bd_out, b2d_out))
    carry[...] = jnp.zeros(carry.shape, f32)
    sums[...] = sums_in[...]
    share = x // NT
    for s in range(NT):
        mask_up[:, pl.ds(s * share, share)] = up_ref[pl.ds(s, 1), pl.ds(LATE0 * x, share)] * 4.0 - SHIFT
    g_rows, bg_rows, b2g_rows, d_rows, bd_rows, b2d_rows = (
        Mended(n, low, high, whole, ends, (ghosts, 2 * k), (ghosts, 2 * k + 1))
        for k, (low, high, whole, ends) in enumerate(zip(
            LOW, HIGH, (g_in, bg_in, b2g_in, d_ref, bd_in, b2d_in), (g_out, bg_out, b2g_out, None, bd_out, b2d_out)))
    )

    def zeroth(c, _):
        x0 = at_chunk(c)
        here = pl.ds(x0, CHUNK)
        g_rows.store(-1, here, row_of(down_ref, G1, x, x0))
        g_rows.store(0, here, g_in[1, :, here] + row_of(down_ref, WM1, x, x0))
        g_rows.store(n, here, (row_of(up_ref, G0, x, x0) + eps_in[0, :, here]) * not_last)
        bd_rows.store(-1, here, row_of(down_ref, BD1, x, x0))
        bd_rows.store(0, here, bd_in[1, :, here] + row_of(down_ref, WD1, x, x0))
        bd_rows.store(n, here, (row_of(up_ref, BD0, x, x0) + eps_in[1, :, here]) * not_last)
        return 0

    lax.fori_loop(0, chunks(x), zeroth, 0)

    def first(c, _):
        x0 = at_chunk(c)
        here = pl.ds(x0, CHUNK)
        before = slope_ref[:, here]
        slope = si_ref[n, :, here]
        slot = end_rows(n, x0, g_rows, bg_rows, before, si_ref, sc_ref, mask_ref, not_first, carry, 0)
        slot = end_rows(n, x0, bd_rows, b2d_rows, before, si_ref, sc_ref, mask_ref, not_first, carry, slot)
        wide = pl.ds(x0, CHUNK + LANES)
        slope_up, cross_up = row_of(up_first, SI0, x, x0), row_of(up_first, SC0, x, x0)
        diagonal = mask_up[:, here]
        own, inner = beyond(eps_in, 0, wide, diagonal, cross_up, slope_up, carry, slot)
        eps = own + to_next(boundary(g_rows, n - 1, slope, here))
        eps_ref[0, :, here] = eps
        eps_ref[1, :, here] = to_next(inner)
        bg_rows.store(n, here, (row_of(up_ref, BG0, x, x0) + eps) * not_last)
        own, _ = beyond(eps_in, 1, wide, diagonal, cross_up, slope_up, carry, slot + 1)
        eps = own + to_next(boundary(bd_rows, n - 1, slope, here))
        b2d_rows.store(n, here, (row_of(up_ref, B2D0, x, x0) + eps) * not_last)
        bg_rows.store(-1, here, row_of(down_ref, BG1, x, x0) + to_self(boundary(g_rows, -1, before, here, not_first)))
        return 0

    lax.fori_loop(0, chunks(x), first, 0)
    carry[...] = jnp.zeros(carry.shape, f32)

    def second(c, _):
        x0 = at_chunk(c)
        here = pl.ds(x0, CHUNK)
        wide = pl.ds(x0, CHUNK + LANES)
        before = slope_ref[:, here]
        slot = end_rows(n, x0, bg_rows, b2g_rows, before, si_ref, sc_ref, mask_ref, not_first, carry, 0)
        own, _ = beyond(
            eps_ref, 0, wide, mask_up[:, here], row_of(up_first, SC0, x, x0), row_of(up_first, SI0, x, x0),
            carry, slot, eps_ref[1, :, here])
        edge = to_next(boundary(bg_rows, n - 1, si_ref[n, :, here], here))
        b2g_rows.store(n, here, (row_of(up_ref, B2G0, x, x0) + own + edge) * not_last)
        return 0

    lax.fori_loop(0, chunks(x), second, 0)

    def third(c, _):
        loads = [rows.load for rows in (g_rows, bg_rows, b2g_rows, d_rows, bd_rows, b2d_rows)]
        products(n, at_chunk(c), loads, mask_ref, si_ref, sc_ref, sums, lambda done: not done)
        return 0

    lax.fori_loop(0, chunks(x), third, 0)
    for k in range(N_MOMENTS):
        moments_ref[pl.ds(k, 1), :] = jnp.sum(sums[k], axis=0, keepdims=True)
    moments_ref[pl.ds(N_MOMENTS, 24 - N_MOMENTS), :] = jnp.zeros((24 - N_MOMENTS, LANES), f32)


def add_terms(terms):
    total = None
    for term in terms:
        total = term if total is None else total + term
    return total


def solve(moments):
    mu, nu, xi = moments[:6], moments[6:12], moments[12:]

    def entry(a, b, i, j):
        if a == 0 and b == 0:
            return mu[i + j]
        if a == 1 and b == 1:
            return xi[i + j]
        return nu[i + j]

    shifted = {}

    def entry_a(a, b, i, j):
        which = a + b
        if (which, i + j) not in shifted:
            if i + j == 4:
                value = entry(a, b, 2, 3)
            else:
                value = entry(a, b, i, j + 1) + SHIFT * entry(a, b, i, j)
            shifted[which, i + j] = value * 0.25
        return shifted[which, i + j]

    def form(get, u, v):
        rows = []
        for (a, i), left in u.items():
            inner = add_terms(right * get(a, b, i, j) for (b, j), right in v.items())
            rows.append(left * inner)
        return add_terms(rows)

    def axpy(scale, u, v):
        out = dict(v)
        for key, value in u.items():
            term = scale * value
            out[key] = out[key] + term if key in out else term
        return out

    one = jnp.ones_like(mu[0])
    gradient = {(0, 0): 0.25 * one}
    direction = {(1, 0): one}
    model = {}
    for iteration in range(ITERS):
        mixing = -form(entry_a, gradient, direction) / form(entry_a, direction, direction)
        direction = axpy(mixing, direction, gradient)
        step = form(entry, gradient, direction) / form(entry_a, direction, direction)
        model = axpy(step, direction, model)
        if iteration < ITERS - 1:
            image = {key: value * (0.25 * SHIFT) for key, value in direction.items()}
            image = axpy(0.25, {(a, i + 1): value for (a, i), value in direction.items()}, image)
            gradient = axpy(-step, image, gradient)
    return model, direction


def last_kernel(
    n, x, moments_ref, m_ref, d_ref, g_in, bg_in, b2g_in, bd_in, b2d_in, g_end, bg_end, b2g_end, bd_end, b2d_end,
    model_hbm, dir_hbm, mo_ref, do_ref, sems,
):
    moments = [
        jnp.broadcast_to(jnp.sum(moments_ref[pl.ds(k, 1), :], axis=1, keepdims=True), (NT, LANES))
        for k in range(N_MOMENTS)
    ]
    model, direction = solve(moments)
    rows = [
        Mended(n, LOW[k], HIGH[k], whole, ends)
        for k, whole, ends in ((0, g_in, g_end), (1, bg_in, bg_end), (2, b2g_in, b2g_end), (4, bd_in, bd_end), (5, b2d_in, b2d_end))
    ]
    keys = ((0, 0), (0, 1), (0, 2), (1, 1), (1, 2))
    copies = []
    for i in range(n):
        def step(c, _):
            x0 = pl.multiple_of(c * LANES, LANES)
            here = pl.ds(x0, LANES)
            values = {key: vector.load(i, here) for key, vector in zip(keys, rows)}
            values[1, 0] = d_ref[i + 1, :, here]
            mo_ref[i, :, here] = m_ref[i + 1, :, here] + add_terms(
                model[key] * value for key, value in values.items())
            do_ref[i, :, here] = add_terms(direction[key] * value for key, value in values.items())
            return 0

        lax.fori_loop(0, x // LANES, step, 0, unroll=4)
        for k, (src, dst) in enumerate(((mo_ref, model_hbm), (do_ref, dir_hbm))):
            copy = pltpu.make_async_copy(src.at[i], dst.at[i], sems.at[2 * i + k])
            copy.start()
            copies.append(copy)
    for copy in copies:
        copy.wait()


def in_vmem(values):
    return [pltpu.with_memory_space_constraint(v, pltpu.VMEM) for v in values]


def kept(shape, dtype=f32):
    return pltpu.VMEM(shape, dtype)


def on_device(*args):
    n, _, x = args[0].shape
    peers = lax.axis_size("inline")
    assert peers & (peers - 1) == 0 and n >= 7 and x % CHUNK == 0
    vmem = pl.BlockSpec(memory_space=pltpu.VMEM)
    hbm = pl.BlockSpec(memory_space=pl.ANY)
    params = pltpu.CompilerParams(vmem_limit_bytes=VMEM_LIMIT)
    wide = kept((n + 2, NT, x + LANES))
    share = x // NT

    args = [pltpu.with_memory_space_constraint(v, pltpu.HBM) for v in args]

    def call(kernel, out_shape, in_specs, scratch_shapes, name):
        return pl.pallas_call(
            functools.partial(kernel, n, x),
            out_shape=out_shape,
            in_specs=in_specs,
            out_specs=[vmem] * len(out_shape),
            scratch_shapes=scratch_shapes,
            compiler_params=params,
            name=name,
        )

    def carry(slots):
        return pltpu.VMEM((slots, 2, NT, LANES), f32)

    def ends(rows):
        return kept((rows, NT, x + LANES))

    def to_before(value):
        return lax.ppermute(value, "inline", [(i, i - 1) for i in range(1, peers)])

    def to_after(value):
        return lax.ppermute(value, "inline", [(i, i + 1) for i in range(peers - 1)])

    up_first, = call(
        pack_kernel, [kept((NT, FIRST0 * x))], [hbm] * 4, [pltpu.SemaphoreType.DMA((4,))], "pack",
    )(*args[2:])
    up_first = to_before(up_first)

    *loaded, up, slope = call(
        first_kernel,
        [kept((n, NT, x)), kept((n, x), jnp.int32), kept((n + 2, NT, x)), kept((n, NT, x)), wide, wide,
         kept((NT, LATE0 * x + share)), kept((NT, x))],
        [hbm] * 6,
        [pltpu.VMEM((4, NT, x + LANES), f32)] * 3 + [carry(5), pltpu.SemaphoreType.DMA((11,))], "first",
    )(*args)
    loaded = in_vmem(loaded)
    _, mask, si, sc, m, d = loaded
    up = to_before(up)
    slope = to_after(slope)

    down, eps = call(
        down_kernel, [kept((NT, DOWN1 * x)), ends(2)], [vmem] * 7,
        [pltpu.VMEM((n + 2, NT, x + LANES), f32), carry(3)], "down",
    )(*loaded, up_first)
    received = to_after(down)

    made = call(
        local_kernel, [wide, wide, wide, wide, wide, kept((N_MOMENTS, NT, LANES))], [vmem] * 7,
        [carry(2 * n)], "local",
    )(*loaded, down)
    g, bg, b2g, bd, b2d, sums = in_vmem(made)

    out = call(
        join_kernel,
        [ends(LOW[k] + HIGH[k]) for k in (0, 1, 2, 4, 5)] + [jax.ShapeDtypeStruct((24, LANES), f32)], [vmem] * 15,
        [pltpu.VMEM((2, NT, x + LANES), f32), pltpu.VMEM((1, x), f32), pltpu.VMEM((12, NT, x + LANES), f32), carry(8),
         pltpu.VMEM((N_MOMENTS, NT, LANES), f32)], "join",
    )(d, si, sc, mask, g, bg, b2g, bd, b2d, sums, eps, up_first, up, slope, received)
    moments = out[5]

    reach = 1
    while reach < peers:
        span = min(4, peers // reach)
        others = [lax.ppermute(moments, "inline", [(i, i ^ (k * reach)) for i in range(peers)]) for k in range(1, span)]
        moments = moments + add_terms(others)
        reach *= span

    return pl.pallas_call(
        functools.partial(last_kernel, n, x),
        out_shape=[jax.ShapeDtypeStruct((n, NT, x), f32)] * 2,
        in_specs=[vmem] * 13,
        out_specs=[hbm] * 2,
        scratch_shapes=[
            pltpu.VMEM((n, NT, x), f32),
            pltpu.VMEM((n, NT, x), f32),
            pltpu.SemaphoreType.DMA((2 * n,)),
        ],
        compiler_params=params,
        name="last",
    )(
        moments, m, d, g, bg, b2g, bd, b2d, *in_vmem(out[:5]))


def solution(mesh):
    rows = P(("groups", "inline"), None, None)
    return jax.shard_map(
        on_device,
        mesh=mesh,
        in_specs=(rows, P(("groups", "inline"), None), rows, rows, rows, rows),
        out_specs=(rows, rows),
        check_vma=False,
    )
```

```python
import functools

import jax
import jax.numpy as jnp
from jax import lax
from jax.experimental import pallas as pl
from jax.experimental.pallas import tpu as pltpu
from jax.sharding import PartitionSpec as P

ITERS = 3
NT = 8
LANES = 128
CHUNK = 4096
SHIFT = 18.0
M0, D0, SI0, SC0, FIRST0 = range(5)
G0, BD0, BG0, B2D0, B2G0, LATE0 = range(6)
WM1, WD1, G1, BD1, BG1, DOWN1 = range(6)
N_MOMENTS = 18
VMEM_LIMIT = 16 * 1024 * 1024

f32 = jnp.float32


def time_ahead(v):
    rolled = pltpu.roll(v, NT - 1, 0)
    return jnp.where(lax.broadcasted_iota(jnp.int32, v.shape, 0) == NT - 1, 0.0, rolled)


def time_behind(v):
    rolled = pltpu.roll(v, 1, 0)
    return jnp.where(lax.broadcasted_iota(jnp.int32, v.shape, 0) == 0, 0.0, rolled)


def sum_diff(v):
    ahead = time_ahead(v)
    return ahead + v, ahead - v


def head(pair, width):
    return pair[0][:, :width], pair[1][:, :width]


def inline_res(here, after, slope):
    return (after[0] - here[0]) + slope * (after[1] + here[1])


def parts(res, slope):
    scaled = slope * res
    return res - scaled, res + scaled


def to_next(ef):
    return ef[0] + time_behind(ef[1])


def to_self(ef):
    return -(ef[1] + time_behind(ef[0]))


def lane_ahead(v):
    width = v.shape[1]
    return pltpu.roll(v, width - 1, 1)[:, : width - LANES]


def lane_behind(before, v):
    joined = jnp.concatenate([before, v], axis=1)
    return pltpu.roll(joined, 1, 1)[:, LANES:]


def cross_res(sd, slope):
    width = sd[0].shape[1] - LANES
    here = head(sd, width)
    return (lane_ahead(sd[0]) - here[0]) + slope * (lane_ahead(sd[1]) + here[1])


def cross_terms(sd, slope, carry, slot):
    e, f = parts(cross_res(sd, slope), slope)
    e_behind = lane_behind(carry[slot, 0], e)
    f_behind = lane_behind(carry[slot, 1], f)
    carry[slot, 0] = e[:, -LANES:]
    carry[slot, 1] = f[:, -LANES:]
    return e_behind - f, f_behind - e


def stencil(load, slope_in, slope_cr, lo, hi, res_lo, res_hi, carry, slot, scale_lo=None):
    out = {}
    sd = {}

    def pair(i):
        if i not in sd:
            sd[i] = sum_diff(load(i))
        return sd[i]

    before = None
    for i in range(lo - 1, hi + 1):
        here = None
        if res_lo <= i <= res_hi:
            first = pair(i)
            second = pair(i + 1)
            width = first[0].shape[1] - LANES
            slope = slope_in(i)
            res = inline_res(head(first, width), head(second, width), slope)
            if i == -1 and scale_lo is not None:
                res = res * scale_lo
            here = parts(res, slope)
        if i >= lo:
            same, later = cross_terms(pair(i), slope_cr(i), carry, slot + i - lo)
            if before is not None:
                same = same + before[0]
                later = later + before[1]
            if here is not None:
                same = same - here[1]
                later = later - here[0]
            out[i] = same + time_behind(later)
        before = here
    return out


class Mended:
    def __init__(self, n, low, high, whole, ends, before=None, after=None):
        self.n, self.low, self.high, self.whole, self.ends, self.before, self.after = n, low, high, whole, ends, before, after

    def at(self, i):
        if i < 0:
            return self.before
        if i >= self.n:
            return self.after
        if i < self.low:
            return self.ends, i
        if i >= self.n - self.high:
            return self.ends, self.low + i - self.n + self.high
        return self.whole, i + 1

    def load(self, i, lanes):
        ref, row = self.at(i)
        return ref[row, :, lanes]

    def store(self, i, lanes, value):
        ref, row = self.at(i)
        ref[row, :, lanes] = value


def chunks(x):
    return x // CHUNK


def at_chunk(c):
    return multiple(c * CHUNK)


def multiple(lane):
    return lane if isinstance(lane, int) else pl.multiple_of(lane, CHUNK)


def sweep(x, body):
    if chunks(x) == 1:
        body(0, 0)
    else:
        lax.fori_loop(0, chunks(x), body, 0)


class Own:
    def __init__(self, n, x0, si_ref, sc_ref, mask_ref, carry):
        self.n, self.x0, self.here = n, x0, pl.ds(x0, CHUNK)
        self.si_ref, self.sc_ref, self.mask_ref, self.carry = si_ref, sc_ref, mask_ref, carry

    def known4(self, i):
        return self.mask_ref[pl.ds(i, 1), self.here].astype(f32) * 4.0

    def level(self, src, lo, hi, slot):
        return stencil(
            lambda i: src[i + 1, :, pl.ds(self.x0, CHUNK + LANES)],
            lambda i: self.si_ref[i + 1, :, self.here],
            lambda i: self.sc_ref[i, :, self.here],
            lo, hi, 0, self.n - 2, self.carry, slot,
        )

    def applied(self, src, lo, hi, slot):
        out = self.level(src, lo, hi, slot)
        return {i: (self.known4(i) - SHIFT) * src[i + 1, :, self.here] + out[i] for i in out}

    def gradient(self, data_ref, m_ref, lo, hi, slot):
        out = self.level(m_ref, lo, hi, slot)
        return {i: self.known4(i) * (data_ref[i, :, self.here] - m_ref[i + 1, :, self.here]) - out[i] for i in out}


def put(ref, slot, x, x0, value):
    ref[:, pl.ds(multiple(x0 + slot * x), CHUNK)] = value


def pack_kernel(n, x, si_hbm, sc_hbm, model_hbm, dir_hbm, up_ref, sems):
    copies = [
        pltpu.make_async_copy(source.at[0], up_ref.at[:, pl.ds(slot * x, x)], sems.at[slot])
        for source, slot in ((model_hbm, M0), (dir_hbm, D0), (si_hbm, SI0), (sc_hbm, SC0))
    ]
    for copy in copies:
        copy.start()
    for copy in copies:
        copy.wait()


def first_kernel(
    n, x,
    data_hbm, mask_hbm, si_hbm, sc_hbm, model_hbm, dir_hbm,
    data_ref, mask_ref, si_ref, sc_ref, m_ref, d_ref, up_ref, slope_ref,
    g_ref, bg_ref, bd_ref, carry, sems,
):
    lanes = pl.ds(0, x)
    copies = [pltpu.make_async_copy(mask_hbm, mask_ref, sems.at[0])]
    for top in (True, False):
        for source, target, skip in (
            (model_hbm, m_ref, 1), (si_hbm, si_ref, 1), (sc_hbm, sc_ref, 0), (data_hbm, data_ref, 0), (dir_hbm, d_ref, 1),
        ):
            start, size = (0, 4) if top else (4, n - 4)
            copies.append(pltpu.make_async_copy(
                source.at[pl.ds(start, size)], target.at[pl.ds(start + skip, size), :, lanes], sems.at[len(copies)]))
    for copy in copies:
        copy.start()
    clear_pads(x, (m_ref, d_ref, g_ref, bg_ref, bd_ref))
    carry[...] = jnp.zeros(carry.shape, f32)
    for copy in copies[:6]:
        copy.wait()
    share = x // NT
    for s in range(NT):
        up_ref[pl.ds(s, 1), pl.ds(LATE0 * x, share)] = mask_ref[pl.ds(0, 1), pl.ds(s * share, share)].astype(f32)

    def first(c, _):
        x0 = at_chunk(c)
        own = Own(n, x0, si_ref, sc_ref, mask_ref, carry)
        out = own.gradient(data_ref, m_ref, 0, 2, 0)
        put(up_ref, G0, x, x0, out[0])
        for i, value in out.items():
            g_ref[i + 1, :, own.here] = value
        out = own.applied(d_ref, 0, 1, 3)
        put(up_ref, BD0, x, x0, out[0])
        for i, value in out.items():
            bd_ref[i + 1, :, own.here] = value
        return 0

    sweep(x, first)
    carry[...] = jnp.zeros(carry.shape, f32)

    def second(c, _):
        x0 = at_chunk(c)
        own = Own(n, x0, si_ref, sc_ref, mask_ref, carry)
        out = own.applied(g_ref, 0, 1, 0)
        put(up_ref, BG0, x, x0, out[0])
        for i, value in out.items():
            bg_ref[i + 1, :, own.here] = value
        put(up_ref, B2D0, x, x0, own.applied(bd_ref, 0, 0, 2)[0])
        return 0

    sweep(x, second)
    carry[...] = jnp.zeros(carry.shape, f32)

    def third(c, _):
        x0 = at_chunk(c)
        put(up_ref, B2G0, x, x0, Own(n, x0, si_ref, sc_ref, mask_ref, carry).applied(bg_ref, 0, 0, 0)[0])
        return 0

    sweep(x, third)
    for copy in copies[6:]:
        copy.wait()
    slope_ref[...] = si_ref[n, :, lanes]


def down_kernel(
    n, x, data_ref, mask_ref, si_ref, sc_ref, m_ref, d_ref, up_first,
    down_ref, eps_ref,
    g_ref, carry,
):
    clear_pads(x, (g_ref, eps_ref))
    carry[...] = jnp.zeros(carry.shape, f32)

    def first(c, _):
        x0 = at_chunk(c)
        here = pl.ds(x0, CHUNK)
        own = Own(n, x0, si_ref, sc_ref, mask_ref, carry)
        slope = si_ref[n, :, here]
        out = own.gradient(data_ref, m_ref, n - 2, n - 1, 0)
        ef = parts(inline_res(sum_diff(m_ref[n, :, here]), sum_diff(row_of(up_first, M0, x, x0)), slope), slope)
        g_ref[n - 1, :, here] = out[n - 2]
        g_ref[n, :, here] = out[n - 1] - to_self(ef)
        put(down_ref, G1, x, x0, g_ref[n, :, here])
        eps_ref[0, :, here] = -to_next(ef)
        put(down_ref, WM1, x, x0, eps_ref[0, :, here])
        ef = parts(inline_res(sum_diff(d_ref[n, :, here]), sum_diff(row_of(up_first, D0, x, x0)), slope), slope)
        put(down_ref, BD1, x, x0, own.applied(d_ref, n - 1, n - 1, 2)[n - 1] + to_self(ef))
        eps_ref[1, :, here] = to_next(ef)
        put(down_ref, WD1, x, x0, eps_ref[1, :, here])
        return 0

    sweep(x, first)
    carry[...] = jnp.zeros(carry.shape, f32)

    def second(c, _):
        x0 = at_chunk(c)
        own = Own(n, x0, si_ref, sc_ref, mask_ref, carry)
        put(down_ref, BG1, x, x0, own.applied(g_ref, n - 1, n - 1, 0)[n - 1])
        return 0

    sweep(x, second)


def local_kernel(
    n, x, data_ref, mask_ref, si_ref, sc_ref, m_ref, d_ref, down_ref,
    g_ref, bg_ref, b2g_ref, bd_ref, b2d_ref, sums_ref, carry,
):
    clear_pads(x, (g_ref, bg_ref, b2g_ref, bd_ref, b2d_ref))
    carry[...] = jnp.zeros(carry.shape, f32)
    sums_ref[...] = jnp.zeros(sums_ref.shape, f32)

    def first(c, _):
        x0 = at_chunk(c)
        here = pl.ds(x0, CHUNK)
        own = Own(n, x0, si_ref, sc_ref, mask_ref, carry)
        for i, value in own.gradient(data_ref, m_ref, 0, n - 2, 0).items():
            g_ref[i + 1, :, here] = value
        for i, value in own.applied(d_ref, 0, n - 2, n).items():
            bd_ref[i + 1, :, here] = value
        g_ref[n, :, here] = row_of(down_ref, G1, x, x0)
        bd_ref[n, :, here] = row_of(down_ref, BD1, x, x0)
        return 0

    sweep(x, first)
    carry[...] = jnp.zeros(carry.shape, f32)

    def second(c, _):
        x0 = at_chunk(c)
        own = Own(n, x0, si_ref, sc_ref, mask_ref, carry)
        for i, value in own.applied(g_ref, 2, n - 2, 0).items():
            bg_ref[i + 1, :, own.here] = value
        for i, value in own.applied(bd_ref, 2, n - 2, n).items():
            b2d_ref[i + 1, :, own.here] = value
        return 0

    sweep(x, second)
    carry[...] = jnp.zeros(carry.shape, f32)

    def third(c, _):
        x0 = at_chunk(c)
        own = Own(n, x0, si_ref, sc_ref, mask_ref, carry)
        for i, value in own.applied(bg_ref, 3, n - 3, 0).items():
            b2g_ref[i + 1, :, own.here] = value
        return 0

    sweep(x, third)

    def fourth(c, _):
        x0 = at_chunk(c)
        loads = [lambda i, lanes, ref=ref: ref[i + 1, :, lanes] for ref in (g_ref, bg_ref, b2g_ref, d_ref, bd_ref, b2d_ref)]
        products(n, x0, loads, mask_ref, si_ref, sc_ref, sums_ref, lambda done: done)
        return 0

    sweep(x, fourth)


PAIRS = ((0, 0), (0, 1), (1, 1), (1, 2), (2, 2), None, (0, 3), (0, 4), (1, 4), (1, 5), (2, 5), None,
         (3, 3), (3, 4), (4, 4), (4, 5), (5, 5), None)


class Totals:
    def __init__(self):
        self.of = {}

    def add(self, k, left, right):
        product = left * right
        acc = product[:, :LANES]
        for j in range(1, CHUNK // LANES):
            acc = acc + product[:, j * LANES:(j + 1) * LANES]
        self.of[k] = self.of[k] + acc if k in self.of else acc

    def put(self, sums):
        for k, value in self.of.items():
            sums[k] = sums[k] + value


class Pairs:
    def __init__(self, load, x0):
        self.load, self.lanes, self.of = load, pl.ds(x0, CHUNK + LANES), {}

    def at(self, i):
        if i not in self.of:
            self.of[i] = sum_diff(self.load(i, self.lanes))
        return self.of[i]

    def inline(self, i, slope):
        return inline_res(head(self.at(i), CHUNK), head(self.at(i + 1), CHUNK), slope)

    def cross(self, i, slope):
        return cross_res(self.at(i), slope)


LOW = (1, 2, 3, 0, 1, 2)
HIGH = (0, 1, 2, 0, 0, 1)


def products(n, x0, loads, mask_ref, si_ref, sc_ref, sums, take):
    here = pl.ds(x0, CHUNK)
    totals = Totals()
    pair_g, pair_d = Pairs(loads[2], x0), Pairs(loads[5], x0)

    def turn(i, *vectors):
        return take(all(LOW[v] <= i < n - HIGH[v] for v in vectors))

    for i in range(n):
        values = {}

        def row(v):
            if v not in values:
                values[v] = loads[v](i, here)
            return values[v]

        for k, which in enumerate(PAIRS):
            if which is not None and turn(i, *which):
                totals.add(k, row(which[0]), row(which[1]))
        res = {}
        for k, left, right in ((5, 2, 2), (11, 2, 5), (17, 5, 5)):
            if turn(i, left, right):
                known = mask_ref[pl.ds(i, 1), here].astype(f32) * 4.0
                totals.add(k, known * row(left), row(right))
                for v, pair in ((left, pair_g if left == 2 else pair_d), (right, pair_d if right == 5 else pair_g)):
                    if ("cross", v) not in res:
                        res["cross", v] = pair.cross(i, sc_ref[i, :, here])
                totals.add(k, res["cross", left], res["cross", right])
            if take(all(LOW[v] <= i < n - 1 - HIGH[v] for v in (left, right))):
                for v, pair in ((left, pair_g if left == 2 else pair_d), (right, pair_d if right == 5 else pair_g)):
                    if ("inline", v) not in res:
                        res["inline", v] = pair.inline(i, si_ref[i + 1, :, here])
                totals.add(k, res["inline", left], res["inline", right])
    totals.put(sums)


def place_flags():
    place = lax.axis_index("inline")
    return (place > 0).astype(f32), (place < lax.axis_size("inline") - 1).astype(f32)


def row_of(ref, slot, x, x0):
    return ref[:, pl.ds(multiple(x0 + slot * x), CHUNK)]


def boundary(rows, i, slope, here, scale=None):
    res = inline_res(sum_diff(rows.load(i, here)), sum_diff(rows.load(i + 1, here)), slope)
    if scale is not None:
        res = res * scale
    return parts(res, slope)


def clear_pads(x, refs):
    for ref in refs:
        for i in range(ref.shape[0]):
            ref[i, :, pl.ds(x, LANES)] = jnp.zeros((NT, LANES), f32)


def end_rows(n, x0, src, dst, slope_before, si_ref, sc_ref, mask_ref, scale, carry, slot):
    here = pl.ds(x0, CHUNK)
    for lo, hi in ((0, dst.low - 1), (n - dst.high, n - 1)):
        out = stencil(
            lambda i: src.load(i, pl.ds(x0, CHUNK + LANES)),
            lambda i: slope_before if i == -1 else si_ref[i + 1, :, here],
            lambda i: sc_ref[i, :, here],
            lo, hi, -1, n - 1, carry, slot, scale,
        )
        for i in range(lo, hi + 1):
            known = mask_ref[pl.ds(i, 1), here].astype(f32) * 4.0
            dst.store(i, here, (known - SHIFT) * src.load(i, here) + out[i])
        slot += hi - lo + 1
    return slot


def beyond(rows_ref, row, wide, diagonal, cross, slope, carry, slot, further=None):
    here = pl.ds(wide.start, CHUNK)
    sd = sum_diff(rows_ref[row, :, wide])
    near = head(sd, CHUNK)
    same, later = cross_terms(sd, cross, carry, slot)
    if further is None:
        inner = parts(slope * near[1] - near[0], slope)
    else:
        inner = parts(inline_res(near, sum_diff(further), slope), slope)
    return diagonal * rows_ref[row, :, here] + (same - inner[1]) + time_behind(later - inner[0]), inner


def join_kernel(
    n, x,
    d_ref, si_ref, sc_ref, mask_ref, g_in, bg_in, b2g_in, bd_in, b2d_in, sums_in, eps_in,
    up_first, up_ref, slope_ref, down_ref,
    g_out, bg_out, b2g_out, bd_out, b2d_out, moments_ref,
    eps_ref, mask_up, ghosts, carry, sums,
):
    not_first, not_last = place_flags()
    clear_pads(x, (eps_ref, ghosts, g_out, bg_out, b2g_out, bd_out, b2d_out))
    carry[...] = jnp.zeros(carry.shape, f32)
    sums[...] = sums_in[...]
    share = x // NT
    for s in range(NT):
        mask_up[:, pl.ds(s * share, share)] = up_ref[pl.ds(s, 1), pl.ds(LATE0 * x, share)] * 4.0 - SHIFT
    g_rows, bg_rows, b2g_rows, d_rows, bd_rows, b2d_rows = (
        Mended(n, low, high, whole, ends, (ghosts, 2 * k), (ghosts, 2 * k + 1))
        for k, (low, high, whole, ends) in enumerate(zip(
            LOW, HIGH, (g_in, bg_in, b2g_in, d_ref, bd_in, b2d_in), (g_out, bg_out, b2g_out, None, bd_out, b2d_out)))
    )

    def zeroth(c, _):
        x0 = at_chunk(c)
        here = pl.ds(x0, CHUNK)
        g_rows.store(-1, here, row_of(down_ref, G1, x, x0))
        g_rows.store(0, here, g_in[1, :, here] + row_of(down_ref, WM1, x, x0))
        g_rows.store(n, here, (row_of(up_ref, G0, x, x0) + eps_in[0, :, here]) * not_last)
        bd_rows.store(-1, here, row_of(down_ref, BD1, x, x0))
        bd_rows.store(0, here, bd_in[1, :, here] + row_of(down_ref, WD1, x, x0))
        bd_rows.store(n, here, (row_of(up_ref, BD0, x, x0) + eps_in[1, :, here]) * not_last)
        return 0

    sweep(x, zeroth)

    def first(c, _):
        x0 = at_chunk(c)
        here = pl.ds(x0, CHUNK)
        before = slope_ref[:, here]
        slope = si_ref[n, :, here]
        slot = end_rows(n, x0, g_rows, bg_rows, before, si_ref, sc_ref, mask_ref, not_first, carry, 0)
        slot = end_rows(n, x0, bd_rows, b2d_rows, before, si_ref, sc_ref, mask_ref, not_first, carry, slot)
        wide = pl.ds(x0, CHUNK + LANES)
        slope_up, cross_up = row_of(up_first, SI0, x, x0), row_of(up_first, SC0, x, x0)
        diagonal = mask_up[:, here]
        own, inner = beyond(eps_in, 0, wide, diagonal, cross_up, slope_up, carry, slot)
        eps = own + to_next(boundary(g_rows, n - 1, slope, here))
        eps_ref[0, :, here] = eps
        eps_ref[1, :, here] = to_next(inner)
        bg_rows.store(n, here, (row_of(up_ref, BG0, x, x0) + eps) * not_last)
        own, _ = beyond(eps_in, 1, wide, diagonal, cross_up, slope_up, carry, slot + 1)
        eps = own + to_next(boundary(bd_rows, n - 1, slope, here))
        b2d_rows.store(n, here, (row_of(up_ref, B2D0, x, x0) + eps) * not_last)
        bg_rows.store(-1, here, row_of(down_ref, BG1, x, x0) + to_self(boundary(g_rows, -1, before, here, not_first)))
        return 0

    sweep(x, first)
    carry[...] = jnp.zeros(carry.shape, f32)

    def second(c, _):
        x0 = at_chunk(c)
        here = pl.ds(x0, CHUNK)
        wide = pl.ds(x0, CHUNK + LANES)
        before = slope_ref[:, here]
        slot = end_rows(n, x0, bg_rows, b2g_rows, before, si_ref, sc_ref, mask_ref, not_first, carry, 0)
        own, _ = beyond(
            eps_ref, 0, wide, mask_up[:, here], row_of(up_first, SC0, x, x0), row_of(up_first, SI0, x, x0),
            carry, slot, eps_ref[1, :, here])
        edge = to_next(boundary(bg_rows, n - 1, si_ref[n, :, here], here))
        b2g_rows.store(n, here, (row_of(up_ref, B2G0, x, x0) + own + edge) * not_last)
        return 0

    sweep(x, second)

    def third(c, _):
        loads = [rows.load for rows in (g_rows, bg_rows, b2g_rows, d_rows, bd_rows, b2d_rows)]
        products(n, at_chunk(c), loads, mask_ref, si_ref, sc_ref, sums, lambda done: not done)
        return 0

    sweep(x, third)
    for k in range(N_MOMENTS):
        moments_ref[pl.ds(k, 1), :] = jnp.sum(sums[k], axis=0, keepdims=True)
    moments_ref[pl.ds(N_MOMENTS, 24 - N_MOMENTS), :] = jnp.zeros((24 - N_MOMENTS, LANES), f32)


def add_terms(terms):
    terms = list(terms)
    while len(terms) > 1:
        pairs = [left + right for left, right in zip(terms[::2], terms[1::2])]
        terms = pairs + terms[len(pairs) * 2:]
    return terms[0]


def solve(moments):
    mu, nu, xi = moments[:6], moments[6:12], moments[12:]

    def entry(a, b, i, j):
        if a == 0 and b == 0:
            return mu[i + j]
        if a == 1 and b == 1:
            return xi[i + j]
        return nu[i + j]

    shifted = {}

    def entry_a(a, b, i, j):
        which = a + b
        if (which, i + j) not in shifted:
            if i + j == 4:
                value = entry(a, b, 2, 3)
            else:
                value = entry(a, b, i, j + 1) + SHIFT * entry(a, b, i, j)
            shifted[which, i + j] = value * 0.25
        return shifted[which, i + j]

    def form(get, u, v):
        return add_terms(
            left * add_terms(right * get(a, b, i, j) for (b, j), right in v.items()) for (a, i), left in u.items())

    def axpy(scale, u, v):
        out = dict(v)
        for key, value in u.items():
            term = scale * value
            out[key] = out[key] + term if key in out else term
        return out

    one = jnp.ones_like(mu[0])
    gradient = {(0, 0): 0.25 * one}
    direction = {(1, 0): one}
    model = {}
    for iteration in range(ITERS):
        mixing = -form(entry_a, gradient, direction) / form(entry_a, direction, direction)
        direction = axpy(mixing, direction, gradient)
        step = form(entry, gradient, direction) / form(entry_a, direction, direction)
        model = axpy(step, direction, model)
        if iteration < ITERS - 1:
            image = {key: value * (0.25 * SHIFT) for key, value in direction.items()}
            image = axpy(0.25, {(a, i + 1): value for (a, i), value in direction.items()}, image)
            gradient = axpy(-step, image, gradient)
    return model, direction


def last_kernel(
    n, x, moments_ref, m_ref, d_ref, g_in, bg_in, b2g_in, bd_in, b2d_in, g_end, bg_end, b2g_end, bd_end, b2d_end,
    model_hbm, dir_hbm, mo_ref, do_ref, sems,
):
    moments = [
        jnp.broadcast_to(jnp.sum(moments_ref[pl.ds(k, 1), :], axis=1, keepdims=True), (NT, LANES))
        for k in range(N_MOMENTS)
    ]
    model, direction = solve(moments)
    rows = [
        Mended(n, LOW[k], HIGH[k], whole, ends)
        for k, whole, ends in ((0, g_in, g_end), (1, bg_in, bg_end), (2, b2g_in, b2g_end), (4, bd_in, bd_end), (5, b2d_in, b2d_end))
    ]
    keys = ((0, 0), (0, 1), (0, 2), (1, 1), (1, 2))
    copies = []
    for i in range(n):
        for c in range(x // LANES):
            here = pl.ds(c * LANES, LANES)
            values = {key: vector.load(i, here) for key, vector in zip(keys, rows)}
            values[1, 0] = d_ref[i + 1, :, here]
            mo_ref[i, :, here] = m_ref[i + 1, :, here] + add_terms(model[key] * value for key, value in values.items())
            do_ref[i, :, here] = add_terms(direction[key] * value for key, value in values.items())
        for k, (src, dst) in enumerate(((mo_ref, model_hbm), (do_ref, dir_hbm))):
            copy = pltpu.make_async_copy(src.at[i], dst.at[i], sems.at[2 * i + k])
            copy.start()
            copies.append(copy)
    for copy in copies:
        copy.wait()


def in_vmem(values):
    return [pltpu.with_memory_space_constraint(v, pltpu.VMEM) for v in values]


def kept(shape, dtype=f32):
    return pltpu.VMEM(shape, dtype)


def on_device(*args):
    n, _, x = args[0].shape
    peers = lax.axis_size("inline")
    assert peers & (peers - 1) == 0 and n >= 7 and x % CHUNK == 0
    vmem = pl.BlockSpec(memory_space=pltpu.VMEM)
    hbm = pl.BlockSpec(memory_space=pl.ANY)
    params = pltpu.CompilerParams(vmem_limit_bytes=VMEM_LIMIT)
    wide = kept((n + 2, NT, x + LANES))
    share = x // NT

    args = [pltpu.with_memory_space_constraint(v, pltpu.HBM) for v in args]

    def call(kernel, out_shape, in_specs, scratch_shapes, name):
        return pl.pallas_call(
            functools.partial(kernel, n, x),
            out_shape=out_shape,
            in_specs=in_specs,
            out_specs=[vmem] * len(out_shape),
            scratch_shapes=scratch_shapes,
            compiler_params=params,
            name=name,
        )

    def carry(slots):
        return pltpu.VMEM((slots, 2, NT, LANES), f32)

    def ends(rows):
        return kept((rows, NT, x + LANES))

    def to_before(value):
        return lax.ppermute(value, "inline", [(i, i - 1) for i in range(1, peers)])

    def to_after(value):
        return lax.ppermute(value, "inline", [(i, i + 1) for i in range(peers - 1)])

    up_first, = call(
        pack_kernel, [kept((NT, FIRST0 * x))], [hbm] * 4, [pltpu.SemaphoreType.DMA((4,))], "pack",
    )(*args[2:])
    up_first = to_before(up_first)

    *loaded, up, slope = call(
        first_kernel,
        [kept((n, NT, x)), kept((n, x), jnp.int32), kept((n + 2, NT, x)), kept((n, NT, x)), wide, wide,
         kept((NT, LATE0 * x + share)), kept((NT, x))],
        [hbm] * 6,
        [pltpu.VMEM((4, NT, x + LANES), f32)] * 3 + [carry(5), pltpu.SemaphoreType.DMA((11,))], "first",
    )(*args)
    loaded = in_vmem(loaded)
    _, mask, si, sc, m, d = loaded
    up = to_before(up)
    slope = to_after(slope)

    down, eps = call(
        down_kernel, [kept((NT, DOWN1 * x)), ends(2)], [vmem] * 7,
        [pltpu.VMEM((n + 2, NT, x + LANES), f32), carry(3)], "down",
    )(*loaded, up_first)
    received = to_after(down)

    made = call(
        local_kernel, [wide, wide, wide, wide, wide, kept((N_MOMENTS, NT, LANES))], [vmem] * 7,
        [carry(2 * n)], "local",
    )(*loaded, down)
    g, bg, b2g, bd, b2d, sums = in_vmem(made)

    out = call(
        join_kernel,
        [ends(LOW[k] + HIGH[k]) for k in (0, 1, 2, 4, 5)] + [jax.ShapeDtypeStruct((24, LANES), f32)], [vmem] * 15,
        [pltpu.VMEM((2, NT, x + LANES), f32), pltpu.VMEM((1, x), f32), pltpu.VMEM((12, NT, x + LANES), f32), carry(8),
         pltpu.VMEM((N_MOMENTS, NT, LANES), f32)], "join",
    )(d, si, sc, mask, g, bg, b2g, bd, b2d, sums, eps, up_first, up, slope, received)
    moments = out[5]

    reach = 1
    while reach < peers:
        span = min(4, peers // reach)
        others = [lax.ppermute(moments, "inline", [(i, i ^ (k * reach)) for i in range(peers)]) for k in range(1, span)]
        moments = moments + add_terms(others)
        reach *= span

    return pl.pallas_call(
        functools.partial(last_kernel, n, x),
        out_shape=[jax.ShapeDtypeStruct((n, NT, x), f32)] * 2,
        in_specs=[vmem] * 13,
        out_specs=[hbm] * 2,
        scratch_shapes=[
            pltpu.VMEM((n, NT, x), f32),
            pltpu.VMEM((n, NT, x), f32),
            pltpu.SemaphoreType.DMA((2 * n,)),
        ],
        compiler_params=params,
        name="last",
    )(
        moments, m, d, g, bg, b2g, bd, b2d, *in_vmem(out[:5]))


def solution(mesh):
    rows = P(("groups", "inline"), None, None)
    return jax.shard_map(
        on_device,
        mesh=mesh,
        in_specs=(rows, P(("groups", "inline"), None), rows, rows, rows, rows),
        out_specs=(rows, rows),
        check_vma=False,
    )
```

```python
import functools

import jax
import jax.numpy as jnp
from jax import lax
from jax.experimental import pallas as pl
from jax.experimental.pallas import tpu as pltpu
from jax.sharding import PartitionSpec as P

ITERS = 3
NT = 8
LANES = 128
CHUNK = 4096
SHIFT = 18.0
M0, D0, SI0, SC0, FIRST0 = range(5)
G0, BD0, BG0, B2D0, B2G0, LATE0 = range(6)
WM1, WD1, G1, BD1, BG1, DOWN1 = range(6)
N_MOMENTS = 18
VMEM_LIMIT = 16 * 1024 * 1024

f32 = jnp.float32


def time_ahead(v):
    rolled = pltpu.roll(v, NT - 1, 0)
    return jnp.where(lax.broadcasted_iota(jnp.int32, v.shape, 0) == NT - 1, 0.0, rolled)


def time_behind(v):
    rolled = pltpu.roll(v, 1, 0)
    return jnp.where(lax.broadcasted_iota(jnp.int32, v.shape, 0) == 0, 0.0, rolled)


def sum_diff(v):
    ahead = time_ahead(v)
    return ahead + v, ahead - v


def head(pair, width):
    return pair[0][:, :width], pair[1][:, :width]


def inline_res(here, after, slope):
    return (after[0] - here[0]) + slope * (after[1] + here[1])


def parts(res, slope):
    scaled = slope * res
    return res - scaled, res + scaled


def to_next(ef):
    return ef[0] + time_behind(ef[1])


def to_self(ef):
    return -(ef[1] + time_behind(ef[0]))


def lane_ahead(v):
    width = v.shape[1]
    return pltpu.roll(v, width - 1, 1)[:, : width - LANES]


def lane_behind(before, v):
    joined = jnp.concatenate([before, v], axis=1)
    return pltpu.roll(joined, 1, 1)[:, LANES:]


def cross_res(sd, slope):
    width = sd[0].shape[1] - LANES
    here = head(sd, width)
    return (lane_ahead(sd[0]) - here[0]) + slope * (lane_ahead(sd[1]) + here[1])


def cross_terms(sd, slope, carry, slot):
    e, f = parts(cross_res(sd, slope), slope)
    e_behind = lane_behind(carry[slot, 0], e)
    f_behind = lane_behind(carry[slot, 1], f)
    carry[slot, 0] = e[:, -LANES:]
    carry[slot, 1] = f[:, -LANES:]
    return e_behind - f, f_behind - e


def stencil(load, slope_in, slope_cr, lo, hi, res_lo, res_hi, carry, slot, scale_lo=None):
    out = {}
    sd = {}

    def pair(i):
        if i not in sd:
            sd[i] = sum_diff(load(i))
        return sd[i]

    before = None
    for i in range(lo - 1, hi + 1):
        here = None
        if res_lo <= i <= res_hi:
            first = pair(i)
            second = pair(i + 1)
            width = first[0].shape[1] - LANES
            slope = slope_in(i)
            res = inline_res(head(first, width), head(second, width), slope)
            if i == -1 and scale_lo is not None:
                res = res * scale_lo
            here = parts(res, slope)
        if i >= lo:
            same, later = cross_terms(pair(i), slope_cr(i), carry, slot + i - lo)
            if before is not None:
                same = same + before[0]
                later = later + before[1]
            if here is not None:
                same = same - here[1]
                later = later - here[0]
            out[i] = same + time_behind(later)
        before = here
    return out


class Mended:
    def __init__(self, n, low, high, whole, ends, before=None, after=None):
        self.n, self.low, self.high, self.whole, self.ends, self.before, self.after = n, low, high, whole, ends, before, after

    def at(self, i):
        if i < 0:
            return self.before
        if i >= self.n:
            return self.after
        if i < self.low:
            return self.ends, i
        if i >= self.n - self.high:
            return self.ends, self.low + i - self.n + self.high
        return self.whole, i + 1

    def load(self, i, lanes):
        ref, row = self.at(i)
        return ref[row, :, lanes]

    def store(self, i, lanes, value):
        ref, row = self.at(i)
        ref[row, :, lanes] = value


def chunks(x):
    return x // CHUNK


def at_chunk(c):
    return multiple(c * CHUNK)


def multiple(lane):
    return lane if isinstance(lane, int) else pl.multiple_of(lane, CHUNK)


def sweep(x, body):
    if chunks(x) == 1:
        body(0, 0)
    else:
        lax.fori_loop(0, chunks(x), body, 0)


class Own:
    def __init__(self, n, x0, si_ref, sc_ref, mask_ref, carry):
        self.n, self.x0, self.here = n, x0, pl.ds(x0, CHUNK)
        self.si_ref, self.sc_ref, self.mask_ref, self.carry = si_ref, sc_ref, mask_ref, carry

    def known4(self, i):
        return self.mask_ref[pl.ds(i, 1), self.here].astype(f32) * 4.0

    def level(self, src, lo, hi, slot):
        return stencil(
            lambda i: src[i + 1, :, pl.ds(self.x0, CHUNK + LANES)],
            lambda i: self.si_ref[i + 1, :, self.here],
            lambda i: self.sc_ref[i, :, self.here],
            lo, hi, 0, self.n - 2, self.carry, slot,
        )

    def applied(self, src, lo, hi, slot):
        out = self.level(src, lo, hi, slot)
        return {i: (self.known4(i) - SHIFT) * src[i + 1, :, self.here] + out[i] for i in out}

    def gradient(self, data_ref, m_ref, lo, hi, slot):
        out = self.level(m_ref, lo, hi, slot)
        return {i: self.known4(i) * (data_ref[i, :, self.here] - m_ref[i + 1, :, self.here]) - out[i] for i in out}


def put(ref, slot, x, x0, value):
    ref[:, pl.ds(multiple(x0 + slot * x), CHUNK)] = value


def pack_kernel(n, x, si_hbm, sc_hbm, model_hbm, dir_hbm, up_ref, sems):
    copies = [
        pltpu.make_async_copy(source.at[0], up_ref.at[:, pl.ds(slot * x, x)], sems.at[slot])
        for source, slot in ((model_hbm, M0), (dir_hbm, D0), (si_hbm, SI0), (sc_hbm, SC0))
    ]
    for copy in copies:
        copy.start()
    for copy in copies:
        copy.wait()


def first_kernel(
    n, x,
    data_hbm, mask_hbm, si_hbm, sc_hbm, model_hbm, dir_hbm,
    data_ref, mask_ref, si_ref, sc_ref, m_ref, d_ref, up_ref, slope_ref,
    g_ref, bg_ref, bd_ref, carry, sems,
):
    lanes = pl.ds(0, x)
    copies = [pltpu.make_async_copy(mask_hbm, mask_ref, sems.at[0])]
    for top in (True, False):
        for source, target, skip in (
            (model_hbm, m_ref, 1), (si_hbm, si_ref, 1), (sc_hbm, sc_ref, 0), (data_hbm, data_ref, 0), (dir_hbm, d_ref, 1),
        ):
            start, size = (0, 4) if top else (4, n - 4)
            copies.append(pltpu.make_async_copy(
                source.at[pl.ds(start, size)], target.at[pl.ds(start + skip, size), :, lanes], sems.at[len(copies)]))
    for copy in copies:
        copy.start()
    clear_pads(x, (m_ref, d_ref, g_ref, bg_ref, bd_ref))
    carry[...] = jnp.zeros(carry.shape, f32)
    for copy in copies[:6]:
        copy.wait()
    share = x // NT
    for s in range(NT):
        up_ref[pl.ds(s, 1), pl.ds(LATE0 * x, share)] = mask_ref[pl.ds(0, 1), pl.ds(s * share, share)].astype(f32)

    def first(c, _):
        x0 = at_chunk(c)
        own = Own(n, x0, si_ref, sc_ref, mask_ref, carry)
        out = own.gradient(data_ref, m_ref, 0, 2, 0)
        put(up_ref, G0, x, x0, out[0])
        for i, value in out.items():
            g_ref[i + 1, :, own.here] = value
        out = own.applied(d_ref, 0, 1, 3)
        put(up_ref, BD0, x, x0, out[0])
        for i, value in out.items():
            bd_ref[i + 1, :, own.here] = value
        return 0

    sweep(x, first)
    carry[...] = jnp.zeros(carry.shape, f32)

    def second(c, _):
        x0 = at_chunk(c)
        own = Own(n, x0, si_ref, sc_ref, mask_ref, carry)
        out = own.applied(g_ref, 0, 1, 0)
        put(up_ref, BG0, x, x0, out[0])
        for i, value in out.items():
            bg_ref[i + 1, :, own.here] = value
        put(up_ref, B2D0, x, x0, own.applied(bd_ref, 0, 0, 2)[0])
        return 0

    sweep(x, second)
    carry[...] = jnp.zeros(carry.shape, f32)

    def third(c, _):
        x0 = at_chunk(c)
        put(up_ref, B2G0, x, x0, Own(n, x0, si_ref, sc_ref, mask_ref, carry).applied(bg_ref, 0, 0, 0)[0])
        return 0

    sweep(x, third)
    for copy in copies[6:]:
        copy.wait()
    slope_ref[...] = si_ref[n, :, lanes]


def down_kernel(
    n, x, data_ref, mask_ref, si_ref, sc_ref, m_ref, d_ref, up_first,
    down_ref, eps_ref,
    g_ref, carry,
):
    clear_pads(x, (g_ref, eps_ref))
    carry[...] = jnp.zeros(carry.shape, f32)

    def first(c, _):
        x0 = at_chunk(c)
        here = pl.ds(x0, CHUNK)
        own = Own(n, x0, si_ref, sc_ref, mask_ref, carry)
        slope = si_ref[n, :, here]
        out = own.gradient(data_ref, m_ref, n - 2, n - 1, 0)
        ef = parts(inline_res(sum_diff(m_ref[n, :, here]), sum_diff(row_of(up_first, M0, x, x0)), slope), slope)
        g_ref[n - 1, :, here] = out[n - 2]
        g_ref[n, :, here] = out[n - 1] - to_self(ef)
        put(down_ref, G1, x, x0, g_ref[n, :, here])
        eps_ref[0, :, here] = -to_next(ef)
        put(down_ref, WM1, x, x0, eps_ref[0, :, here])
        ef = parts(inline_res(sum_diff(d_ref[n, :, here]), sum_diff(row_of(up_first, D0, x, x0)), slope), slope)
        put(down_ref, BD1, x, x0, own.applied(d_ref, n - 1, n - 1, 2)[n - 1] + to_self(ef))
        eps_ref[1, :, here] = to_next(ef)
        put(down_ref, WD1, x, x0, eps_ref[1, :, here])
        return 0

    sweep(x, first)
    carry[...] = jnp.zeros(carry.shape, f32)

    def second(c, _):
        x0 = at_chunk(c)
        own = Own(n, x0, si_ref, sc_ref, mask_ref, carry)
        put(down_ref, BG1, x, x0, own.applied(g_ref, n - 1, n - 1, 0)[n - 1])
        return 0

    sweep(x, second)


def local_kernel(
    n, x, data_ref, mask_ref, si_ref, sc_ref, m_ref, d_ref, down_ref,
    g_ref, bg_ref, b2g_ref, bd_ref, b2d_ref, sums_ref, carry,
):
    clear_pads(x, (g_ref, bg_ref, b2g_ref, bd_ref, b2d_ref))
    carry[...] = jnp.zeros(carry.shape, f32)
    sums_ref[...] = jnp.zeros(sums_ref.shape, f32)

    def first(c, _):
        x0 = at_chunk(c)
        here = pl.ds(x0, CHUNK)
        own = Own(n, x0, si_ref, sc_ref, mask_ref, carry)
        for i, value in own.gradient(data_ref, m_ref, 0, n - 2, 0).items():
            g_ref[i + 1, :, here] = value
        for i, value in own.applied(d_ref, 0, n - 2, n).items():
            bd_ref[i + 1, :, here] = value
        g_ref[n, :, here] = row_of(down_ref, G1, x, x0)
        bd_ref[n, :, here] = row_of(down_ref, BD1, x, x0)
        return 0

    sweep(x, first)
    carry[...] = jnp.zeros(carry.shape, f32)

    def second(c, _):
        x0 = at_chunk(c)
        own = Own(n, x0, si_ref, sc_ref, mask_ref, carry)
        for i, value in own.applied(g_ref, 2, n - 2, 0).items():
            bg_ref[i + 1, :, own.here] = value
        for i, value in own.applied(bd_ref, 2, n - 2, n).items():
            b2d_ref[i + 1, :, own.here] = value
        return 0

    sweep(x, second)
    carry[...] = jnp.zeros(carry.shape, f32)

    def third(c, _):
        x0 = at_chunk(c)
        own = Own(n, x0, si_ref, sc_ref, mask_ref, carry)
        for i, value in own.applied(bg_ref, 3, n - 3, 0).items():
            b2g_ref[i + 1, :, own.here] = value
        return 0

    sweep(x, third)

    def fourth(c, _):
        x0 = at_chunk(c)
        loads = [lambda i, lanes, ref=ref: ref[i + 1, :, lanes] for ref in (g_ref, bg_ref, b2g_ref, d_ref, bd_ref, b2d_ref)]
        products(n, x0, loads, mask_ref, si_ref, sc_ref, sums_ref, lambda done: done)
        return 0

    sweep(x, fourth)


PAIRS = ((0, 0), (0, 1), (1, 1), (1, 2), (2, 2), None, (0, 3), (0, 4), (1, 4), (1, 5), (2, 5), None,
         (3, 3), (3, 4), (4, 4), (4, 5), (5, 5), None)


class Totals:
    def __init__(self):
        self.of = {}

    def add(self, k, left, right):
        product = left * right
        acc = product[:, :LANES]
        for j in range(1, CHUNK // LANES):
            acc = acc + product[:, j * LANES:(j + 1) * LANES]
        self.of[k] = self.of[k] + acc if k in self.of else acc

    def put(self, sums):
        for k, value in self.of.items():
            sums[k] = sums[k] + value


class Pairs:
    def __init__(self, load, x0):
        self.load, self.lanes, self.of = load, pl.ds(x0, CHUNK + LANES), {}

    def at(self, i):
        if i not in self.of:
            self.of[i] = sum_diff(self.load(i, self.lanes))
        return self.of[i]

    def inline(self, i, slope):
        return inline_res(head(self.at(i), CHUNK), head(self.at(i + 1), CHUNK), slope)

    def cross(self, i, slope):
        return cross_res(self.at(i), slope)


LOW = (1, 2, 3, 0, 1, 2)
HIGH = (0, 1, 2, 0, 0, 1)


def products(n, x0, loads, mask_ref, si_ref, sc_ref, sums, take):
    here = pl.ds(x0, CHUNK)
    totals = Totals()
    pair_g, pair_d = Pairs(loads[2], x0), Pairs(loads[5], x0)

    def turn(i, *vectors):
        return take(all(LOW[v] <= i < n - HIGH[v] for v in vectors))

    for i in range(n):
        values = {}

        def row(v):
            if v not in values:
                values[v] = loads[v](i, here)
            return values[v]

        for k, which in enumerate(PAIRS):
            if which is not None and turn(i, *which):
                totals.add(k, row(which[0]), row(which[1]))
        res = {}
        for k, left, right in ((5, 2, 2), (11, 2, 5), (17, 5, 5)):
            if turn(i, left, right):
                known = mask_ref[pl.ds(i, 1), here].astype(f32) * 4.0
                totals.add(k, known * row(left), row(right))
                for v, pair in ((left, pair_g if left == 2 else pair_d), (right, pair_d if right == 5 else pair_g)):
                    if ("cross", v) not in res:
                        res["cross", v] = pair.cross(i, sc_ref[i, :, here])
                totals.add(k, res["cross", left], res["cross", right])
            if take(all(LOW[v] <= i < n - 1 - HIGH[v] for v in (left, right))):
                for v, pair in ((left, pair_g if left == 2 else pair_d), (right, pair_d if right == 5 else pair_g)):
                    if ("inline", v) not in res:
                        res["inline", v] = pair.inline(i, si_ref[i + 1, :, here])
                totals.add(k, res["inline", left], res["inline", right])
    totals.put(sums)


def place_flags():
    place = lax.axis_index("inline")
    return (place > 0).astype(f32), (place < lax.axis_size("inline") - 1).astype(f32)


def row_of(ref, slot, x, x0):
    return ref[:, pl.ds(multiple(x0 + slot * x), CHUNK)]


def boundary(rows, i, slope, here, scale=None):
    res = inline_res(sum_diff(rows.load(i, here)), sum_diff(rows.load(i + 1, here)), slope)
    if scale is not None:
        res = res * scale
    return parts(res, slope)


def clear_pads(x, refs):
    for ref in refs:
        for i in range(ref.shape[0]):
            ref[i, :, pl.ds(x, LANES)] = jnp.zeros((NT, LANES), f32)


def end_rows(n, x0, src, dst, slope_before, si_ref, sc_ref, mask_ref, scale, carry, slot):
    here = pl.ds(x0, CHUNK)
    for lo, hi in ((0, dst.low - 1), (n - dst.high, n - 1)):
        out = stencil(
            lambda i: src.load(i, pl.ds(x0, CHUNK + LANES)),
            lambda i: slope_before if i == -1 else si_ref[i + 1, :, here],
            lambda i: sc_ref[i, :, here],
            lo, hi, -1, n - 1, carry, slot, scale,
        )
        for i in range(lo, hi + 1):
            known = mask_ref[pl.ds(i, 1), here].astype(f32) * 4.0
            dst.store(i, here, (known - SHIFT) * src.load(i, here) + out[i])
        slot += hi - lo + 1
    return slot


def beyond(rows_ref, row, wide, diagonal, cross, slope, carry, slot, further=None):
    here = pl.ds(wide.start, CHUNK)
    sd = sum_diff(rows_ref[row, :, wide])
    near = head(sd, CHUNK)
    same, later = cross_terms(sd, cross, carry, slot)
    if further is None:
        inner = parts(slope * near[1] - near[0], slope)
    else:
        inner = parts(inline_res(near, sum_diff(further), slope), slope)
    return diagonal * rows_ref[row, :, here] + (same - inner[1]) + time_behind(later - inner[0]), inner


def join_kernel(
    n, x,
    d_ref, si_ref, sc_ref, mask_ref, g_in, bg_in, b2g_in, bd_in, b2d_in, sums_in, eps_in,
    up_first, up_ref, slope_ref, down_ref,
    g_out, bg_out, b2g_out, bd_out, b2d_out, moments_ref,
    eps_ref, mask_up, ghosts, carry, sums, rows_ref,
):
    not_first, not_last = place_flags()
    clear_pads(x, (eps_ref, ghosts, g_out, bg_out, b2g_out, bd_out, b2d_out))
    carry[...] = jnp.zeros(carry.shape, f32)
    sums[...] = sums_in[...]
    share = x // NT
    for s in range(NT):
        mask_up[:, pl.ds(s * share, share)] = up_ref[pl.ds(s, 1), pl.ds(LATE0 * x, share)] * 4.0 - SHIFT
    g_rows, bg_rows, b2g_rows, d_rows, bd_rows, b2d_rows = (
        Mended(n, low, high, whole, ends, (ghosts, 2 * k), (ghosts, 2 * k + 1))
        for k, (low, high, whole, ends) in enumerate(zip(
            LOW, HIGH, (g_in, bg_in, b2g_in, d_ref, bd_in, b2d_in), (g_out, bg_out, b2g_out, None, bd_out, b2d_out)))
    )

    def zeroth(c, _):
        x0 = at_chunk(c)
        here = pl.ds(x0, CHUNK)
        g_rows.store(-1, here, row_of(down_ref, G1, x, x0))
        g_rows.store(0, here, g_in[1, :, here] + row_of(down_ref, WM1, x, x0))
        g_rows.store(n, here, (row_of(up_ref, G0, x, x0) + eps_in[0, :, here]) * not_last)
        bd_rows.store(-1, here, row_of(down_ref, BD1, x, x0))
        bd_rows.store(0, here, bd_in[1, :, here] + row_of(down_ref, WD1, x, x0))
        bd_rows.store(n, here, (row_of(up_ref, BD0, x, x0) + eps_in[1, :, here]) * not_last)
        return 0

    sweep(x, zeroth)

    def first(c, _):
        x0 = at_chunk(c)
        here = pl.ds(x0, CHUNK)
        before = slope_ref[:, here]
        slope = si_ref[n, :, here]
        slot = end_rows(n, x0, g_rows, bg_rows, before, si_ref, sc_ref, mask_ref, not_first, carry, 0)
        slot = end_rows(n, x0, bd_rows, b2d_rows, before, si_ref, sc_ref, mask_ref, not_first, carry, slot)
        wide = pl.ds(x0, CHUNK + LANES)
        slope_up, cross_up = row_of(up_first, SI0, x, x0), row_of(up_first, SC0, x, x0)
        diagonal = mask_up[:, here]
        own, inner = beyond(eps_in, 0, wide, diagonal, cross_up, slope_up, carry, slot)
        eps = own + to_next(boundary(g_rows, n - 1, slope, here))
        eps_ref[0, :, here] = eps
        eps_ref[1, :, here] = to_next(inner)
        bg_rows.store(n, here, (row_of(up_ref, BG0, x, x0) + eps) * not_last)
        own, _ = beyond(eps_in, 1, wide, diagonal, cross_up, slope_up, carry, slot + 1)
        eps = own + to_next(boundary(bd_rows, n - 1, slope, here))
        b2d_rows.store(n, here, (row_of(up_ref, B2D0, x, x0) + eps) * not_last)
        bg_rows.store(-1, here, row_of(down_ref, BG1, x, x0) + to_self(boundary(g_rows, -1, before, here, not_first)))
        return 0

    sweep(x, first)
    carry[...] = jnp.zeros(carry.shape, f32)

    def second(c, _):
        x0 = at_chunk(c)
        here = pl.ds(x0, CHUNK)
        wide = pl.ds(x0, CHUNK + LANES)
        before = slope_ref[:, here]
        slot = end_rows(n, x0, bg_rows, b2g_rows, before, si_ref, sc_ref, mask_ref, not_first, carry, 0)
        own, _ = beyond(
            eps_ref, 0, wide, mask_up[:, here], row_of(up_first, SC0, x, x0), row_of(up_first, SI0, x, x0),
            carry, slot, eps_ref[1, :, here])
        edge = to_next(boundary(bg_rows, n - 1, si_ref[n, :, here], here))
        b2g_rows.store(n, here, (row_of(up_ref, B2G0, x, x0) + own + edge) * not_last)
        return 0

    sweep(x, second)

    def third(c, _):
        loads = [rows.load for rows in (g_rows, bg_rows, b2g_rows, d_rows, bd_rows, b2d_rows)]
        products(n, at_chunk(c), loads, mask_ref, si_ref, sc_ref, sums, lambda done: not done)
        return 0

    sweep(x, third)
    for k in range(N_MOMENTS):
        rows_ref[pl.ds(k, 1), :] = jnp.sum(sums[k], axis=0, keepdims=True)
    rows_ref[pl.ds(N_MOMENTS, 24 - N_MOMENTS), :] = jnp.zeros((24 - N_MOMENTS, LANES), f32)
    rows = rows_ref[...]
    rows = rows + pltpu.roll(rows, LANES // 2, 1)
    rows = rows + pltpu.roll(rows, LANES // 4, 1)
    group = lax.broadcasted_iota(jnp.int32, (8, LANES), 1) // (LANES // 4)
    moments_ref[...] = jnp.where(group == 0, rows[:8], jnp.where(group == 1, rows[8:16], rows[16:]))


def add_terms(terms):
    terms = list(terms)
    while len(terms) > 1:
        pairs = [left + right for left, right in zip(terms[::2], terms[1::2])]
        terms = pairs + terms[len(pairs) * 2:]
    return terms[0]


def solve(moments):
    mu, nu, xi = moments[:6], moments[6:12], moments[12:]

    def entry(a, b, i, j):
        if a == 0 and b == 0:
            return mu[i + j]
        if a == 1 and b == 1:
            return xi[i + j]
        return nu[i + j]

    shifted = {}

    def entry_a(a, b, i, j):
        which = a + b
        if (which, i + j) not in shifted:
            if i + j == 4:
                value = entry(a, b, 2, 3)
            else:
                value = entry(a, b, i, j + 1) + SHIFT * entry(a, b, i, j)
            shifted[which, i + j] = value * 0.25
        return shifted[which, i + j]

    def form(get, u, v):
        return add_terms(
            left * add_terms(right * get(a, b, i, j) for (b, j), right in v.items()) for (a, i), left in u.items())

    def axpy(scale, u, v):
        out = dict(v)
        for key, value in u.items():
            term = scale * value
            out[key] = out[key] + term if key in out else term
        return out

    one = jnp.ones_like(mu[0])
    gradient = {(0, 0): 0.25 * one}
    direction = {(1, 0): one}
    model = {}
    for iteration in range(ITERS):
        mixing = -form(entry_a, gradient, direction) / form(entry_a, direction, direction)
        direction = axpy(mixing, direction, gradient)
        step = form(entry, gradient, direction) / form(entry_a, direction, direction)
        model = axpy(step, direction, model)
        if iteration < ITERS - 1:
            image = {key: value * (0.25 * SHIFT) for key, value in direction.items()}
            image = axpy(0.25, {(a, i + 1): value for (a, i), value in direction.items()}, image)
            gradient = axpy(-step, image, gradient)
    return model, direction


def last_kernel(
    n, x, moments_ref, m_ref, d_ref, g_in, bg_in, b2g_in, bd_in, b2d_in, g_end, bg_end, b2g_end, bd_end, b2d_end,
    model_hbm, dir_hbm, mo_ref, do_ref, sems,
):
    group = lax.broadcasted_iota(jnp.int32, (1, LANES), 1) // (LANES // 4)
    moments = [
        jnp.broadcast_to(
            jnp.sum(jnp.where(group == k // 8, moments_ref[pl.ds(k % 8, 1), :], 0.0), axis=1, keepdims=True), (NT, LANES))
        for k in range(N_MOMENTS)
    ]
    model, direction = solve(moments)
    rows = [
        Mended(n, LOW[k], HIGH[k], whole, ends)
        for k, whole, ends in ((0, g_in, g_end), (1, bg_in, bg_end), (2, b2g_in, b2g_end), (4, bd_in, bd_end), (5, b2d_in, b2d_end))
    ]
    keys = ((0, 0), (0, 1), (0, 2), (1, 1), (1, 2))
    copies = []
    for i in range(n):
        for c in range(x // LANES):
            here = pl.ds(c * LANES, LANES)
            values = {key: vector.load(i, here) for key, vector in zip(keys, rows)}
            values[1, 0] = d_ref[i + 1, :, here]
            mo_ref[i, :, here] = m_ref[i + 1, :, here] + add_terms(model[key] * value for key, value in values.items())
            do_ref[i, :, here] = add_terms(direction[key] * value for key, value in values.items())
        for k, (src, dst) in enumerate(((mo_ref, model_hbm), (do_ref, dir_hbm))):
            copy = pltpu.make_async_copy(src.at[i], dst.at[i], sems.at[2 * i + k])
            copy.start()
            copies.append(copy)
    for copy in copies:
        copy.wait()


def in_vmem(values):
    return [pltpu.with_memory_space_constraint(v, pltpu.VMEM) for v in values]


def kept(shape, dtype=f32):
    return pltpu.VMEM(shape, dtype)


def on_device(*args):
    n, _, x = args[0].shape
    peers = lax.axis_size("inline")
    assert peers & (peers - 1) == 0 and n >= 7 and x % CHUNK == 0
    vmem = pl.BlockSpec(memory_space=pltpu.VMEM)
    hbm = pl.BlockSpec(memory_space=pl.ANY)
    params = pltpu.CompilerParams(vmem_limit_bytes=VMEM_LIMIT)
    wide = kept((n + 2, NT, x + LANES))
    share = x // NT

    args = [pltpu.with_memory_space_constraint(v, pltpu.HBM) for v in args]

    def call(kernel, out_shape, in_specs, scratch_shapes, name):
        return pl.pallas_call(
            functools.partial(kernel, n, x),
            out_shape=out_shape,
            in_specs=in_specs,
            out_specs=[vmem] * len(out_shape),
            scratch_shapes=scratch_shapes,
            compiler_params=params,
            name=name,
        )

    def carry(slots):
        return pltpu.VMEM((slots, 2, NT, LANES), f32)

    def ends(rows):
        return kept((rows, NT, x + LANES))

    def to_before(value):
        return lax.ppermute(value, "inline", [(i, i - 1) for i in range(1, peers)])

    def to_after(value):
        return lax.ppermute(value, "inline", [(i, i + 1) for i in range(peers - 1)])

    up_first, = call(
        pack_kernel, [kept((NT, FIRST0 * x))], [hbm] * 4, [pltpu.SemaphoreType.DMA((4,))], "pack",
    )(*args[2:])
    up_first = to_before(up_first)

    *loaded, up, slope = call(
        first_kernel,
        [kept((n, NT, x)), kept((n, x), jnp.int32), kept((n + 2, NT, x)), kept((n, NT, x)), wide, wide,
         kept((NT, LATE0 * x + share)), kept((NT, x))],
        [hbm] * 6,
        [pltpu.VMEM((4, NT, x + LANES), f32)] * 3 + [carry(5), pltpu.SemaphoreType.DMA((11,))], "first",
    )(*args)
    loaded = in_vmem(loaded)
    _, mask, si, sc, m, d = loaded
    up = to_before(up)
    slope = to_after(slope)

    down, eps = call(
        down_kernel, [kept((NT, DOWN1 * x)), ends(2)], [vmem] * 7,
        [pltpu.VMEM((n + 2, NT, x + LANES), f32), carry(3)], "down",
    )(*loaded, up_first)
    received = to_after(down)

    made = call(
        local_kernel, [wide, wide, wide, wide, wide, kept((N_MOMENTS, NT, LANES))], [vmem] * 7,
        [carry(2 * n)], "local",
    )(*loaded, down)
    g, bg, b2g, bd, b2d, sums = in_vmem(made)

    out = call(
        join_kernel,
        [ends(LOW[k] + HIGH[k]) for k in (0, 1, 2, 4, 5)] + [jax.ShapeDtypeStruct((8, LANES), f32)], [vmem] * 15,
        [pltpu.VMEM((2, NT, x + LANES), f32), pltpu.VMEM((1, x), f32), pltpu.VMEM((12, NT, x + LANES), f32), carry(8),
         pltpu.VMEM((N_MOMENTS, NT, LANES), f32), pltpu.VMEM((24, LANES), f32)], "join",
    )(d, si, sc, mask, g, bg, b2g, bd, b2d, sums, eps, up_first, up, slope, received)
    moments = out[5]

    reach = 1
    while reach < peers:
        span = min(4, peers // reach)
        others = [lax.ppermute(moments, "inline", [(i, i ^ (k * reach)) for i in range(peers)]) for k in range(1, span)]
        moments = moments + add_terms(others)
        reach *= span

    return pl.pallas_call(
        functools.partial(last_kernel, n, x),
        out_shape=[jax.ShapeDtypeStruct((n, NT, x), f32)] * 2,
        in_specs=[vmem] * 13,
        out_specs=[hbm] * 2,
        scratch_shapes=[
            pltpu.VMEM((n, NT, x), f32),
            pltpu.VMEM((n, NT, x), f32),
            pltpu.SemaphoreType.DMA((2 * n,)),
        ],
        compiler_params=params,
        name="last",
    )(
        moments, m, d, g, bg, b2g, bd, b2d, *in_vmem(out[:5]))


def solution(mesh):
    rows = P(("groups", "inline"), None, None)
    return jax.shard_map(
        on_device,
        mesh=mesh,
        in_specs=(rows, P(("groups", "inline"), None), rows, rows, rows, rows),
        out_specs=(rows, rows),
        check_vma=False,
    )
```

```python
import functools

import jax
import jax.numpy as jnp
from jax import lax
from jax.experimental import pallas as pl
from jax.experimental.pallas import tpu as pltpu
from jax.sharding import PartitionSpec as P

ITERS = 3
NT = 8
LANES = 128
CHUNK = 4096
SHIFT = 18.0
M0, D0, SI0, SC0, FIRST0 = range(5)
G0, BD0, BG0, B2D0, B2G0, LATE0 = range(6)
WM1, WD1, G1, BD1, BG1, DOWN1 = range(6)
N_MOMENTS = 18
VMEM_LIMIT = 16 * 1024 * 1024

f32 = jnp.float32


def time_ahead(v):
    rolled = pltpu.roll(v, NT - 1, 0)
    return jnp.where(lax.broadcasted_iota(jnp.int32, v.shape, 0) == NT - 1, 0.0, rolled)


def time_behind(v):
    rolled = pltpu.roll(v, 1, 0)
    return jnp.where(lax.broadcasted_iota(jnp.int32, v.shape, 0) == 0, 0.0, rolled)


def sum_diff(v):
    ahead = time_ahead(v)
    return ahead + v, ahead - v


def head(pair, width):
    return pair[0][:, :width], pair[1][:, :width]


def inline_res(here, after, slope):
    return (after[0] - here[0]) + slope * (after[1] + here[1])


def parts(res, slope):
    scaled = slope * res
    return res - scaled, res + scaled


def to_next(ef):
    return ef[0] + time_behind(ef[1])


def to_self(ef):
    return -(ef[1] + time_behind(ef[0]))


def lane_ahead(v):
    width = v.shape[1]
    return pltpu.roll(v, width - 1, 1)[:, : width - LANES]


def lane_behind(before, v):
    joined = jnp.concatenate([before, v], axis=1)
    return pltpu.roll(joined, 1, 1)[:, LANES:]


def cross_res(sd, slope):
    width = sd[0].shape[1] - LANES
    here = head(sd, width)
    return (lane_ahead(sd[0]) - here[0]) + slope * (lane_ahead(sd[1]) + here[1])


def cross_terms(sd, slope, carry, slot):
    e, f = parts(cross_res(sd, slope), slope)
    e_behind = lane_behind(carry[slot, 0], e)
    f_behind = lane_behind(carry[slot, 1], f)
    carry[slot, 0] = e[:, -LANES:]
    carry[slot, 1] = f[:, -LANES:]
    return e_behind - f, f_behind - e


def stencil(load, slope_in, slope_cr, lo, hi, res_lo, res_hi, carry, slot, scale_lo=None):
    out = {}
    sd = {}

    def pair(i):
        if i not in sd:
            sd[i] = sum_diff(load(i))
        return sd[i]

    before = None
    for i in range(lo - 1, hi + 1):
        here = None
        if res_lo <= i <= res_hi:
            first = pair(i)
            second = pair(i + 1)
            width = first[0].shape[1] - LANES
            slope = slope_in(i)
            res = inline_res(head(first, width), head(second, width), slope)
            if i == -1 and scale_lo is not None:
                res = res * scale_lo
            here = parts(res, slope)
        if i >= lo:
            same, later = cross_terms(pair(i), slope_cr(i), carry, slot + i - lo)
            if before is not None:
                same = same + before[0]
                later = later + before[1]
            if here is not None:
                same = same - here[1]
                later = later - here[0]
            out[i] = same + time_behind(later)
        before = here
    return out


class Mended:
    def __init__(self, n, low, high, whole, ends, before=None, after=None):
        self.n, self.low, self.high, self.whole, self.ends, self.before, self.after = n, low, high, whole, ends, before, after

    def at(self, i):
        if i < 0:
            return self.before
        if i >= self.n:
            return self.after
        if i < self.low:
            return self.ends, i
        if i >= self.n - self.high:
            return self.ends, self.low + i - self.n + self.high
        return self.whole, i + 1

    def load(self, i, lanes):
        ref, row = self.at(i)
        return ref[row, :, lanes]

    def store(self, i, lanes, value):
        ref, row = self.at(i)
        ref[row, :, lanes] = value


def chunks(x):
    return x // CHUNK


def at_chunk(c):
    return multiple(c * CHUNK)


def multiple(lane):
    return lane if isinstance(lane, int) else pl.multiple_of(lane, CHUNK)


def sweep(x, body):
    if chunks(x) == 1:
        body(0, 0)
    else:
        lax.fori_loop(0, chunks(x), body, 0)


class Own:
    def __init__(self, n, x0, si_ref, sc_ref, mask_ref, carry):
        self.n, self.x0, self.here = n, x0, pl.ds(x0, CHUNK)
        self.si_ref, self.sc_ref, self.mask_ref, self.carry = si_ref, sc_ref, mask_ref, carry

    def known4(self, i):
        return self.mask_ref[pl.ds(i, 1), self.here].astype(f32) * 4.0

    def level(self, src, lo, hi, slot):
        return stencil(
            lambda i: src[i + 1, :, pl.ds(self.x0, CHUNK + LANES)],
            lambda i: self.si_ref[i + 1, :, self.here],
            lambda i: self.sc_ref[i, :, self.here],
            lo, hi, 0, self.n - 2, self.carry, slot,
        )

    def applied(self, src, lo, hi, slot):
        out = self.level(src, lo, hi, slot)
        return {i: (self.known4(i) - SHIFT) * src[i + 1, :, self.here] + out[i] for i in out}

    def gradient(self, data_ref, m_ref, lo, hi, slot):
        out = self.level(m_ref, lo, hi, slot)
        return {i: self.known4(i) * (data_ref[i, :, self.here] - m_ref[i + 1, :, self.here]) - out[i] for i in out}


def put(ref, slot, x, x0, value):
    ref[:, pl.ds(multiple(x0 + slot * x), CHUNK)] = value


def pack_kernel(n, x, si_hbm, sc_hbm, model_hbm, dir_hbm, up_ref, sems):
    copies = [
        pltpu.make_async_copy(source.at[0], up_ref.at[:, pl.ds(slot * x, x)], sems.at[slot])
        for source, slot in ((model_hbm, M0), (dir_hbm, D0), (si_hbm, SI0), (sc_hbm, SC0))
    ]
    for copy in copies:
        copy.start()
    for copy in copies:
        copy.wait()


def first_kernel(
    n, x,
    data_hbm, mask_hbm, si_hbm, sc_hbm, model_hbm, dir_hbm,
    data_ref, mask_ref, si_ref, sc_ref, m_ref, d_ref, up_ref, slope_ref,
    g_ref, bg_ref, bd_ref, carry, sems,
):
    lanes = pl.ds(0, x)
    copies = [pltpu.make_async_copy(mask_hbm, mask_ref, sems.at[0])]
    for top in (True, False):
        for source, target, skip in (
            (model_hbm, m_ref, 1), (si_hbm, si_ref, 1), (sc_hbm, sc_ref, 0), (data_hbm, data_ref, 0), (dir_hbm, d_ref, 1),
        ):
            start, size = (0, 4) if top else (4, n - 4)
            copies.append(pltpu.make_async_copy(
                source.at[pl.ds(start, size)], target.at[pl.ds(start + skip, size), :, lanes], sems.at[len(copies)]))
    for copy in copies:
        copy.start()
    clear_pads(x, (m_ref, d_ref, g_ref, bg_ref, bd_ref))
    carry[...] = jnp.zeros(carry.shape, f32)
    for copy in copies[:5]:
        copy.wait()
    share = x // NT
    for s in range(NT):
        up_ref[pl.ds(s, 1), pl.ds(LATE0 * x, share)] = mask_ref[pl.ds(0, 1), pl.ds(s * share, share)].astype(f32)

    def first(c, _):
        x0 = at_chunk(c)
        own = Own(n, x0, si_ref, sc_ref, mask_ref, carry)
        out = own.gradient(data_ref, m_ref, 0, 2, 0)
        put(up_ref, G0, x, x0, out[0])
        for i, value in out.items():
            g_ref[i + 1, :, own.here] = value
        return 0

    def first_of_direction(c, _):
        x0 = at_chunk(c)
        own = Own(n, x0, si_ref, sc_ref, mask_ref, carry)
        out = own.applied(d_ref, 0, 1, 3)
        put(up_ref, BD0, x, x0, out[0])
        for i, value in out.items():
            bd_ref[i + 1, :, own.here] = value
        return 0

    sweep(x, first)
    copies[5].wait()
    sweep(x, first_of_direction)
    carry[...] = jnp.zeros(carry.shape, f32)

    def second(c, _):
        x0 = at_chunk(c)
        own = Own(n, x0, si_ref, sc_ref, mask_ref, carry)
        out = own.applied(g_ref, 0, 1, 0)
        put(up_ref, BG0, x, x0, out[0])
        for i, value in out.items():
            bg_ref[i + 1, :, own.here] = value
        put(up_ref, B2D0, x, x0, own.applied(bd_ref, 0, 0, 2)[0])
        return 0

    sweep(x, second)
    carry[...] = jnp.zeros(carry.shape, f32)

    def third(c, _):
        x0 = at_chunk(c)
        put(up_ref, B2G0, x, x0, Own(n, x0, si_ref, sc_ref, mask_ref, carry).applied(bg_ref, 0, 0, 0)[0])
        return 0

    sweep(x, third)
    for copy in copies[6:]:
        copy.wait()
    slope_ref[...] = si_ref[n, :, lanes]


def down_kernel(
    n, x, data_ref, mask_ref, si_ref, sc_ref, m_ref, d_ref, up_first,
    down_ref, eps_ref,
    g_ref, carry,
):
    clear_pads(x, (g_ref, eps_ref))
    carry[...] = jnp.zeros(carry.shape, f32)

    def first(c, _):
        x0 = at_chunk(c)
        here = pl.ds(x0, CHUNK)
        own = Own(n, x0, si_ref, sc_ref, mask_ref, carry)
        slope = si_ref[n, :, here]
        out = own.gradient(data_ref, m_ref, n - 2, n - 1, 0)
        ef = parts(inline_res(sum_diff(m_ref[n, :, here]), sum_diff(row_of(up_first, M0, x, x0)), slope), slope)
        g_ref[n - 1, :, here] = out[n - 2]
        g_ref[n, :, here] = out[n - 1] - to_self(ef)
        put(down_ref, G1, x, x0, g_ref[n, :, here])
        eps_ref[0, :, here] = -to_next(ef)
        put(down_ref, WM1, x, x0, eps_ref[0, :, here])
        ef = parts(inline_res(sum_diff(d_ref[n, :, here]), sum_diff(row_of(up_first, D0, x, x0)), slope), slope)
        put(down_ref, BD1, x, x0, own.applied(d_ref, n - 1, n - 1, 2)[n - 1] + to_self(ef))
        eps_ref[1, :, here] = to_next(ef)
        put(down_ref, WD1, x, x0, eps_ref[1, :, here])
        return 0

    sweep(x, first)
    carry[...] = jnp.zeros(carry.shape, f32)

    def second(c, _):
        x0 = at_chunk(c)
        own = Own(n, x0, si_ref, sc_ref, mask_ref, carry)
        put(down_ref, BG1, x, x0, own.applied(g_ref, n - 1, n - 1, 0)[n - 1])
        return 0

    sweep(x, second)


def local_kernel(
    n, x, data_ref, mask_ref, si_ref, sc_ref, m_ref, d_ref, down_ref,
    g_ref, bg_ref, b2g_ref, bd_ref, b2d_ref, sums_ref, carry,
):
    clear_pads(x, (g_ref, bg_ref, b2g_ref, bd_ref, b2d_ref))
    carry[...] = jnp.zeros(carry.shape, f32)
    sums_ref[...] = jnp.zeros(sums_ref.shape, f32)

    def first(c, _):
        x0 = at_chunk(c)
        here = pl.ds(x0, CHUNK)
        own = Own(n, x0, si_ref, sc_ref, mask_ref, carry)
        for i, value in own.gradient(data_ref, m_ref, 0, n - 2, 0).items():
            g_ref[i + 1, :, here] = value
        for i, value in own.applied(d_ref, 0, n - 2, n).items():
            bd_ref[i + 1, :, here] = value
        g_ref[n, :, here] = row_of(down_ref, G1, x, x0)
        bd_ref[n, :, here] = row_of(down_ref, BD1, x, x0)
        return 0

    sweep(x, first)
    carry[...] = jnp.zeros(carry.shape, f32)

    def second(c, _):
        x0 = at_chunk(c)
        own = Own(n, x0, si_ref, sc_ref, mask_ref, carry)
        for i, value in own.applied(g_ref, 2, n - 2, 0).items():
            bg_ref[i + 1, :, own.here] = value
        for i, value in own.applied(bd_ref, 2, n - 2, n).items():
            b2d_ref[i + 1, :, own.here] = value
        return 0

    sweep(x, second)
    carry[...] = jnp.zeros(carry.shape, f32)

    def third(c, _):
        x0 = at_chunk(c)
        own = Own(n, x0, si_ref, sc_ref, mask_ref, carry)
        for i, value in own.applied(bg_ref, 3, n - 3, 0).items():
            b2g_ref[i + 1, :, own.here] = value
        return 0

    sweep(x, third)

    def fourth(c, _):
        x0 = at_chunk(c)
        loads = [lambda i, lanes, ref=ref: ref[i + 1, :, lanes] for ref in (g_ref, bg_ref, b2g_ref, d_ref, bd_ref, b2d_ref)]
        products(n, x0, loads, mask_ref, si_ref, sc_ref, sums_ref, lambda done: done)
        return 0

    sweep(x, fourth)


PAIRS = ((0, 0), (0, 1), (1, 1), (1, 2), (2, 2), None, (0, 3), (0, 4), (1, 4), (1, 5), (2, 5), None,
         (3, 3), (3, 4), (4, 4), (4, 5), (5, 5), None)


class Totals:
    def __init__(self):
        self.of = {}

    def add(self, k, left, right):
        product = left * right
        acc = product[:, :LANES]
        for j in range(1, CHUNK // LANES):
            acc = acc + product[:, j * LANES:(j + 1) * LANES]
        self.of[k] = self.of[k] + acc if k in self.of else acc

    def put(self, sums):
        for k, value in self.of.items():
            sums[k] = sums[k] + value


class Pairs:
    def __init__(self, load, x0):
        self.load, self.lanes, self.of = load, pl.ds(x0, CHUNK + LANES), {}

    def at(self, i):
        if i not in self.of:
            self.of[i] = sum_diff(self.load(i, self.lanes))
        return self.of[i]

    def inline(self, i, slope):
        return inline_res(head(self.at(i), CHUNK), head(self.at(i + 1), CHUNK), slope)

    def cross(self, i, slope):
        return cross_res(self.at(i), slope)


LOW = (1, 2, 3, 0, 1, 2)
HIGH = (0, 1, 2, 0, 0, 1)


def products(n, x0, loads, mask_ref, si_ref, sc_ref, sums, take):
    here = pl.ds(x0, CHUNK)
    totals = Totals()
    pair_g, pair_d = Pairs(loads[2], x0), Pairs(loads[5], x0)

    def turn(i, *vectors):
        return take(all(LOW[v] <= i < n - HIGH[v] for v in vectors))

    for i in range(n):
        values = {}

        def row(v):
            if v not in values:
                values[v] = loads[v](i, here)
            return values[v]

        for k, which in enumerate(PAIRS):
            if which is not None and turn(i, *which):
                totals.add(k, row(which[0]), row(which[1]))
        res = {}
        for k, left, right in ((5, 2, 2), (11, 2, 5), (17, 5, 5)):
            if turn(i, left, right):
                known = mask_ref[pl.ds(i, 1), here].astype(f32) * 4.0
                totals.add(k, known * row(left), row(right))
                for v, pair in ((left, pair_g if left == 2 else pair_d), (right, pair_d if right == 5 else pair_g)):
                    if ("cross", v) not in res:
                        res["cross", v] = pair.cross(i, sc_ref[i, :, here])
                totals.add(k, res["cross", left], res["cross", right])
            if take(all(LOW[v] <= i < n - 1 - HIGH[v] for v in (left, right))):
                for v, pair in ((left, pair_g if left == 2 else pair_d), (right, pair_d if right == 5 else pair_g)):
                    if ("inline", v) not in res:
                        res["inline", v] = pair.inline(i, si_ref[i + 1, :, here])
                totals.add(k, res["inline", left], res["inline", right])
    totals.put(sums)


def place_flags():
    place = lax.axis_index("inline")
    return (place > 0).astype(f32), (place < lax.axis_size("inline") - 1).astype(f32)


def row_of(ref, slot, x, x0):
    return ref[:, pl.ds(multiple(x0 + slot * x), CHUNK)]


def boundary(rows, i, slope, here, scale=None):
    res = inline_res(sum_diff(rows.load(i, here)), sum_diff(rows.load(i + 1, here)), slope)
    if scale is not None:
        res = res * scale
    return parts(res, slope)


def clear_pads(x, refs):
    for ref in refs:
        for i in range(ref.shape[0]):
            ref[i, :, pl.ds(x, LANES)] = jnp.zeros((NT, LANES), f32)


def end_rows(n, x0, src, dst, slope_before, si_ref, sc_ref, mask_ref, scale, carry, slot):
    here = pl.ds(x0, CHUNK)
    for lo, hi in ((0, dst.low - 1), (n - dst.high, n - 1)):
        out = stencil(
            lambda i: src.load(i, pl.ds(x0, CHUNK + LANES)),
            lambda i: slope_before if i == -1 else si_ref[i + 1, :, here],
            lambda i: sc_ref[i, :, here],
            lo, hi, -1, n - 1, carry, slot, scale,
        )
        for i in range(lo, hi + 1):
            known = mask_ref[pl.ds(i, 1), here].astype(f32) * 4.0
            dst.store(i, here, (known - SHIFT) * src.load(i, here) + out[i])
        slot += hi - lo + 1
    return slot


def beyond(rows_ref, row, wide, diagonal, cross, slope, carry, slot, further=None):
    here = pl.ds(wide.start, CHUNK)
    sd = sum_diff(rows_ref[row, :, wide])
    near = head(sd, CHUNK)
    same, later = cross_terms(sd, cross, carry, slot)
    if further is None:
        inner = parts(slope * near[1] - near[0], slope)
    else:
        inner = parts(inline_res(near, sum_diff(further), slope), slope)
    return diagonal * rows_ref[row, :, here] + (same - inner[1]) + time_behind(later - inner[0]), inner


def join_kernel(
    n, x,
    d_ref, si_ref, sc_ref, mask_ref, g_in, bg_in, b2g_in, bd_in, b2d_in, sums_in, eps_in,
    up_first, up_ref, slope_ref, down_ref,
    g_out, bg_out, b2g_out, bd_out, b2d_out, moments_ref,
    eps_ref, mask_up, ghosts, carry, sums,
):
    not_first, not_last = place_flags()
    clear_pads(x, (eps_ref, ghosts, g_out, bg_out, b2g_out, bd_out, b2d_out))
    carry[...] = jnp.zeros(carry.shape, f32)
    sums[...] = sums_in[...]
    share = x // NT
    for s in range(NT):
        mask_up[:, pl.ds(s * share, share)] = up_ref[pl.ds(s, 1), pl.ds(LATE0 * x, share)] * 4.0 - SHIFT
    g_rows, bg_rows, b2g_rows, d_rows, bd_rows, b2d_rows = (
        Mended(n, low, high, whole, ends, (ghosts, 2 * k), (ghosts, 2 * k + 1))
        for k, (low, high, whole, ends) in enumerate(zip(
            LOW, HIGH, (g_in, bg_in, b2g_in, d_ref, bd_in, b2d_in), (g_out, bg_out, b2g_out, None, bd_out, b2d_out)))
    )

    def zeroth(c, _):
        x0 = at_chunk(c)
        here = pl.ds(x0, CHUNK)
        g_rows.store(-1, here, row_of(down_ref, G1, x, x0))
        g_rows.store(0, here, g_in[1, :, here] + row_of(down_ref, WM1, x, x0))
        g_rows.store(n, here, (row_of(up_ref, G0, x, x0) + eps_in[0, :, here]) * not_last)
        bd_rows.store(-1, here, row_of(down_ref, BD1, x, x0))
        bd_rows.store(0, here, bd_in[1, :, here] + row_of(down_ref, WD1, x, x0))
        bd_rows.store(n, here, (row_of(up_ref, BD0, x, x0) + eps_in[1, :, here]) * not_last)
        return 0

    sweep(x, zeroth)

    def first(c, _):
        x0 = at_chunk(c)
        here = pl.ds(x0, CHUNK)
        before = slope_ref[:, here]
        slope = si_ref[n, :, here]
        slot = end_rows(n, x0, g_rows, bg_rows, before, si_ref, sc_ref, mask_ref, not_first, carry, 0)
        slot = end_rows(n, x0, bd_rows, b2d_rows, before, si_ref, sc_ref, mask_ref, not_first, carry, slot)
        wide = pl.ds(x0, CHUNK + LANES)
        slope_up, cross_up = row_of(up_first, SI0, x, x0), row_of(up_first, SC0, x, x0)
        diagonal = mask_up[:, here]
        own, inner = beyond(eps_in, 0, wide, diagonal, cross_up, slope_up, carry, slot)
        eps = own + to_next(boundary(g_rows, n - 1, slope, here))
        eps_ref[0, :, here] = eps
        eps_ref[1, :, here] = to_next(inner)
        bg_rows.store(n, here, (row_of(up_ref, BG0, x, x0) + eps) * not_last)
        own, _ = beyond(eps_in, 1, wide, diagonal, cross_up, slope_up, carry, slot + 1)
        eps = own + to_next(boundary(bd_rows, n - 1, slope, here))
        b2d_rows.store(n, here, (row_of(up_ref, B2D0, x, x0) + eps) * not_last)
        bg_rows.store(-1, here, row_of(down_ref, BG1, x, x0) + to_self(boundary(g_rows, -1, before, here, not_first)))
        return 0

    sweep(x, first)
    carry[...] = jnp.zeros(carry.shape, f32)

    def second(c, _):
        x0 = at_chunk(c)
        here = pl.ds(x0, CHUNK)
        wide = pl.ds(x0, CHUNK + LANES)
        before = slope_ref[:, here]
        slot = end_rows(n, x0, bg_rows, b2g_rows, before, si_ref, sc_ref, mask_ref, not_first, carry, 0)
        own, _ = beyond(
            eps_ref, 0, wide, mask_up[:, here], row_of(up_first, SC0, x, x0), row_of(up_first, SI0, x, x0),
            carry, slot, eps_ref[1, :, here])
        edge = to_next(boundary(bg_rows, n - 1, si_ref[n, :, here], here))
        b2g_rows.store(n, here, (row_of(up_ref, B2G0, x, x0) + own + edge) * not_last)
        return 0

    sweep(x, second)

    def third(c, _):
        loads = [rows.load for rows in (g_rows, bg_rows, b2g_rows, d_rows, bd_rows, b2d_rows)]
        products(n, at_chunk(c), loads, mask_ref, si_ref, sc_ref, sums, lambda done: not done)
        return 0

    sweep(x, third)
    for k in range(N_MOMENTS):
        moments_ref[pl.ds(k, 1), :] = jnp.sum(sums[k], axis=0, keepdims=True)
    moments_ref[pl.ds(N_MOMENTS, 24 - N_MOMENTS), :] = jnp.zeros((24 - N_MOMENTS, LANES), f32)


def add_terms(terms):
    terms = list(terms)
    while len(terms) > 1:
        pairs = [left + right for left, right in zip(terms[::2], terms[1::2])]
        terms = pairs + terms[len(pairs) * 2:]
    return terms[0]


def solve(moments):
    mu, nu, xi = moments[:6], moments[6:12], moments[12:]

    def entry(a, b, i, j):
        if a == 0 and b == 0:
            return mu[i + j]
        if a == 1 and b == 1:
            return xi[i + j]
        return nu[i + j]

    shifted = {}

    def entry_a(a, b, i, j):
        which = a + b
        if (which, i + j) not in shifted:
            if i + j == 4:
                value = entry(a, b, 2, 3)
            else:
                value = entry(a, b, i, j + 1) + SHIFT * entry(a, b, i, j)
            shifted[which, i + j] = value * 0.25
        return shifted[which, i + j]

    def form(get, u, v):
        return add_terms(
            left * add_terms(right * get(a, b, i, j) for (b, j), right in v.items()) for (a, i), left in u.items())

    def axpy(scale, u, v):
        out = dict(v)
        for key, value in u.items():
            term = scale * value
            out[key] = out[key] + term if key in out else term
        return out

    one = jnp.ones_like(mu[0])
    gradient = {(0, 0): 0.25 * one}
    direction = {(1, 0): one}
    model = {}
    for iteration in range(ITERS):
        mixing = -form(entry_a, gradient, direction) / form(entry_a, direction, direction)
        direction = axpy(mixing, direction, gradient)
        step = form(entry, gradient, direction) / form(entry_a, direction, direction)
        model = axpy(step, direction, model)
        if iteration < ITERS - 1:
            image = {key: value * (0.25 * SHIFT) for key, value in direction.items()}
            image = axpy(0.25, {(a, i + 1): value for (a, i), value in direction.items()}, image)
            gradient = axpy(-step, image, gradient)
    return model, direction


def last_kernel(
    n, x, moments_ref, m_ref, d_ref, g_in, bg_in, b2g_in, bd_in, b2d_in, g_end, bg_end, b2g_end, bd_end, b2d_end,
    model_hbm, dir_hbm, mo_ref, do_ref, sems,
):
    moments = [
        jnp.broadcast_to(jnp.sum(moments_ref[pl.ds(k, 1), :], axis=1, keepdims=True), (NT, LANES))
        for k in range(N_MOMENTS)
    ]
    model, direction = solve(moments)
    rows = [
        Mended(n, LOW[k], HIGH[k], whole, ends)
        for k, whole, ends in ((0, g_in, g_end), (1, bg_in, bg_end), (2, b2g_in, b2g_end), (4, bd_in, bd_end), (5, b2d_in, b2d_end))
    ]
    keys = ((0, 0), (0, 1), (0, 2), (1, 1), (1, 2))
    copies = []
    for i in range(n):
        for c in range(x // LANES):
            here = pl.ds(c * LANES, LANES)
            values = {key: vector.load(i, here) for key, vector in zip(keys, rows)}
            values[1, 0] = d_ref[i + 1, :, here]
            mo_ref[i, :, here] = m_ref[i + 1, :, here] + add_terms(model[key] * value for key, value in values.items())
            do_ref[i, :, here] = add_terms(direction[key] * value for key, value in values.items())
        for k, (src, dst) in enumerate(((mo_ref, model_hbm), (do_ref, dir_hbm))):
            copy = pltpu.make_async_copy(src.at[i], dst.at[i], sems.at[2 * i + k])
            copy.start()
            copies.append(copy)
    for copy in copies:
        copy.wait()


def in_vmem(values):
    return [pltpu.with_memory_space_constraint(v, pltpu.VMEM) for v in values]


def kept(shape, dtype=f32):
    return pltpu.VMEM(shape, dtype)


def on_device(*args):
    n, _, x = args[0].shape
    peers = lax.axis_size("inline")
    assert peers & (peers - 1) == 0 and n >= 7 and x % CHUNK == 0
    vmem = pl.BlockSpec(memory_space=pltpu.VMEM)
    hbm = pl.BlockSpec(memory_space=pl.ANY)
    params = pltpu.CompilerParams(vmem_limit_bytes=VMEM_LIMIT)
    wide = kept((n + 2, NT, x + LANES))
    share = x // NT

    args = [pltpu.with_memory_space_constraint(v, pltpu.HBM) for v in args]

    def call(kernel, out_shape, in_specs, scratch_shapes, name):
        return pl.pallas_call(
            functools.partial(kernel, n, x),
            out_shape=out_shape,
            in_specs=in_specs,
            out_specs=[vmem] * len(out_shape),
            scratch_shapes=scratch_shapes,
            compiler_params=params,
            name=name,
        )

    def carry(slots):
        return pltpu.VMEM((slots, 2, NT, LANES), f32)

    def ends(rows):
        return kept((rows, NT, x + LANES))

    def to_before(value):
        return lax.ppermute(value, "inline", [(i, i - 1) for i in range(1, peers)])

    def to_after(value):
        return lax.ppermute(value, "inline", [(i, i + 1) for i in range(peers - 1)])

    up_first, = call(
        pack_kernel, [kept((NT, FIRST0 * x))], [hbm] * 4, [pltpu.SemaphoreType.DMA((4,))], "pack",
    )(*args[2:])
    up_first = to_before(up_first)

    *loaded, up, slope = call(
        first_kernel,
        [kept((n, NT, x)), kept((n, x), jnp.int32), kept((n + 2, NT, x)), kept((n, NT, x)), wide, wide,
         kept((NT, LATE0 * x + share)), kept((NT, x))],
        [hbm] * 6,
        [pltpu.VMEM((4, NT, x + LANES), f32)] * 3 + [carry(5), pltpu.SemaphoreType.DMA((11,))], "first",
    )(*args)
    loaded = in_vmem(loaded)
    _, mask, si, sc, m, d = loaded
    up = to_before(up)
    slope = to_after(slope)

    down, eps = call(
        down_kernel, [kept((NT, DOWN1 * x)), ends(2)], [vmem] * 7,
        [pltpu.VMEM((n + 2, NT, x + LANES), f32), carry(3)], "down",
    )(*loaded, up_first)
    received = to_after(down)

    made = call(
        local_kernel, [wide, wide, wide, wide, wide, kept((N_MOMENTS, NT, LANES))], [vmem] * 7,
        [carry(2 * n)], "local",
    )(*loaded, down)
    g, bg, b2g, bd, b2d, sums = in_vmem(made)

    out = call(
        join_kernel,
        [ends(LOW[k] + HIGH[k]) for k in (0, 1, 2, 4, 5)] + [jax.ShapeDtypeStruct((24, LANES), f32)], [vmem] * 15,
        [pltpu.VMEM((2, NT, x + LANES), f32), pltpu.VMEM((1, x), f32), pltpu.VMEM((12, NT, x + LANES), f32), carry(8),
         pltpu.VMEM((N_MOMENTS, NT, LANES), f32)], "join",
    )(d, si, sc, mask, g, bg, b2g, bd, b2d, sums, eps, up_first, up, slope, received)
    moments = out[5]

    reach = 1
    while reach < peers:
        span = min(4, peers // reach)
        others = [lax.ppermute(moments, "inline", [(i, i ^ (k * reach)) for i in range(peers)]) for k in range(1, span)]
        moments = moments + add_terms(others)
        reach *= span

    return pl.pallas_call(
        functools.partial(last_kernel, n, x),
        out_shape=[jax.ShapeDtypeStruct((n, NT, x), f32)] * 2,
        in_specs=[vmem] * 13,
        out_specs=[hbm] * 2,
        scratch_shapes=[
            pltpu.VMEM((n, NT, x), f32),
            pltpu.VMEM((n, NT, x), f32),
            pltpu.SemaphoreType.DMA((2 * n,)),
        ],
        compiler_params=params,
        name="last",
    )(
        moments, m, d, g, bg, b2g, bd, b2d, *in_vmem(out[:5]))


def solution(mesh):
    rows = P(("groups", "inline"), None, None)
    return jax.shard_map(
        on_device,
        mesh=mesh,
        in_specs=(rows, P(("groups", "inline"), None), rows, rows, rows, rows),
        out_specs=(rows, rows),
        check_vma=False,
    )
```
